128 devices in a mesh: dp: 16 (over z, y), leaf: 4 (over x), head: 2 (over core).
Axes of the slice: x: 4, y: 4, z: 4, core: 2. Of those that a mesh axis runs over, the one named last changes fastest.
Arguments:
- queries: bfloat16 [16384, 4096], P(('dp', 'leaf'), 'head'), may hold values from -200 to 200
- branch_kv: bfloat16 [2, 16384, 512], P(None, ('dp', 'leaf'), 'head'), may hold values from -6 to 6
- ancestor_key_value: bfloat16 [2, 2048, 512], P(None, ('dp', 'leaf'), 'head'), may hold values from -6 to 6
- upstream: bfloat16 [16384, 4096], P(('dp', 'leaf'), 'head'), may hold values from -6 to 6
- lengths: int32 [64, 4], P(('dp', 'leaf')), may hold values from 1 to 128, 256 in all within a row
- ancestors: int32 [256, 64], P(('dp', 'leaf')), may hold values 0 or 1
Outputs:
- normed: float32 [16384, 4096], P(('dp', 'leaf'), 'head')
- d_queries: float32 [16384, 4096], P(('dp', 'leaf'), 'head')
- d_branch_kv: float32 [2, 16384, 512], P(None, ('dp', 'leaf'), 'head')
- d_prefix_kv: float32 [2, 2048, 512], P(None, ('dp', 'leaf'), 'head')
The draws below stay inside these ranges and needn't reach their ends.
Inputs may be any that keep to these rules, and one draw needn't show every extreme that they name: Every row holds segment lengths that sum to 256; the largest in each row is 128.
All inputs are finite; a program needn't handle non-finite values. No bound on the sum of `ancestors` on one device may be relied on, other than what follows from the above.
Results may differ from the reference program's by a relative error of at most 0.015.
Values may be sent and summed in bfloat16 or wider, within the bound.
No kernel may reach another device: no remote copies, remote signals or barrier semaphores. Data moves between devices by JAX's collectives and lax.ppermute only.
A program may use at most 64 MiB of HBM per device.

```python
import math
import jax
import jax.numpy as jnp
import numpy as np
from jax import lax

QUERY_HEADS = 32
KEY_VALUE_HEADS = 4
HEAD_SIZE = 128
TOK_DEV = 256
SEGS = 4
OWNED_TOKENS = 32
ANCESTOR_COUNT = 64
BRANCH_TOKENS = 16384
NSEG = 256
N_DP = 16
N_LEAF = 4


def base_keys(key):
    return jnp.clip(jax.random.normal(key, (BRANCH_TOKENS, KEY_VALUE_HEADS * HEAD_SIZE), jnp.float32), -6.0, 6.0)


def draw_queries(key, part):
    key = jax.random.fold_in(key, 7)
    value_tensor = jnp.clip(jax.random.normal(key, (BRANCH_TOKENS, QUERY_HEADS * HEAD_SIZE), jnp.float32), -6.0, 6.0)
    return value_tensor.astype(jnp.bfloat16)


def draw_branch_kv(key, part):
    shared_segment = base_keys(key)
    key = jax.random.fold_in(key, 11)
    value_tensor = jnp.clip(jax.random.normal(key, (BRANCH_TOKENS, KEY_VALUE_HEADS * HEAD_SIZE), jnp.float32), -6.0, 6.0)
    return jnp.stack([shared_segment, value_tensor]).astype(jnp.bfloat16)


def with_ends(result, rng, low, high):
    longest = result.shape.index(max(result.shape))
    spots = []
    for shift in (0, 1):
        where = [jax.random.randint(jax.random.fold_in(rng, axis), (), 0, length) for axis, length in enumerate(result.shape)]
        where[longest] = (where[longest] + shift) % result.shape[longest]
        spots.append(tuple(where))
    return result.at[spots[0]].set(low).at[spots[1]].set(high)


def block_scale(key, dims, shards, low, high):
    def one(dim, parts):
        heights = jax.random.uniform(jax.random.fold_in(jax.random.fold_in(key, 6), dim), (parts,), jnp.float32, low / len(shards), high / len(shards))
        return jnp.repeat(jnp.exp(heights), dims[dim] // parts).reshape((-1,) + (1,) * (len(dims) - dim - 1))

    factor_of = one(*shards[0])
    for cut in shards[1:]:
        factor_of = factor_of * one(*cut)
    return factor_of


def split_up(count, total, reach, lean):
    loads = [(1 << 20) // math.isqrt(standing ** lean) + 1 for standing in range(2, count + 1)]
    surplus, holding = total - reach - (count - 1), [1] * (count - 1)
    while surplus > 0:
        candidates = [i for i in range(count - 1) if holding[i] < reach]
        pool, remaining = sum([loads[i] for i in candidates]), surplus
        for i in candidates:
            more = min(reach - holding[i], max(1, remaining * loads[i] // pool), surplus)
            holding[i] = holding[i] + more
            surplus = surplus - more
    return np.array([reach] + holding)


def ragged_sizes(rng, number_of, total, bound, slope):
    if number_of == 2:
        one = jax.random.randint(rng, (), max(1, total - bound), min(bound, total - 1) + 1)
        return jnp.stack([one, total - one])
    sizes = jnp.asarray(split_up(number_of, total, bound, slope), jnp.int32)
    twos = (number_of - 1) // 2
    source_of, taker = sizes[1:1 + 2 * twos:2], sizes[2:2 + 2 * twos:2]
    margin = jnp.minimum(source_of - 1, bound - taker)
    moved = jax.random.randint(jax.random.fold_in(rng, 1), (twos,), 0, 1 << 20) % (margin + 1)
    sizes = sizes.at[1:1 + 2 * twos:2].set(source_of - moved).at[2:2 + 2 * twos:2].set(taker + moved)
    return sizes[jax.random.permutation(jax.random.fold_in(rng, 2), number_of)]


def scatter_about(rng, extent, scale, reach, shards=(), held_as=jnp.bfloat16):
    result = jax.random.normal(rng, extent, jnp.float32) * scale
    if len(shards) > 0:
        result = block_scale(rng, extent, shards, -0.22, 0.18) * result
    return jnp.clip(result, min=-reach, max=reach).astype(held_as)


def setup_inputs(seed: int = 0) -> dict:
    seeds = jax.random.split(jax.random.key(seed), 7)
    return {
        "queries": draw_queries(jax.random.fold_in(seeds[6], 71), 0),
        "branch_kv": draw_branch_kv(jax.random.fold_in(seeds[6], 71), 0),
        "ancestor_key_value": scatter_about(seeds[2], (2, ANCESTOR_COUNT * OWNED_TOKENS, KEY_VALUE_HEADS * HEAD_SIZE), 1.0, 6.0, ((1, 64), (2, 2))),
        "upstream": scatter_about(seeds[3], (BRANCH_TOKENS, QUERY_HEADS * HEAD_SIZE), 1.0, 6.0, ((0, 64), (1, 2))),
        "lengths": jax.vmap(lambda own: ragged_sizes(own, SEGS, TOK_DEV, TOK_DEV // 2, 2))(jax.random.split(seeds[4], (N_DP * N_LEAF))).reshape((N_DP * N_LEAF, SEGS)).astype(jnp.int32),
        "ancestors": with_ends((jax.random.randint(seeds[5], (NSEG, ANCESTOR_COUNT), 0, 3) < 1).astype(jnp.int32), jax.random.fold_in(seeds[5], 1), 0, 1),
    }


NEGATIVE = -1e+30
EPSILON = 1e-05

def segment_masks(seg_lengths, anc_rows, token_count):
    positions = jnp.arange(token_count, dtype=jnp.int32)
    finish = jnp.cumsum(seg_lengths).astype(jnp.int32)
    begin = (finish - seg_lengths).astype(jnp.int32)
    member = (positions[:, None] >= begin[None, :]) & (positions[:, None] < finish[None, :])
    seg_ids = lax.optimization_barrier(jnp.sum((positions[:, None] >= finish[None, :]).astype(jnp.int32), axis=1))
    causal = (seg_ids[:, None] == seg_ids[None, :]) & (positions[None, :] <= positions[:, None])
    token_anc = jnp.dot(member.astype(jnp.float32), anc_rows.astype(jnp.float32), precision=lax.Precision.HIGHEST)
    return (causal, token_anc)

def block_pass(query_block_rows, branch_part, block_upstream, seg_lengths, anc_rows, ancestor_part):
    token_count = query_block_rows.shape[0]
    query_groups = QUERY_HEADS // KEY_VALUE_HEADS
    scaling = HEAD_SIZE ** (-0.5)
    causal, token_anc = segment_masks(seg_lengths, anc_rows, token_count)
    prefix_allowed = jnp.repeat(token_anc, OWNED_TOKENS, axis=1) > 0.5
    allowed = jnp.concatenate([causal, prefix_allowed], axis=1)
    key_matrix = jnp.concatenate([branch_part[0], ancestor_part[0]], axis=0).reshape(-1, KEY_VALUE_HEADS, HEAD_SIZE).astype(jnp.float32)
    value_matrix = jnp.concatenate([branch_part[1], ancestor_part[1]], axis=0).reshape(-1, KEY_VALUE_HEADS, HEAD_SIZE).astype(jnp.float32)
    heads_of_query = query_block_rows.reshape(token_count, KEY_VALUE_HEADS, query_groups, HEAD_SIZE).astype(jnp.float32)
    scores = jnp.einsum('rkgd,mkd->rkgm', heads_of_query, key_matrix) * scaling
    scores = jnp.where(allowed[:, None, None, :], scores, NEGATIVE)
    highest = lax.optimization_barrier(jnp.max(scores, axis=-1, keepdims=True))
    logsum = highest + jnp.log(lax.optimization_barrier(jnp.sum(jnp.exp(scores - highest), axis=-1, keepdims=True)))
    weights = jnp.exp(scores - logsum)
    rounded = lax.optimization_barrier(weights.astype(jnp.bfloat16)).astype(jnp.float32)
    attended_float = jnp.einsum('rkgm,mkd->rkgd', rounded, value_matrix).reshape(token_count, QUERY_HEADS * HEAD_SIZE)
    scaler = lax.rsqrt(lax.optimization_barrier(jnp.mean(attended_float * attended_float, axis=-1)) + EPSILON)
    normed = attended_float * scaler[:, None]
    upper = block_upstream.astype(jnp.float32)
    inner = lax.optimization_barrier(jnp.sum(upper * attended_float, axis=-1))
    attended_gradient = (scaler[:, None] * upper - attended_float * (scaler ** 3 * inner / (QUERY_HEADS * HEAD_SIZE))[:, None]).astype(jnp.bfloat16)
    heads_gradient = lax.optimization_barrier(attended_gradient).astype(jnp.float32).reshape(token_count, KEY_VALUE_HEADS, query_groups, HEAD_SIZE)
    row_dot_sum = lax.optimization_barrier(jnp.sum(heads_gradient * attended_float.reshape(token_count, KEY_VALUE_HEADS, query_groups, HEAD_SIZE), axis=-1))
    d_weights = jnp.einsum('rkgd,mkd->rkgm', heads_gradient, value_matrix)
    d_scores = (weights * (d_weights - row_dot_sum[..., None])).astype(jnp.bfloat16)
    d_scores = lax.optimization_barrier(d_scores).astype(jnp.float32)
    d_query = (jnp.einsum('rkgm,mkd->rkgd', d_scores, key_matrix) * scaling).reshape(token_count, QUERY_HEADS * HEAD_SIZE)
    keys_gradient = jnp.einsum('rkgm,rkgd->mkd', d_scores, heads_of_query) * scaling
    values_gradient = jnp.einsum('rkgm,rkgd->mkd', rounded, heads_gradient)
    keys_gradient = keys_gradient.reshape(-1, KEY_VALUE_HEADS * HEAD_SIZE)
    values_gradient = values_gradient.reshape(-1, KEY_VALUE_HEADS * HEAD_SIZE)
    d_branch = jnp.stack([keys_gradient[:token_count], values_gradient[:token_count]])
    d_prefix = jnp.stack([keys_gradient[token_count:], values_gradient[token_count:]])
    return (normed, d_query, d_branch, d_prefix)

def reference(queries, branch_kv, ancestor_key_value, upstream, lengths, ancestors):
    blocks = N_DP * N_LEAF
    width = QUERY_HEADS * HEAD_SIZE
    key_value_width = KEY_VALUE_HEADS * HEAD_SIZE
    query_blocks = queries.reshape(blocks, TOK_DEV, width)
    branch_blocks = branch_kv.reshape(2, blocks, TOK_DEV, key_value_width).transpose(1, 0, 2, 3)
    upstream_blocks = upstream.reshape(blocks, TOK_DEV, width)
    anc_blocks = ancestors.reshape(blocks, SEGS, ANCESTOR_COUNT)

    def step(total, inputs):
        query_block_rows, branch_part, block_upstream, seg_lengths, anc_rows = inputs
        normed, d_query, d_branch, d_prefix = block_pass(query_block_rows, branch_part, block_upstream, seg_lengths, anc_rows, ancestor_key_value)
        return (total + d_prefix, (normed, d_query, d_branch))
    start_total = jnp.zeros((2, ANCESTOR_COUNT * OWNED_TOKENS, key_value_width), jnp.float32)
    total, outputs = lax.scan(step, start_total, (query_blocks, branch_blocks, upstream_blocks, lengths, anc_blocks))
    normed, d_query, d_branch = outputs
    normed = normed.reshape(BRANCH_TOKENS, width)
    d_query = d_query.reshape(BRANCH_TOKENS, width)
    d_branch = d_branch.transpose(1, 0, 2, 3).reshape(2, BRANCH_TOKENS, key_value_width)
    return (normed, d_query, d_branch, total)
```

```python
import functools

import jax
import jax.numpy as jnp
from jax import lax
from jax.experimental import pallas as pl
from jax.experimental.pallas import tpu as pltpu
from jax.sharding import PartitionSpec as P

QUERY_HEADS = 32
HEAD_SIZE = 128
NEGATIVE = -1e30
EPSILON = 1e-05
LOG2E = 1.4426950408889634

TILE = 32
CHUNK = 8
REACH = 128

ROWS_BY_ROWS = (((1,), (1,)), ((), ()))
COLS_BY_COLS = (((0,), (0,)), ((), ()))
PLAIN = (((1,), (0,)), ((), ()))


def dot(a, b, dims):
    return lax.dot_general(a, b, dims, preferred_element_type=jnp.float32)


def head_columns(index):
    return pl.ds(index * HEAD_SIZE, HEAD_SIZE)


def stacked(ref, base, kv_head, groups):
    return jnp.concatenate(
        [ref[pl.ds(base, TILE), head_columns(kv_head * groups + g)] for g in range(groups)], axis=0
    )


def fold(values, op):
    rows, width = values.shape
    return op(values.reshape(rows // 8, 8, width), axis=0)


def self_window(base, seg_row, width):
    window = pl.multiple_of(jnp.maximum(base - REACH, 0), TILE)
    keys = window + lax.broadcasted_iota(jnp.int32, (REACH + TILE, width), 0)
    tokens = base + (lax.broadcasted_iota(jnp.int32, (REACH + TILE, width), 1) & (TILE - 1))
    return window, (keys <= tokens) & (keys >= seg_row)


def chunk_ids(list_ref, t, c, owners):
    ids = [list_ref[t, c * CHUNK + i] for i in range(CHUNK)]
    return ids, [jnp.minimum(j, owners - 1) for j in ids]


def forward_kernel(
    steps_ref, list_ref, q_ref, up_ref, bkv_ref, anc_ref, bias_ref, hot_ref, seg_ref,
    att_ref, lse_ref, stat_ref, s_scr, o_scr,
):
    owners, _, owned, _ = anc_ref.shape
    token_count, width = q_ref.shape
    kv_heads = bkv_ref.shape[2] // HEAD_SIZE
    groups = width // HEAD_SIZE // kv_heads
    lanes = groups * TILE
    near = REACH + TILE
    span = CHUNK * owned
    factor = HEAD_SIZE ** (-0.5) * LOG2E

    def tile(t, carry):
        base = pl.multiple_of(t * TILE, TILE)
        steps = steps_ref[t]
        hot = jnp.concatenate([hot_ref[pl.ds(base, TILE), :]] * groups, axis=0)
        q = [stacked(q_ref, base, k, groups) for k in range(kv_heads)]
        qx = [jnp.concatenate([part, hot], axis=1) for part in q]
        window, allowed = self_window(base, seg_ref[pl.ds(t, 1), :], lanes)
        tops = []
        for k in range(kv_heads):
            keys = bkv_ref[0, pl.ds(window, near), head_columns(k)]
            scores = jnp.where(allowed, dot(keys, q[k], ROWS_BY_ROWS), NEGATIVE)
            s_scr[k, pl.ds(0, near), :] = scores
            tops.append(fold(scores, jnp.max))

        def score(c, tops):
            ids, clipped = chunk_ids(list_ref, t, c, owners)
            bias = jnp.concatenate([bias_ref[j] for j in ids for _ in range(2)], axis=0)
            start = pl.multiple_of(near + c * span, TILE)
            out = []
            for k in range(kv_heads):
                keys = jnp.concatenate([anc_ref[j, 0, :, head_columns(k)] for j in clipped], axis=0)
                scores = dot(jnp.concatenate([keys, bias], axis=1), qx[k], ROWS_BY_ROWS)
                s_scr[k, pl.ds(start, span), :] = scores
                out.append(jnp.maximum(tops[k], fold(scores, jnp.max)))
            return tuple(out)

        tops = lax.fori_loop(0, steps, score, tuple(tops))
        tops = [jnp.max(top, axis=0, keepdims=True) for top in tops]

        sums = []
        for k in range(kv_heads):
            values = bkv_ref[1, pl.ds(window, near), head_columns(k)]
            weights = jnp.exp2((s_scr[k, pl.ds(0, near), :] - tops[k]) * factor)
            sums.append(fold(weights, jnp.sum))
            o_scr[k] = dot(values, weights.astype(jnp.bfloat16), COLS_BY_COLS)

        def gather(c, sums):
            ids, clipped = chunk_ids(list_ref, t, c, owners)
            start = pl.multiple_of(near + c * span, TILE)
            out = []
            for k in range(kv_heads):
                values = jnp.concatenate([anc_ref[j, 1, :, head_columns(k)] for j in clipped], axis=0)
                weights = jnp.exp2((s_scr[k, pl.ds(start, span), :] - tops[k]) * factor)
                out.append(sums[k] + fold(weights, jnp.sum))
                o_scr[k] += dot(values, weights.astype(jnp.bfloat16), COLS_BY_COLS)
            return tuple(out)

        sums = lax.fori_loop(0, steps, gather, tuple(sums))

        squares = jnp.zeros((TILE, HEAD_SIZE), jnp.float32)
        inner = jnp.zeros((TILE, HEAD_SIZE), jnp.float32)
        for k in range(kv_heads):
            total = jnp.sum(sums[k], axis=0, keepdims=True)
            lse_ref[k, pl.ds(t, 1), :] = tops[k] * factor + jnp.log2(total)
            attended = (o_scr[k] * (1.0 / total)).T
            for g in range(groups):
                slab = attended[g * TILE : (g + 1) * TILE, :]
                upper = up_ref[pl.ds(base, TILE), head_columns(k * groups + g)].astype(jnp.float32)
                att_ref[pl.ds(base, TILE), head_columns(k * groups + g)] = slab
                squares += slab * slab
                inner += slab * upper
        stat_ref[pl.ds(base, TILE), 0:HEAD_SIZE] = squares
        stat_ref[pl.ds(base, TILE), HEAD_SIZE : 2 * HEAD_SIZE] = inner
        return carry

    lax.fori_loop(0, token_count // TILE, tile, 0)


def backward_kernel(
    steps_ref, list_ref, q_ref, up_ref, bkv_ref, anc_ref, bias_ref, hot_ref, seg_ref,
    att_ref, lse_ref, stat_ref, other_ref,
    norm_ref, dq_ref, dbr_ref, dpre_ref, acc_scr, dq_scr,
):
    owners, _, owned, _ = anc_ref.shape
    token_count, width = q_ref.shape
    kv_heads = bkv_ref.shape[2] // HEAD_SIZE
    groups = width // HEAD_SIZE // kv_heads
    lanes = groups * TILE
    near = REACH + TILE
    span = CHUNK * owned
    scaling = HEAD_SIZE ** (-0.5)
    factor = scaling * LOG2E
    columns = QUERY_HEADS * HEAD_SIZE
    acc_scr[...] = jnp.zeros_like(acc_scr)
    dbr_ref[...] = jnp.zeros_like(dbr_ref)
    lane = lax.broadcasted_iota(jnp.int32, (TILE, HEAD_SIZE), 1)
    ones = (lax.broadcasted_iota(jnp.int32, (span, HEAD_SIZE), 1) < 3).astype(jnp.bfloat16)

    def tile(t, carry):
        base = pl.multiple_of(t * TILE, TILE)
        steps = steps_ref[t]
        hot = jnp.concatenate([hot_ref[pl.ds(base, TILE), :]] * groups, axis=0)
        q = [stacked(q_ref, base, k, groups) for k in range(kv_heads)]
        qx = [jnp.concatenate([part, hot], axis=1) for part in q]
        window, allowed = self_window(base, seg_ref[pl.ds(t, 1), :], lanes)
        stats = stat_ref[pl.ds(base, TILE), :] + other_ref[pl.ds(base, TILE), :]
        squares = jnp.sum(stats[:, :HEAD_SIZE], axis=1, keepdims=True)
        inner = jnp.sum(stats[:, HEAD_SIZE:], axis=1, keepdims=True)
        scaler = lax.rsqrt(squares / columns + EPSILON)
        pull = scaler * scaler * scaler * inner / columns
        d_out, d_outx, lse = [], [], []
        for k in range(kv_heads):
            slabs, extra = [], []
            for g in range(groups):
                place = (pl.ds(base, TILE), head_columns(k * groups + g))
                slab = att_ref[place]
                norm_ref[place] = slab * scaler
                upper = up_ref[place].astype(jnp.float32)
                rounded = (scaler * upper - slab * pull).astype(jnp.bfloat16)
                delta = -jnp.sum(rounded.astype(jnp.float32) * slab, axis=1, keepdims=True)
                first = delta.astype(jnp.bfloat16).astype(jnp.float32)
                second = (delta - first).astype(jnp.bfloat16).astype(jnp.float32)
                third = delta - first - second
                parts = jnp.where(lane == 0, first, jnp.where(lane == 1, second, third))
                extra.append(jnp.where(lane < 3, parts, 0.0).astype(jnp.bfloat16))
                slabs.append(rounded)
            d_out.append(jnp.concatenate(slabs, axis=0))
            d_outx.append(jnp.concatenate([d_out[k], jnp.concatenate(extra, axis=0)], axis=1))
            lse.append(lse_ref[k, pl.ds(t, 1), :])

        for k in range(kv_heads):
            keys = bkv_ref[0, pl.ds(window, near), head_columns(k)]
            values = bkv_ref[1, pl.ds(window, near), head_columns(k)]
            scores = dot(keys, q[k], ROWS_BY_ROWS)
            weights = jnp.where(allowed, jnp.exp2(scores * factor - lse[k]), 0.0)
            valued = jnp.concatenate([values, ones[:near]], axis=1)
            d_scores = (weights * dot(valued, d_outx[k], ROWS_BY_ROWS)).astype(jnp.bfloat16)
            dbr_ref[0, pl.ds(window, near), head_columns(k)] += dot(d_scores, q[k], PLAIN) * scaling
            dbr_ref[1, pl.ds(window, near), head_columns(k)] += dot(
                weights.astype(jnp.bfloat16), d_out[k], PLAIN
            )
            dq_scr[k] = dot(keys, d_scores, COLS_BY_COLS)

        def step(c, carry):
            ids, clipped = chunk_ids(list_ref, t, c, owners)
            bias = jnp.concatenate([bias_ref[j] for j in ids for _ in range(2)], axis=0)
            for k in range(kv_heads):
                keys = jnp.concatenate([anc_ref[j, 0, :, head_columns(k)] for j in clipped], axis=0)
                values = jnp.concatenate([anc_ref[j, 1, :, head_columns(k)] for j in clipped], axis=0)
                scores = dot(jnp.concatenate([keys, bias], axis=1), qx[k], ROWS_BY_ROWS)
                weights = jnp.exp2(scores * factor - lse[k])
                valued = jnp.concatenate([values, ones], axis=1)
                d_scores = (weights * dot(valued, d_outx[k], ROWS_BY_ROWS)).astype(jnp.bfloat16)
                d_values = dot(weights.astype(jnp.bfloat16), d_out[k], PLAIN)
                d_keys = dot(d_scores, q[k], PLAIN)
                dq_scr[k] += dot(keys, d_scores, COLS_BY_COLS)
                for i, j in enumerate(clipped):
                    rows = slice(i * owned, (i + 1) * owned)
                    acc_scr[j, 0, :, head_columns(k)] += d_keys[rows]
                    acc_scr[j, 1, :, head_columns(k)] += d_values[rows]
            return carry

        lax.fori_loop(0, steps, step, 0)
        for k in range(kv_heads):
            d_query = (dq_scr[k] * scaling).T
            for g in range(groups):
                dq_ref[pl.ds(base, TILE), head_columns(k * groups + g)] = d_query[
                    g * TILE : (g + 1) * TILE, :
                ]
        return carry

    lax.fori_loop(0, token_count // TILE, tile, 0)

    def finish(j, carry):
        dpre_ref[j, 0] = (acc_scr[j, 0] * scaling).astype(jnp.bfloat16)
        dpre_ref[j, 1] = acc_scr[j, 1].astype(jnp.bfloat16)
        return carry

    lax.fori_loop(0, owners, finish, 0)


def call(kernel, scalars, arrays, outs, scratch):
    return pl.pallas_call(
        kernel,
        out_shape=outs,
        in_specs=[pl.BlockSpec(memory_space=pltpu.SMEM)] * scalars
        + [pl.BlockSpec(memory_space=pltpu.VMEM)] * (len(arrays) - scalars),
        out_specs=[pl.BlockSpec(memory_space=pltpu.VMEM)] * len(outs),
        scratch_shapes=scratch,
        compiler_params=pltpu.CompilerParams(vmem_limit_bytes=56 * 1024 * 1024),
    )(*arrays)


def prepare(seg_lengths, anc_rows, token_count, groups):
    segments, owners = anc_rows.shape
    order = jnp.arange(segments, dtype=jnp.int32)
    finish = jnp.sum(jnp.where(order[:, None] <= order[None, :], seg_lengths[:, None], 0), axis=0)
    begin = finish - seg_lengths
    positions = jnp.arange(token_count, dtype=jnp.int32)
    member = (positions[:, None] >= begin) & (positions[:, None] < finish)
    starts = jnp.sum(jnp.where(member, begin, 0), axis=1)
    seg = jnp.tile(starts.reshape(token_count // TILE, TILE), (1, groups))
    column = jnp.arange(HEAD_SIZE, dtype=jnp.int32)
    hot = jnp.sum(
        jnp.where(member[:, :, None] & (column == order[:, None]), 1.0, 0.0), axis=1
    ).astype(jnp.bfloat16)
    banned = jnp.concatenate([anc_rows == 0, jnp.ones((segments, 1), bool)], axis=1)
    bias = jnp.sum(
        jnp.where(banned[:, :, None] & (column == order[:, None, None]), NEGATIVE, 0.0), axis=0
    ).astype(jnp.bfloat16)
    bias = jnp.broadcast_to(bias[:, None, :], (owners + 1, 16, HEAD_SIZE))
    tiles = jnp.arange(token_count // TILE, dtype=jnp.int32)[:, None] * TILE
    active = (begin < tiles + TILE) & (finish > tiles)
    union = jnp.any(active[:, :, None] & (anc_rows != 0), axis=1)
    each = jnp.arange(owners, dtype=jnp.int32)
    place = jnp.sum((union[:, None, :] & (each[None, :] < each[:, None])).astype(jnp.int32), axis=2)
    counts = jnp.sum(union.astype(jnp.int32), axis=1)
    hit = union[:, None, :] & (place[:, None, :] == each[:, None])
    listed = jnp.sum(jnp.where(hit, each, 0), axis=2)
    listed = jnp.where(each < counts[:, None], listed, owners)
    return (counts + CHUNK - 1) // CHUNK, listed, bias, hot, seg


def local(queries, branch_kv, ancestor_key_value, upstream, lengths, ancestors):
    token_count, width = queries.shape
    kv_heads = branch_kv.shape[2] // HEAD_SIZE
    groups = width // HEAD_SIZE // kv_heads
    owners = ancestors.shape[1]
    owned = ancestor_key_value.shape[1]
    tiles = token_count // TILE
    lanes = groups * TILE
    steps, listed, bias, hot, seg = prepare(lengths[0], ancestors, token_count, groups)
    copies = jnp.broadcast_to(ancestor_key_value[None], (owners,) + ancestor_key_value.shape)
    gathered = lax.all_to_all(copies, ("dp", "leaf"), 0, 0, tiled=True)
    shared = [steps, listed, queries, upstream, branch_kv, gathered, bias, hot, seg]
    f32 = jnp.float32
    attended, lse, stats = call(
        forward_kernel, 2, shared,
        [
            jax.ShapeDtypeStruct((token_count, width), f32),
            jax.ShapeDtypeStruct((kv_heads, tiles, lanes), f32),
            jax.ShapeDtypeStruct((token_count, 2 * HEAD_SIZE), f32),
        ],
        [
            pltpu.VMEM((kv_heads, REACH + TILE + owners * owned, lanes), f32),
            pltpu.VMEM((kv_heads, HEAD_SIZE, lanes), f32),
        ],
    )
    other = lax.ppermute(stats, "head", [(0, 1), (1, 0)])
    normed, d_queries, d_branch, terms = call(
        backward_kernel, 2, shared + [attended, lse, stats, other],
        [
            jax.ShapeDtypeStruct((token_count, width), f32),
            jax.ShapeDtypeStruct((token_count, width), f32),
            jax.ShapeDtypeStruct(branch_kv.shape, f32),
            jax.ShapeDtypeStruct((owners,) + ancestor_key_value.shape, jnp.bfloat16),
        ],
        [
            pltpu.VMEM((owners,) + ancestor_key_value.shape, f32),
            pltpu.VMEM((kv_heads, HEAD_SIZE, lanes), f32),
        ],
    )
    received = lax.all_to_all(terms, ("dp", "leaf"), 0, 0, tiled=True)
    summed = jnp.sum(received.astype(f32), axis=0)
    return (normed, d_queries, d_branch, summed)


def solution(mesh):
    placed = (
        P(("dp", "leaf"), "head"),
        P(None, ("dp", "leaf"), "head"),
        P(None, ("dp", "leaf"), "head"),
        P(("dp", "leaf"), "head"),
        P(("dp", "leaf"), None),
        P(("dp", "leaf"), None),
    )
    return jax.shard_map(
        local,
        mesh=mesh,
        in_specs=placed,
        out_specs=(
            P(("dp", "leaf"), "head"),
            P(("dp", "leaf"), "head"),
            P(None, ("dp", "leaf"), "head"),
            P(None, ("dp", "leaf"), "head"),
        ),
        check_vma=False,
    )
```

```python
import jax
import jax.numpy as jnp
from jax import lax
from jax.experimental import pallas as pl
from jax.experimental.pallas import tpu as pltpu
from jax.sharding import PartitionSpec as P

QUERY_HEADS = 32
HEAD_SIZE = 128
NEGATIVE = -1e30
EPSILON = 1e-05
RANGE = 1e25
LOG2E = 1.4426950408889634

TILE = 64
CHUNK = 8
REACH = 128
SEGMENTS = 4
SCALING = HEAD_SIZE ** (-0.5)
FACTOR = SCALING * LOG2E

ROWS_BY_ROWS = (((1,), (1,)), ((), ()))
COLS_BY_COLS = (((0,), (0,)), ((), ()))
PLAIN = (((1,), (0,)), ((), ()))


def dot(a, b, dims):
    return lax.dot_general(a, b, dims, preferred_element_type=jnp.float32)


def head_columns(index):
    return pl.ds(index * HEAD_SIZE, HEAD_SIZE)


def stacked(ref, kv_head, groups):
    return jnp.concatenate(
        [ref[:, head_columns(kv_head * groups + g)] for g in range(groups)], axis=0
    )


def halves(values, op):
    return op(values[:, :HEAD_SIZE], values[:, HEAD_SIZE:])


def column(values):
    lane = lax.broadcasted_iota(jnp.int32, values.shape[:1] + (HEAD_SIZE,), 1)
    first = values.astype(jnp.bfloat16).astype(jnp.float32)
    second = (values - first).astype(jnp.bfloat16).astype(jnp.float32)
    return lane, first, second, values - first - second


def pieces(values, place):
    lane, first, second, third = column(values)
    parts = jnp.where(lane == place, first, jnp.where(lane == place + 1, second, third))
    wanted = (lane >= place) & (lane < place + 3)
    return jnp.where(wanted, parts, 0.0).astype(jnp.bfloat16)


def allowed_keys(t, starts, shape, key_axis):
    window = pl.multiple_of(jnp.maximum(t * TILE - REACH, 0), TILE)
    keys = window + lax.broadcasted_iota(jnp.int32, shape, key_axis)
    tokens = t * TILE + (lax.broadcasted_iota(jnp.int32, shape, 1 - key_axis) & (TILE - 1))
    return window, (keys <= tokens) & (keys >= starts)


def chunk_ids(list_ref, t, c, owners):
    ids = [list_ref[t, c * CHUNK + i] for i in range(CHUNK)]
    return ids, [jnp.minimum(j, owners - 1) for j in ids]


def chunk_rows(anc_ref, clipped, part, kv_head):
    return jnp.concatenate([anc_ref[j, part, :, head_columns(kv_head)] for j in clipped], axis=0)


def chunk_bias(bias_ref, ids):
    return jnp.concatenate([bias_ref[j] for j in ids for _ in range(2)], axis=0)


def row_pieces(values, place):
    first = values.astype(jnp.bfloat16).astype(jnp.float32)
    second = (values - first).astype(jnp.bfloat16).astype(jnp.float32)
    third = values - first - second
    row = lax.broadcasted_iota(jnp.int32, (HEAD_SIZE, values.shape[1]), 0)
    parts = jnp.where(row == place, first, jnp.where(row == place + 1, second, third))
    return jnp.where((row >= place) & (row < place + 3), parts, 0.0).T.astype(jnp.bfloat16)


def near_kernel(q_ref, bkv_ref, row_ref, hot_ref, out_ref, tail_ref, both_ref):
    t = pl.program_id(0)
    kv_heads = bkv_ref.shape[2] // HEAD_SIZE
    groups = q_ref.shape[1] // HEAD_SIZE // kv_heads
    rows, near = groups * TILE, REACH + TILE
    hot = jnp.concatenate([hot_ref[...]] * groups, axis=0)
    window, allowed = allowed_keys(t, row_ref[0], (near, rows), 0)
    for k in range(kv_heads):
        keys = bkv_ref[0, pl.ds(window, near), head_columns(k)]
        values = bkv_ref[1, pl.ds(window, near), head_columns(k)]
        scores = jnp.where(allowed, dot(keys, stacked(q_ref, k, groups), ROWS_BY_ROWS), NEGATIVE)
        top = jnp.max(scores, axis=0, keepdims=True)
        weights = jnp.exp2((scores - top) * FACTOR)
        out_ref[0, k] = dot(values, weights.astype(jnp.bfloat16), COLS_BY_COLS)
        tail_ref[0, k] = hot + row_pieces(-top, SEGMENTS)
        both_ref[0, k, 0:1, :] = top
        both_ref[0, k, 1:2, :] = jnp.sum(weights, axis=0, keepdims=True)


def fold(values, op):
    rows, width = values.shape
    return op(values.reshape(rows // 8, 8, width), axis=0)


def forward_kernel(
    steps_ref, list_ref, q_ref, up_ref, anc_ref, bias_ref, hot_ref, near_ref, near_tail_ref, both_ref,
    att_ref, tail_ref, stat_ref, shift_scr, sum_scr, o_scr,
):
    t = pl.program_id(0)
    owners = anc_ref.shape[0]
    kv_heads = near_ref.shape[1]
    groups = q_ref.shape[1] // HEAD_SIZE // kv_heads
    rows = groups * TILE
    steps = steps_ref[t]
    hot = jnp.concatenate([hot_ref[...]] * groups, axis=0)
    q = [stacked(q_ref, k, groups) for k in range(kv_heads)]
    near_tops = [both_ref[0, k, 0:1, :] for k in range(kv_heads)]

    def gather_all(tails):
        qx = [jnp.concatenate([q[k], tails[k]], axis=1) for k in range(kv_heads)]

        def gather(c, sums):
            ids, clipped = chunk_ids(list_ref, t, c, owners)
            bias = chunk_bias(bias_ref, ids)
            out = []
            for k in range(kv_heads):
                keys = jnp.concatenate([chunk_rows(anc_ref, clipped, 0, k), bias], axis=1)
                weights = jnp.exp2(dot(keys, qx[k], ROWS_BY_ROWS) * FACTOR)
                out.append(sums[k] + fold(weights, jnp.sum))
                o_scr[k] += dot(chunk_rows(anc_ref, clipped, 1, k), weights.astype(jnp.bfloat16), COLS_BY_COLS)
            return tuple(out)

        sums = lax.fori_loop(0, steps, gather, (jnp.zeros((8, rows), jnp.float32),) * kv_heads)
        for k in range(kv_heads):
            sum_scr[k] = jnp.sum(sums[k], axis=0, keepdims=True)

    for k in range(kv_heads):
        o_scr[k] = near_ref[0, k]
        shift_scr[k] = near_tops[k]
    gather_all([near_tail_ref[0, k] for k in range(kv_heads)])

    largest = jnp.max(jnp.maximum(sum_scr[0], sum_scr[1]))

    @pl.when(jnp.logical_not(largest < RANGE))
    def _():
        plain = [jnp.concatenate([q[k], hot], axis=1) for k in range(kv_heads)]

        def score(c, tops):
            ids, clipped = chunk_ids(list_ref, t, c, owners)
            bias = chunk_bias(bias_ref, ids)
            out = []
            for k in range(kv_heads):
                keys = jnp.concatenate([chunk_rows(anc_ref, clipped, 0, k), bias], axis=1)
                out.append(jnp.maximum(tops[k], fold(dot(keys, plain[k], ROWS_BY_ROWS), jnp.max)))
            return tuple(out)

        start = jnp.full((8, rows), NEGATIVE, jnp.float32)
        tops = lax.fori_loop(0, steps, score, (start,) * kv_heads)
        tails = []
        for k in range(kv_heads):
            top = jnp.maximum(jnp.max(tops[k], axis=0, keepdims=True), near_tops[k])
            shift_scr[k] = top
            tails.append(hot + row_pieces(-top, SEGMENTS))
            o_scr[k] = jnp.exp2((near_tops[k] - top) * FACTOR) * near_ref[0, k]
        gather_all(tails)

    squares = jnp.zeros((TILE, HEAD_SIZE), jnp.float32)
    inner = jnp.zeros((TILE, HEAD_SIZE), jnp.float32)
    for k in range(kv_heads):
        shift = shift_scr[k]
        total = sum_scr[k] + jnp.exp2((near_tops[k] - shift) * FACTOR) * both_ref[0, k, 1:2, :]
        attended = (o_scr[k] * (1.0 / total)).T
        tail_ref[0, k] = hot + row_pieces(-(shift + jnp.log2(total) * (1.0 / FACTOR)), SEGMENTS)
        for g in range(groups):
            slab = attended[g * TILE : (g + 1) * TILE, :]
            upper = up_ref[:, head_columns(k * groups + g)].astype(jnp.float32)
            att_ref[:, head_columns(k * groups + g)] = slab
            squares += slab * slab
            inner += slab * upper
    stat_ref[:, 0:HEAD_SIZE] = squares
    stat_ref[:, HEAD_SIZE : 2 * HEAD_SIZE] = inner


def norm_terms(stat_ref, other_ref):
    columns = QUERY_HEADS * HEAD_SIZE
    stats = stat_ref[...] + other_ref[...]
    squares = jnp.sum(stats[:, :HEAD_SIZE], axis=1, keepdims=True)
    inner = jnp.sum(stats[:, HEAD_SIZE:], axis=1, keepdims=True)
    scaler = lax.rsqrt(squares / columns + EPSILON)
    return scaler, scaler * scaler * scaler * inner / columns


def output_gradients(att_ref, up_ref, scaler, pull, kv_heads, groups):
    found, extended = [], []
    for k in range(kv_heads):
        slabs, extra = [], []
        for g in range(groups):
            slab = att_ref[:, head_columns(k * groups + g)]
            upper = up_ref[:, head_columns(k * groups + g)].astype(jnp.float32)
            rounded = (scaler * upper - slab * pull).astype(jnp.bfloat16)
            delta = jnp.sum(rounded.astype(jnp.float32) * slab, axis=1, keepdims=True)
            extra.append(pieces(-delta, 0))
            slabs.append(rounded)
        found.append(jnp.concatenate(slabs, axis=0))
        extended.append(jnp.concatenate([found[k], jnp.concatenate(extra, axis=0)], axis=1))
    return found, extended


def ones_columns(rows, place):
    lane = lax.broadcasted_iota(jnp.int32, (rows, HEAD_SIZE), 1)
    return ((lane >= place) & (lane < place + 3)).astype(jnp.bfloat16)


def shared_gradient_kernel(
    steps_ref, list_ref, q_ref, up_ref, anc_ref, bias_ref, att_ref, tail_ref, stat_ref, other_ref,
    terms_ref, acc_scr,
):
    t = pl.program_id(0)
    owners, _, owned, _ = anc_ref.shape
    kv_heads = tail_ref.shape[1]
    groups = q_ref.shape[1] // HEAD_SIZE // kv_heads
    scaler, pull = norm_terms(stat_ref, other_ref)
    d_out, d_outx = output_gradients(att_ref, up_ref, scaler, pull, kv_heads, groups)
    q = [stacked(q_ref, k, groups) for k in range(kv_heads)]
    qx = [jnp.concatenate([q[k], tail_ref[0, k]], axis=1) for k in range(kv_heads)]
    ones = ones_columns(CHUNK * owned, 0)

    @pl.when(t == 0)
    def _():
        acc_scr[...] = jnp.zeros_like(acc_scr)

    def step(c, carry):
        ids, clipped = chunk_ids(list_ref, t, c, owners)
        bias = chunk_bias(bias_ref, ids)
        for k in range(kv_heads):
            keys = jnp.concatenate([chunk_rows(anc_ref, clipped, 0, k), bias], axis=1)
            values = jnp.concatenate([chunk_rows(anc_ref, clipped, 1, k), ones], axis=1)
            weights = jnp.exp2(dot(keys, qx[k], ROWS_BY_ROWS) * FACTOR)
            d_scores = (weights * dot(values, d_outx[k], ROWS_BY_ROWS)).astype(jnp.bfloat16)
            d_values = dot(weights.astype(jnp.bfloat16), d_out[k], PLAIN)
            d_keys = dot(d_scores, q[k], PLAIN)
            for i, j in enumerate(clipped):
                rows = slice(i * owned, (i + 1) * owned)
                acc_scr[j, 0, :, head_columns(k)] += d_keys[rows]
                acc_scr[j, 1, :, head_columns(k)] += d_values[rows]
        return carry

    lax.fori_loop(0, steps_ref[t], step, 0)

    @pl.when(t == pl.num_programs(0) - 1)
    def _():
        def finish(j, carry):
            terms_ref[j, 0] = (acc_scr[j, 0] * SCALING).astype(jnp.bfloat16)
            terms_ref[j, 1] = acc_scr[j, 1].astype(jnp.bfloat16)
            return carry

        lax.fori_loop(0, owners, finish, 0)


def own_gradient_kernel(
    steps_ref, list_ref, q_ref, up_ref, anc_ref, bias_ref, att_ref, tail_ref, stat_ref, other_ref,
    bkv_ref, row_ref, norm_ref, dq_ref, dbr_ref, dq_scr,
):
    t = pl.program_id(0)
    owners, _, owned, _ = anc_ref.shape
    kv_heads = tail_ref.shape[1]
    groups = q_ref.shape[1] // HEAD_SIZE // kv_heads
    rows, near = groups * TILE, REACH + TILE
    scaler, pull = norm_terms(stat_ref, other_ref)
    norm_ref[...] = att_ref[...] * scaler
    d_out, d_outx = output_gradients(att_ref, up_ref, scaler, pull, kv_heads, groups)
    q = [stacked(q_ref, k, groups) for k in range(kv_heads)]
    qx = [jnp.concatenate([q[k], tail_ref[0, k]], axis=1) for k in range(kv_heads)]
    ones = ones_columns(CHUNK * owned, 0)

    @pl.when(t == 0)
    def _():
        dbr_ref[...] = jnp.zeros_like(dbr_ref)

    window, allowed = allowed_keys(t, row_ref[0], (near, rows), 0)
    for k in range(kv_heads):
        keys = bkv_ref[0, pl.ds(window, near), head_columns(k)]
        values = bkv_ref[1, pl.ds(window, near), head_columns(k)]
        keysx = jnp.concatenate([keys, ones_columns(near, SEGMENTS)], axis=1)
        valuesx = jnp.concatenate([values, ones[:near]], axis=1)
        weights = jnp.where(allowed, jnp.exp2(dot(keysx, qx[k], ROWS_BY_ROWS) * FACTOR), 0.0)
        d_scores = (weights * dot(valuesx, d_outx[k], ROWS_BY_ROWS)).astype(jnp.bfloat16)
        dbr_ref[0, pl.ds(window, near), head_columns(k)] += dot(d_scores, q[k], PLAIN) * SCALING
        dbr_ref[1, pl.ds(window, near), head_columns(k)] += dot(
            weights.astype(jnp.bfloat16), d_out[k], PLAIN
        )
        dq_scr[k] = dot(d_scores, keys, COLS_BY_COLS)

    def step(c, carry):
        ids, clipped = chunk_ids(list_ref, t, c, owners)
        bias = chunk_bias(bias_ref, ids)
        for k in range(kv_heads):
            keys = chunk_rows(anc_ref, clipped, 0, k)
            values = jnp.concatenate([chunk_rows(anc_ref, clipped, 1, k), ones], axis=1)
            scores = dot(qx[k], jnp.concatenate([keys, bias], axis=1), ROWS_BY_ROWS)
            weights = jnp.exp2(scores * FACTOR)
            d_scores = (weights * dot(d_outx[k], values, ROWS_BY_ROWS)).astype(jnp.bfloat16)
            dq_scr[k] += dot(d_scores, keys, PLAIN)
        return carry

    lax.fori_loop(0, steps_ref[t], step, 0)
    for k in range(kv_heads):
        d_query = dq_scr[k] * SCALING
        for g in range(groups):
            dq_ref[:, head_columns(k * groups + g)] = d_query[g * TILE : (g + 1) * TILE, :]


def call(kernel, tiles, ins, outs, scratch=()):
    def spec(array, tiled):
        if tiled is None:
            return pl.BlockSpec(memory_space=pltpu.SMEM)
        if not tiled:
            return pl.BlockSpec(array.shape, lambda t: (0,) * len(array.shape))
        block = (array.shape[0] // tiles,) + array.shape[1:]
        return pl.BlockSpec(block, lambda t: (t,) + (0,) * (len(array.shape) - 1))

    return pl.pallas_call(
        kernel,
        grid=(tiles,),
        in_specs=[spec(*one) for one in ins],
        out_shape=[one[0] for one in outs],
        out_specs=[spec(*one) for one in outs],
        scratch_shapes=list(scratch),
        compiler_params=pltpu.CompilerParams(vmem_limit_bytes=48 * 1024 * 1024),
    )(*[one[0] for one in ins])


def prepare(seg_lengths, anc_rows, token_count, groups):
    segments, owners = anc_rows.shape
    order = jnp.arange(segments, dtype=jnp.int32)
    finish = jnp.sum(jnp.where(order[:, None] <= order[None, :], seg_lengths[:, None], 0), axis=0)
    begin = finish - seg_lengths
    positions = jnp.arange(token_count, dtype=jnp.int32)
    member = (positions[:, None] >= begin) & (positions[:, None] < finish)
    starts = jnp.sum(jnp.where(member, begin, 0), axis=1)
    row = jnp.tile(starts.reshape(token_count // TILE, 1, TILE), (1, 1, groups))
    column = jnp.arange(HEAD_SIZE, dtype=jnp.int32)
    hot = jnp.sum(
        jnp.where(member[:, :, None] & (column == order[:, None]), 1.0, 0.0), axis=1
    ).astype(jnp.bfloat16)
    banned = jnp.concatenate([anc_rows == 0, jnp.ones((segments, 1), bool)], axis=1)
    bias = jnp.sum(
        jnp.where(banned[:, :, None] & (column == order[:, None, None]), NEGATIVE, 0.0), axis=0
    )
    bias = bias + jnp.where((column >= segments) & (column < segments + 3), 1.0, 0.0)
    bias = bias.astype(jnp.bfloat16)
    bias = jnp.broadcast_to(bias[:, None, :], (owners + 1, 16, HEAD_SIZE))
    tiles = jnp.arange(token_count // TILE, dtype=jnp.int32)[:, None] * TILE
    active = (begin < tiles + TILE) & (finish > tiles)
    union = jnp.any(active[:, :, None] & (anc_rows != 0), axis=1)
    each = jnp.arange(owners, dtype=jnp.int32)
    place = jnp.sum((union[:, None, :] & (each[None, :] < each[:, None])).astype(jnp.int32), axis=2)
    counts = jnp.sum(union.astype(jnp.int32), axis=1)
    hit = union[:, None, :] & (place[:, None, :] == each[:, None])
    listed = jnp.sum(jnp.where(hit, each, 0), axis=2)
    listed = jnp.where(each < counts[:, None], listed, owners)
    return (counts + CHUNK - 1) // CHUNK, listed, bias, hot, row


def local(queries, branch_kv, ancestor_key_value, upstream, lengths, ancestors):
    token_count, width = queries.shape
    kv_heads = branch_kv.shape[2] // HEAD_SIZE
    groups = width // HEAD_SIZE // kv_heads
    owners = ancestors.shape[1]
    owned = ancestor_key_value.shape[1]
    tiles = token_count // TILE
    rows = groups * TILE
    copies = jnp.broadcast_to(ancestor_key_value[None], (owners,) + ancestor_key_value.shape)
    gathered = lax.all_to_all(copies, ("dp", "leaf"), 0, 0, tiled=True)
    steps, listed, bias, hot, row = prepare(lengths[0], ancestors, token_count, groups)
    f32, bf16 = jnp.float32, jnp.bfloat16

    def new(shape, dtype=f32):
        return jax.ShapeDtypeStruct(shape, dtype)

    stack = (tiles, kv_heads, rows, HEAD_SIZE)
    near, near_tail, both = call(
        near_kernel, tiles,
        [(queries, True), (branch_kv, False), (row, True), (hot, True)],
        [
            (new((tiles, kv_heads, HEAD_SIZE, rows)), True), (new(stack, bf16), True),
            (new((tiles, kv_heads, 8, rows)), True),
        ],
    )
    attended, tail, stats = call(
        forward_kernel, tiles,
        [
            (steps, None), (listed, None), (queries, True), (upstream, True), (gathered, False),
            (bias, False), (hot, True), (near, True), (near_tail, True), (both, True),
        ],
        [(new((token_count, width)), True), (new(stack, bf16), True), (new((token_count, 2 * HEAD_SIZE)), True)],
        [
            pltpu.VMEM((kv_heads, 1, rows), f32), pltpu.VMEM((kv_heads, 1, rows), f32),
            pltpu.VMEM((kv_heads, HEAD_SIZE, rows), f32),
        ],
    )
    other = lax.ppermute(stats, "head", [(0, 1), (1, 0)])
    shared = [
        (steps, None), (listed, None), (queries, True), (upstream, True), (gathered, False),
        (bias, False), (attended, True), (tail, True), (stats, True), (other, True),
    ]
    (terms,) = call(
        shared_gradient_kernel, tiles, shared,
        [(new((owners,) + ancestor_key_value.shape, bf16), False)],
        [pltpu.VMEM((owners,) + ancestor_key_value.shape, f32)],
    )
    received = lax.all_to_all(terms, ("dp", "leaf"), 0, 0, tiled=True)
    normed, d_queries, d_branch = call(
        own_gradient_kernel, tiles, shared + [(branch_kv, False), (row, True)],
        [(new((token_count, width)), True), (new((token_count, width)), True), (new(branch_kv.shape), False)],
        [pltpu.VMEM((kv_heads, rows, HEAD_SIZE), f32)],
    )
    summed = jnp.sum(received.astype(f32), axis=0)
    return (normed, d_queries, d_branch, summed)


def solution(mesh):
    placed = (
        P(("dp", "leaf"), "head"),
        P(None, ("dp", "leaf"), "head"),
        P(None, ("dp", "leaf"), "head"),
        P(("dp", "leaf"), "head"),
        P(("dp", "leaf"), None),
        P(("dp", "leaf"), None),
    )
    return jax.shard_map(
        local,
        mesh=mesh,
        in_specs=placed,
        out_specs=(
            P(("dp", "leaf"), "head"),
            P(("dp", "leaf"), "head"),
            P(None, ("dp", "leaf"), "head"),
            P(None, ("dp", "leaf"), "head"),
        ),
        check_vma=False,
    )
```

```python
import jax
import jax.numpy as jnp
from jax import lax
from jax.experimental import pallas as pl
from jax.experimental.pallas import tpu as pltpu
from jax.sharding import PartitionSpec as P

QUERY_HEADS = 32
HEAD_SIZE = 128
NEGATIVE = -1e30
EPSILON = 1e-05
RANGE = 1e25
LOG2E = 1.4426950408889634

TILE = 64
CHUNK = 8
REACH = 128
SEGMENTS = 4
SCALING = HEAD_SIZE ** (-0.5)
FACTOR = SCALING * LOG2E

ROWS_BY_ROWS = (((1,), (1,)), ((), ()))
COLS_BY_COLS = (((0,), (0,)), ((), ()))
PLAIN = (((1,), (0,)), ((), ()))


def dot(a, b, dims):
    return lax.dot_general(a, b, dims, preferred_element_type=jnp.float32)


def head_columns(index):
    return pl.ds(index * HEAD_SIZE, HEAD_SIZE)


def stacked(ref, kv_head, groups):
    return jnp.concatenate(
        [ref[:, head_columns(kv_head * groups + g)] for g in range(groups)], axis=0
    )


def halves(values, op):
    return op(values[:, :HEAD_SIZE], values[:, HEAD_SIZE:])


def column(values):
    lane = lax.broadcasted_iota(jnp.int32, values.shape[:1] + (HEAD_SIZE,), 1)
    first = values.astype(jnp.bfloat16).astype(jnp.float32)
    second = (values - first).astype(jnp.bfloat16).astype(jnp.float32)
    return lane, first, second, values - first - second


def pieces(values, place):
    lane, first, second, third = column(values)
    parts = jnp.where(lane == place, first, jnp.where(lane == place + 1, second, third))
    wanted = (lane >= place) & (lane < place + 3)
    return jnp.where(wanted, parts, 0.0).astype(jnp.bfloat16)


def allowed_keys(t, starts, shape, key_axis):
    window = pl.multiple_of(jnp.maximum(t * TILE - REACH, 0), TILE)
    keys = window + lax.broadcasted_iota(jnp.int32, shape, key_axis)
    tokens = t * TILE + (lax.broadcasted_iota(jnp.int32, shape, 1 - key_axis) & (TILE - 1))
    return window, (keys <= tokens) & (keys >= starts)


def chunk_ids(list_ref, t, c, owners):
    ids = [list_ref[t, c * CHUNK + i] for i in range(CHUNK)]
    return ids, [jnp.minimum(j, owners - 1) for j in ids]


def chunk_rows(anc_ref, clipped, part, kv_head):
    return jnp.concatenate([anc_ref[j, part, :, head_columns(kv_head)] for j in clipped], axis=0)


def chunk_bias(bias_ref, ids):
    return jnp.concatenate([bias_ref[j] for j in ids for _ in range(2)], axis=0)


def row_pieces(values, place):
    first = values.astype(jnp.bfloat16).astype(jnp.float32)
    second = (values - first).astype(jnp.bfloat16).astype(jnp.float32)
    third = values - first - second
    row = lax.broadcasted_iota(jnp.int32, (HEAD_SIZE, values.shape[1]), 0)
    parts = jnp.where(row == place, first, jnp.where(row == place + 1, second, third))
    return jnp.where((row >= place) & (row < place + 3), parts, 0.0).T.astype(jnp.bfloat16)


def near_kernel(q_ref, bkv_ref, row_ref, hot_ref, out_ref, tail_ref, both_ref):
    t = pl.program_id(0)
    kv_heads = bkv_ref.shape[2] // HEAD_SIZE
    groups = q_ref.shape[1] // HEAD_SIZE // kv_heads
    rows, near = groups * TILE, REACH + TILE
    hot = jnp.concatenate([hot_ref[...]] * groups, axis=0)
    window, allowed = allowed_keys(t, row_ref[0], (near, rows), 0)
    for k in range(kv_heads):
        keys = bkv_ref[0, pl.ds(window, near), head_columns(k)]
        values = bkv_ref[1, pl.ds(window, near), head_columns(k)]
        scores = jnp.where(allowed, dot(keys, stacked(q_ref, k, groups), ROWS_BY_ROWS), NEGATIVE)
        top = jnp.max(scores, axis=0, keepdims=True)
        weights = jnp.exp2((scores - top) * FACTOR)
        out_ref[0, k] = dot(values, weights.astype(jnp.bfloat16), COLS_BY_COLS)
        tail_ref[0, k] = hot + row_pieces(-top, SEGMENTS)
        both_ref[0, k, 0:1, :] = top
        both_ref[0, k, 1:2, :] = jnp.sum(weights, axis=0, keepdims=True)


def fold(values, op):
    rows, width = values.shape
    return op(values.reshape(rows // 8, 8, width), axis=0)


def forward_kernel(
    steps_ref, list_ref, q_ref, near_tail_ref, q_old_ref, up_ref, near_ref, both_ref, hot_ref, anc_ref, bias_ref,
    att_ref, tail_ref, stat_ref, w_scr, sum_scr, o_scr, shift_scr,
):
    step = pl.program_id(0)
    tiles = pl.num_programs(0) - 1
    now, old = jnp.minimum(step, tiles - 1), jnp.maximum(step - 1, 0)
    owners = anc_ref.shape[0]
    kv_heads = near_ref.shape[1]
    groups = q_ref.shape[1] // HEAD_SIZE // kv_heads
    rows = groups * TILE

    def scored(t, c, qx):
        ids, clipped = chunk_ids(list_ref, t, c, owners)
        bias = chunk_bias(bias_ref, ids)
        keys = [jnp.concatenate([chunk_rows(anc_ref, clipped, 0, k), bias], axis=1) for k in range(kv_heads)]
        return [dot(keys[k], qx[k], ROWS_BY_ROWS) for k in range(kv_heads)]

    def weigh(t, c, qx):
        return [jnp.exp2(scores * FACTOR) for scores in scored(t, c, qx)]

    def valued(t, c):
        _, clipped = chunk_ids(list_ref, t, c, owners)
        return [dot(chunk_rows(anc_ref, clipped, 1, k), w_scr[k], COLS_BY_COLS) for k in range(kv_heads)]

    def keep(weights):
        for k in range(kv_heads):
            w_scr[k] = weights[k].astype(jnp.bfloat16)

    @pl.when(step == 0)
    def _():
        w_scr[...] = jnp.zeros_like(w_scr)
        sum_scr[...] = jnp.ones_like(sum_scr)
        o_scr[...] = jnp.zeros_like(o_scr)

    qx = [
        jnp.concatenate([stacked(q_ref, k, groups), near_tail_ref[0, k]], axis=1) for k in range(kv_heads)
    ]
    last = valued(old, jnp.maximum(steps_ref[old] - 1, 0))
    fresh = weigh(now, 0, qx)
    near_tops = [both_ref[0, k, 0:1, :] for k in range(kv_heads)]
    for k in range(kv_heads):
        o_scr[k] += last[k]
        sum_scr[k, 0:1, :] = jnp.sum(sum_scr[k], axis=0, keepdims=True)
        shift_scr[k] = near_tops[k]
    hot = jnp.concatenate([hot_ref[...]] * groups, axis=0)

    largest = jnp.max(jnp.maximum(sum_scr[0, 0:1, :], sum_scr[1, 0:1, :]))

    @pl.when(jnp.logical_not(largest < RANGE))
    def _():
        steps = steps_ref[old]
        q = [stacked(q_old_ref, k, groups) for k in range(kv_heads)]
        plain = [jnp.concatenate([q[k], hot], axis=1) for k in range(kv_heads)]

        def score(c, tops):
            scores = scored(old, c, plain)
            return tuple(jnp.maximum(tops[k], fold(scores[k], jnp.max)) for k in range(kv_heads))

        start = jnp.full((8, rows), NEGATIVE, jnp.float32)
        tops = lax.fori_loop(0, steps, score, (start,) * kv_heads)
        shifted = []
        for k in range(kv_heads):
            top = jnp.maximum(jnp.max(tops[k], axis=0, keepdims=True), near_tops[k])
            shift_scr[k] = top
            shifted.append(jnp.concatenate([q[k], hot + row_pieces(-top, SEGMENTS)], axis=1))
        o_scr[...] = jnp.zeros_like(o_scr)

        def gather(c, sums):
            weights = weigh(old, c, shifted)
            keep(weights)
            more = valued(old, c)
            for k in range(kv_heads):
                o_scr[k] += more[k]
            return tuple(sums[k] + fold(weights[k], jnp.sum) for k in range(kv_heads))

        sums = lax.fori_loop(0, steps, gather, (jnp.zeros((8, rows), jnp.float32),) * kv_heads)
        for k in range(kv_heads):
            sum_scr[k, 0:1, :] = jnp.sum(sums[k], axis=0, keepdims=True)

    squares = jnp.zeros((TILE, HEAD_SIZE), jnp.float32)
    inner = jnp.zeros((TILE, HEAD_SIZE), jnp.float32)
    for k in range(kv_heads):
        shift = shift_scr[k]
        fade = jnp.exp2((near_tops[k] - shift) * FACTOR)
        total = sum_scr[k, 0:1, :] + fade * both_ref[0, k, 1:2, :]
        attended = ((o_scr[k] + fade * near_ref[0, k]) * (1.0 / total)).T
        tail_ref[0, k] = hot + row_pieces(-(shift + jnp.log2(total) * (1.0 / FACTOR)), SEGMENTS)
        for g in range(groups):
            slab = attended[g * TILE : (g + 1) * TILE, :]
            upper = up_ref[:, head_columns(k * groups + g)].astype(jnp.float32)
            att_ref[:, head_columns(k * groups + g)] = slab
            squares += slab * slab
            inner += slab * upper
    stat_ref[:, 0:HEAD_SIZE] = squares
    stat_ref[:, HEAD_SIZE : 2 * HEAD_SIZE] = inner

    keep(fresh)
    for k in range(kv_heads):
        sum_scr[k] = fold(fresh[k], jnp.sum)
        o_scr[k] = jnp.zeros_like(o_scr[k])

    def advance(c, carry):
        more = valued(now, c - 1)
        weights = weigh(now, c, qx)
        keep(weights)
        for k in range(kv_heads):
            o_scr[k] += more[k]
            sum_scr[k] += fold(weights[k], jnp.sum)
        return carry

    lax.fori_loop(1, jnp.where(step < tiles, steps_ref[now], 0), advance, 0)


def norm_terms(stat_ref, other_ref):
    columns = QUERY_HEADS * HEAD_SIZE
    stats = stat_ref[...] + other_ref[...]
    squares = jnp.sum(stats[:, :HEAD_SIZE], axis=1, keepdims=True)
    inner = jnp.sum(stats[:, HEAD_SIZE:], axis=1, keepdims=True)
    scaler = lax.rsqrt(squares / columns + EPSILON)
    return scaler, scaler * scaler * scaler * inner / columns


def output_gradients(att_ref, up_ref, scaler, pull, kv_heads, groups):
    found, extended = [], []
    for k in range(kv_heads):
        slabs, extra = [], []
        for g in range(groups):
            slab = att_ref[:, head_columns(k * groups + g)]
            upper = up_ref[:, head_columns(k * groups + g)].astype(jnp.float32)
            rounded = (scaler * upper - slab * pull).astype(jnp.bfloat16)
            delta = jnp.sum(rounded.astype(jnp.float32) * slab, axis=1, keepdims=True)
            extra.append(pieces(-delta, 0))
            slabs.append(rounded)
        found.append(jnp.concatenate(slabs, axis=0))
        extended.append(jnp.concatenate([found[k], jnp.concatenate(extra, axis=0)], axis=1))
    return found, extended


def ones_columns(rows, place):
    lane = lax.broadcasted_iota(jnp.int32, (rows, HEAD_SIZE), 1)
    return ((lane >= place) & (lane < place + 3)).astype(jnp.bfloat16)


def gradient_scores(t, c, list_ref, anc_ref, bias_ref, ones, qx, d_outx):
    ids, clipped = chunk_ids(list_ref, t, c, anc_ref.shape[0])
    bias = chunk_bias(bias_ref, ids)
    weights, d_scores = [], []
    for k in range(len(qx)):
        keys = jnp.concatenate([chunk_rows(anc_ref, clipped, 0, k), bias], axis=1)
        values = jnp.concatenate([chunk_rows(anc_ref, clipped, 1, k), ones], axis=1)
        weights.append(jnp.exp2(dot(keys, qx[k], ROWS_BY_ROWS) * FACTOR))
        d_scores.append(weights[k] * dot(values, d_outx[k], ROWS_BY_ROWS))
    return weights, d_scores


def shared_gradient_kernel(
    steps_ref, list_ref, q_ref, up_ref, anc_ref, bias_ref, att_ref, tail_ref, stat_ref, other_ref,
    terms_ref, acc_scr, w_scr, ds_scr, q_scr, do_scr,
):
    t = pl.program_id(0)
    old = jnp.maximum(t - 1, 0)
    owners, _, owned, _ = anc_ref.shape
    kv_heads = tail_ref.shape[1]
    groups = q_ref.shape[1] // HEAD_SIZE // kv_heads
    ones = ones_columns(CHUNK * owned, 0)

    @pl.when(t == 0)
    def _():
        acc_scr[...] = jnp.zeros_like(acc_scr)
        w_scr[...] = jnp.zeros_like(w_scr)
        ds_scr[...] = jnp.zeros_like(ds_scr)
        q_scr[...] = jnp.zeros_like(q_scr)
        do_scr[...] = jnp.zeros_like(do_scr)

    def products():
        return [(dot(ds_scr[k], q_scr[k], PLAIN), dot(w_scr[k], do_scr[k], PLAIN)) for k in range(kv_heads)]

    def add(t, c, found):
        _, clipped = chunk_ids(list_ref, t, c, owners)
        for k in range(kv_heads):
            for i, j in enumerate(clipped):
                rows = slice(i * owned, (i + 1) * owned)
                for part in range(2):
                    acc_scr[j, part, :, head_columns(k)] += found[k][part][rows]

    def keep(weights, d_scores):
        for k in range(kv_heads):
            w_scr[k] = weights[k].astype(jnp.bfloat16)
            ds_scr[k] = d_scores[k].astype(jnp.bfloat16)

    found = products()
    scaler, pull = norm_terms(stat_ref, other_ref)
    d_out, d_outx = output_gradients(att_ref, up_ref, scaler, pull, kv_heads, groups)
    q = [stacked(q_ref, k, groups) for k in range(kv_heads)]
    qx = [jnp.concatenate([q[k], tail_ref[0, k]], axis=1) for k in range(kv_heads)]
    weights, d_scores = gradient_scores(t, 0, list_ref, anc_ref, bias_ref, ones, qx, d_outx)
    keep(weights, d_scores)
    for k in range(kv_heads):
        q_scr[k] = q[k]
        do_scr[k] = d_out[k]
    add(old, jnp.maximum(steps_ref[old] - 1, 0), found)

    def advance(c, carry):
        found = products()
        weights, d_scores = gradient_scores(t, c, list_ref, anc_ref, bias_ref, ones, qx, d_outx)
        keep(weights, d_scores)
        add(t, c - 1, found)
        return carry

    lax.fori_loop(1, steps_ref[t], advance, 0)

    @pl.when(t == pl.num_programs(0) - 1)
    def _():
        add(t, jnp.maximum(steps_ref[t] - 1, 0), products())

        def finish(j, carry):
            terms_ref[j, 0] = (acc_scr[j, 0] * SCALING).astype(jnp.bfloat16)
            terms_ref[j, 1] = acc_scr[j, 1].astype(jnp.bfloat16)
            return carry

        lax.fori_loop(0, owners, finish, 0)


def own_gradient_kernel(
    steps_ref, list_ref, q_ref, up_ref, anc_ref, bias_ref, att_ref, tail_ref, stat_ref, other_ref,
    bkv_ref, row_ref, norm_ref, dq_ref, dbr_ref, dq_scr, ds_scr,
):
    t = pl.program_id(0)
    owners, _, owned, _ = anc_ref.shape
    kv_heads = tail_ref.shape[1]
    groups = q_ref.shape[1] // HEAD_SIZE // kv_heads
    rows, near = groups * TILE, REACH + TILE
    scaler, pull = norm_terms(stat_ref, other_ref)
    norm_ref[...] = att_ref[...] * scaler
    d_out, d_outx = output_gradients(att_ref, up_ref, scaler, pull, kv_heads, groups)
    q = [stacked(q_ref, k, groups) for k in range(kv_heads)]
    qx = [jnp.concatenate([q[k], tail_ref[0, k]], axis=1) for k in range(kv_heads)]
    ones = ones_columns(CHUNK * owned, 0)

    @pl.when(t == 0)
    def _():
        dbr_ref[...] = jnp.zeros_like(dbr_ref)

    window, allowed = allowed_keys(t, row_ref[0], (near, rows), 0)
    for k in range(kv_heads):
        keys = bkv_ref[0, pl.ds(window, near), head_columns(k)]
        values = bkv_ref[1, pl.ds(window, near), head_columns(k)]
        keysx = jnp.concatenate([keys, ones_columns(near, SEGMENTS)], axis=1)
        valuesx = jnp.concatenate([values, ones[:near]], axis=1)
        weights = jnp.where(allowed, jnp.exp2(dot(keysx, qx[k], ROWS_BY_ROWS) * FACTOR), 0.0)
        d_scores = (weights * dot(valuesx, d_outx[k], ROWS_BY_ROWS)).astype(jnp.bfloat16)
        dbr_ref[0, pl.ds(window, near), head_columns(k)] += dot(d_scores, q[k], PLAIN) * SCALING
        dbr_ref[1, pl.ds(window, near), head_columns(k)] += dot(
            weights.astype(jnp.bfloat16), d_out[k], PLAIN
        )
        dq_scr[k] = dot(keys, d_scores, COLS_BY_COLS)

    def keep(d_scores):
        for k in range(kv_heads):
            ds_scr[k] = d_scores[k].astype(jnp.bfloat16)

    def pulled(c):
        _, clipped = chunk_ids(list_ref, t, c, owners)
        return [dot(chunk_rows(anc_ref, clipped, 0, k), ds_scr[k], COLS_BY_COLS) for k in range(kv_heads)]

    keep(gradient_scores(t, 0, list_ref, anc_ref, bias_ref, ones, qx, d_outx)[1])

    def advance(c, carry):
        more = pulled(c - 1)
        keep(gradient_scores(t, c, list_ref, anc_ref, bias_ref, ones, qx, d_outx)[1])
        for k in range(kv_heads):
            dq_scr[k] += more[k]
        return carry

    lax.fori_loop(1, steps_ref[t], advance, 0)
    more = pulled(jnp.maximum(steps_ref[t] - 1, 0))
    for k in range(kv_heads):
        d_query = ((dq_scr[k] + more[k]) * SCALING).T
        for g in range(groups):
            dq_ref[:, head_columns(k * groups + g)] = d_query[g * TILE : (g + 1) * TILE, :]


def copies_kernel(one_ref, many_ref):
    for i in range(many_ref.shape[0]):
        many_ref[i] = one_ref[...]


def total_kernel(terms_ref, sum_ref):
    part = jnp.sum(terms_ref[...].astype(jnp.float32), axis=0)

    @pl.when(pl.program_id(0) == 0)
    def _():
        sum_ref[...] = part

    @pl.when(pl.program_id(0) > 0)
    def _():
        sum_ref[...] += part


NOW, OLD = "now", "old"


def call(kernel, tiles, ins, outs, scratch=(), extra=0, limit=24):
    def spec(array, tiled):
        if tiled is None:
            return pl.BlockSpec(memory_space=pltpu.SMEM)
        rest = (0,) * (len(array.shape) - 1)
        if not tiled:
            return pl.BlockSpec(array.shape, lambda t: (0,) + rest, pipeline_mode=pl.Buffered(1))
        block = (array.shape[0] // tiles,) + array.shape[1:]
        if tiled == NOW:
            return pl.BlockSpec(block, lambda t: (jnp.minimum(t, tiles - 1),) + rest)
        if tiled == OLD:
            return pl.BlockSpec(block, lambda t: (jnp.maximum(t - 1, 0),) + rest)
        return pl.BlockSpec(block, lambda t: (t,) + rest)

    return pl.pallas_call(
        kernel,
        grid=(tiles + extra,),
        in_specs=[spec(*one) for one in ins],
        out_shape=[one[0] for one in outs],
        out_specs=[spec(*one) for one in outs],
        scratch_shapes=list(scratch),
        compiler_params=pltpu.CompilerParams(vmem_limit_bytes=limit * 1024 * 1024),
    )(*[one[0] for one in ins])


def prepare(seg_lengths, anc_rows, token_count, groups):
    segments, owners = anc_rows.shape
    order = jnp.arange(segments, dtype=jnp.int32)
    finish = jnp.sum(jnp.where(order[:, None] <= order[None, :], seg_lengths[:, None], 0), axis=0)
    begin = finish - seg_lengths
    positions = jnp.arange(token_count, dtype=jnp.int32)
    member = (positions[:, None] >= begin) & (positions[:, None] < finish)
    starts = jnp.sum(jnp.where(member, begin, 0), axis=1)
    row = jnp.tile(starts.reshape(token_count // TILE, 1, TILE), (1, 1, groups))
    column = jnp.arange(HEAD_SIZE, dtype=jnp.int32)
    hot = jnp.sum(
        jnp.where(member[:, :, None] & (column == order[:, None]), 1.0, 0.0), axis=1
    ).astype(jnp.bfloat16)
    banned = jnp.concatenate([anc_rows == 0, jnp.ones((segments, 1), bool)], axis=1)
    bias = jnp.sum(
        jnp.where(banned[:, :, None] & (column == order[:, None, None]), NEGATIVE, 0.0), axis=0
    )
    bias = bias + jnp.where((column >= segments) & (column < segments + 3), 1.0, 0.0)
    bias = bias.astype(jnp.bfloat16)
    bias = jnp.broadcast_to(bias[:, None, :], (owners + 1, 16, HEAD_SIZE))
    tiles = jnp.arange(token_count // TILE, dtype=jnp.int32)[:, None] * TILE
    active = (begin < tiles + TILE) & (finish > tiles)
    union = jnp.any(active[:, :, None] & (anc_rows != 0), axis=1)
    each = jnp.arange(owners, dtype=jnp.int32)
    place = jnp.sum((union[:, None, :] & (each[None, :] < each[:, None])).astype(jnp.int32), axis=2)
    counts = jnp.sum(union.astype(jnp.int32), axis=1)
    hit = union[:, None, :] & (place[:, None, :] == each[:, None])
    listed = jnp.sum(jnp.where(hit, each, 0), axis=2)
    listed = jnp.where(each < counts[:, None], listed, owners)
    return (counts + CHUNK - 1) // CHUNK, listed, bias, hot, row


def local(queries, branch_kv, ancestor_key_value, upstream, lengths, ancestors):
    token_count, width = queries.shape
    kv_heads = branch_kv.shape[2] // HEAD_SIZE
    groups = width // HEAD_SIZE // kv_heads
    owners = ancestors.shape[1]
    owned = ancestor_key_value.shape[1]
    tiles = token_count // TILE
    rows = groups * TILE
    each = (owners,) + ancestor_key_value.shape
    (copies,) = call(
        copies_kernel, 4, [(ancestor_key_value, False)], [(jax.ShapeDtypeStruct(each, jnp.bfloat16), True)]
    )
    gathered = lax.all_to_all(copies, ("dp", "leaf"), 0, 0, tiled=True)
    steps, listed, bias, hot, row = prepare(lengths[0], ancestors, token_count, groups)
    f32, bf16 = jnp.float32, jnp.bfloat16

    def new(shape, dtype=f32):
        return jax.ShapeDtypeStruct(shape, dtype)

    stack = (tiles, kv_heads, rows, HEAD_SIZE)
    near, near_tail, both = call(
        near_kernel, tiles,
        [(queries, True), (branch_kv, False), (row, True), (hot, True)],
        [
            (new((tiles, kv_heads, HEAD_SIZE, rows)), True), (new(stack, bf16), True),
            (new((tiles, kv_heads, 8, rows)), True),
        ],
    )
    attended, tail, stats = call(
        forward_kernel, tiles,
        [
            (steps, None), (listed, None), (queries, NOW), (near_tail, NOW), (queries, OLD), (upstream, OLD),
            (near, OLD), (both, OLD), (hot, OLD), (gathered, False), (bias, False),
        ],
        [(new((token_count, width)), OLD), (new(stack, bf16), OLD), (new((token_count, 2 * HEAD_SIZE)), OLD)],
        [
            pltpu.VMEM((kv_heads, CHUNK * owned, rows), bf16),
            pltpu.VMEM((kv_heads, 8, rows), f32),
            pltpu.VMEM((kv_heads, HEAD_SIZE, rows), f32),
            pltpu.VMEM((kv_heads, 1, rows), f32),
        ],
        extra=1,
    )
    other = lax.ppermute(stats, "head", [(0, 1), (1, 0)])
    shared = [
        (steps, None), (listed, None), (queries, True), (upstream, True), (gathered, False),
        (bias, False), (attended, True), (tail, True), (stats, True), (other, True),
    ]
    (terms,) = call(
        shared_gradient_kernel, tiles, shared,
        [(new(each, bf16), False)],
        [
            pltpu.VMEM(each, f32),
            pltpu.VMEM((kv_heads, CHUNK * owned, rows), bf16),
            pltpu.VMEM((kv_heads, CHUNK * owned, rows), bf16),
            pltpu.VMEM((kv_heads, rows, HEAD_SIZE), bf16),
            pltpu.VMEM((kv_heads, rows, HEAD_SIZE), bf16),
        ],
    )
    received = lax.all_to_all(terms, ("dp", "leaf"), 0, 0, tiled=True)
    normed, d_queries, d_branch = call(
        own_gradient_kernel, tiles, shared + [(branch_kv, False), (row, True)],
        [(new((token_count, width)), True), (new((token_count, width)), True), (new(branch_kv.shape), False)],
        [
            pltpu.VMEM((kv_heads, HEAD_SIZE, rows), f32),
            pltpu.VMEM((kv_heads, CHUNK * owned, rows), bf16),
        ],
    )
    (summed,) = call(total_kernel, 4, [(received, True)], [(new(ancestor_key_value.shape), False)])
    return (normed, d_queries, d_branch, summed)


def solution(mesh):
    placed = (
        P(("dp", "leaf"), "head"),
        P(None, ("dp", "leaf"), "head"),
        P(None, ("dp", "leaf"), "head"),
        P(("dp", "leaf"), "head"),
        P(("dp", "leaf"), None),
        P(("dp", "leaf"), None),
    )
    return jax.shard_map(
        local,
        mesh=mesh,
        in_specs=placed,
        out_specs=(
            P(("dp", "leaf"), "head"),
            P(("dp", "leaf"), "head"),
            P(None, ("dp", "leaf"), "head"),
            P(None, ("dp", "leaf"), "head"),
        ),
        check_vma=False,
    )
```

```python
import jax
import jax.numpy as jnp
from jax import lax
from jax.experimental import pallas as pl
from jax.experimental.pallas import tpu as pltpu
from jax.sharding import PartitionSpec as P

QUERY_HEADS = 32
HEAD_SIZE = 128
NEGATIVE = -1e30
EPSILON = 1e-05
RANGE = 1e25
PIECES = 8
LOG2E = 1.4426950408889634

TILE = 64
CHUNK = 8
REACH = 128
SEGMENTS = 4
SCALING = HEAD_SIZE ** (-0.5)
FACTOR = SCALING * LOG2E

ROWS_BY_ROWS = (((1,), (1,)), ((), ()))
COLS_BY_COLS = (((0,), (0,)), ((), ()))
PLAIN = (((1,), (0,)), ((), ()))


def dot(a, b, dims):
    return lax.dot_general(a, b, dims, preferred_element_type=jnp.float32)


def head_columns(index):
    return pl.ds(index * HEAD_SIZE, HEAD_SIZE)


def stacked(ref, kv_head, groups):
    return jnp.concatenate(
        [ref[:, head_columns(kv_head * groups + g)] for g in range(groups)], axis=0
    )


def halves(values, op):
    return op(values[:, :HEAD_SIZE], values[:, HEAD_SIZE:])


def column(values):
    lane = lax.broadcasted_iota(jnp.int32, values.shape[:1] + (HEAD_SIZE,), 1)
    first = values.astype(jnp.bfloat16).astype(jnp.float32)
    second = (values - first).astype(jnp.bfloat16).astype(jnp.float32)
    return lane, first, second, values - first - second


def pieces(values, place):
    lane, first, second, third = column(values)
    parts = jnp.where(lane == place, first, jnp.where(lane == place + 1, second, third))
    wanted = (lane >= place) & (lane < place + 3)
    return jnp.where(wanted, parts, 0.0).astype(jnp.bfloat16)


def allowed_keys(t, starts, shape, key_axis):
    window = pl.multiple_of(jnp.maximum(t * TILE - REACH, 0), TILE)
    keys = window + lax.broadcasted_iota(jnp.int32, shape, key_axis)
    tokens = t * TILE + (lax.broadcasted_iota(jnp.int32, shape, 1 - key_axis) & (TILE - 1))
    return window, (keys <= tokens) & (keys >= starts)


def chunk_ids(list_ref, t, c, owners):
    ids = [list_ref[t, c * CHUNK + i] for i in range(CHUNK)]
    return ids, [jnp.minimum(j, owners - 1) for j in ids]


def chunk_rows(anc_ref, clipped, part, kv_head):
    return jnp.concatenate([anc_ref[j, part, :, head_columns(kv_head)] for j in clipped], axis=0)


def chunk_bias(bias_ref, ids):
    return jnp.concatenate([bias_ref[j] for j in ids for _ in range(2)], axis=0)


def near_kernel(q_ref, bkv_ref, row_ref, out_ref, both_ref):
    t = pl.program_id(0)
    kv_heads = bkv_ref.shape[2] // HEAD_SIZE
    groups = q_ref.shape[1] // HEAD_SIZE // kv_heads
    rows, near = groups * TILE, REACH + TILE
    window, allowed = allowed_keys(t, row_ref[0], (near, rows), 0)
    for k in range(kv_heads):
        keys = bkv_ref[0, pl.ds(window, near), head_columns(k)]
        values = bkv_ref[1, pl.ds(window, near), head_columns(k)]
        scores = jnp.where(allowed, dot(keys, stacked(q_ref, k, groups), ROWS_BY_ROWS), NEGATIVE)
        top = jnp.max(scores, axis=0, keepdims=True)
        weights = jnp.exp2((scores - top) * FACTOR)
        out_ref[0, k] = dot(values, weights.astype(jnp.bfloat16), COLS_BY_COLS)
        both_ref[0, k, 0:1, :] = top
        both_ref[0, k, 1:2, :] = jnp.sum(weights, axis=0, keepdims=True)


def fold(values, op):
    rows, width = values.shape
    return op(values.reshape(rows // 8, 8, width), axis=0)


def tile_rows(ref, t):
    return ref.at[pl.ds(pl.multiple_of(t * TILE, TILE), TILE)]


def arrival(t, sems, pairs, first=0):
    moves = []
    for i, (far, near, stacked_tiles) in enumerate(pairs, first):
        if stacked_tiles:
            moves.append(pltpu.make_async_copy(far.at[t], near.at[t], sems.at[i, t]))
        else:
            moves.append(pltpu.make_async_copy(tile_rows(far, t), tile_rows(near, t), sems.at[i, t]))
    return moves


def forward_kernel(
    steps_ref, list_ref, q_far, up_far, near_far, both_far, hot_ref, anc_ref, bias_ref,
    att_far, lse_ref, stat_ref,
    q_all, up_all, near_all, both_ref, att_all, in_sems, out_sems, w_scr, sum_scr, o_scr, shift_scr,
):
    tiles, kv_heads, _, rows = both_ref.shape
    owners = anc_ref.shape[0]
    groups = rows // TILE
    early = [(q_far, q_all, False), (both_far, both_ref, True)]
    late = [(up_far, up_all, False), (near_far, near_all, True)]
    for t in range(tiles):
        for move in arrival(t, in_sems, early + late):
            move.start()

    def departure(t):
        return pltpu.make_async_copy(tile_rows(att_all, t), tile_rows(att_far, t), out_sems.at[t])

    def hot_of(t):
        return jnp.concatenate([tile_rows(hot_ref, t)[...]] * groups, axis=0)

    def queries_of(t):
        hot = hot_of(t)
        return [
            jnp.concatenate([stacked(tile_rows(q_all, t), k, groups), hot], axis=1) for k in range(kv_heads)
        ]

    def scored(t, c, qx):
        ids, clipped = chunk_ids(list_ref, t, c, owners)
        bias = chunk_bias(bias_ref, ids)
        keys = [jnp.concatenate([chunk_rows(anc_ref, clipped, 0, k), bias], axis=1) for k in range(kv_heads)]
        return [dot(keys[k], qx[k], ROWS_BY_ROWS) for k in range(kv_heads)]

    def weigh(t, c, qx, shifts):
        scores = scored(t, c, qx)
        return [jnp.exp2(scores[k] * FACTOR - shifts[k]) for k in range(kv_heads)]

    def valued(t, c):
        _, clipped = chunk_ids(list_ref, t, c, owners)
        return [dot(chunk_rows(anc_ref, clipped, 1, k), w_scr[k], COLS_BY_COLS) for k in range(kv_heads)]

    def keep(weights):
        for k in range(kv_heads):
            w_scr[k] = weights[k].astype(jnp.bfloat16)

    def near_shifts(t):
        return [both_ref[t, k, 0:1, :] * FACTOR for k in range(kv_heads)]

    def finish(old, last):
        near_tops = near_shifts(old)
        for k in range(kv_heads):
            o_scr[k] += last[k]
            sum_scr[k, 0:1, :] = jnp.sum(sum_scr[k], axis=0, keepdims=True)
            shift_scr[k] = near_tops[k]

        largest = jnp.max(jnp.maximum(sum_scr[0, 0:1, :], sum_scr[1, 0:1, :]))

        @pl.when(jnp.logical_not(largest < RANGE))
        def _():
            steps = steps_ref[old]
            qx = queries_of(old)

            def score(c, tops):
                scores = scored(old, c, qx)
                return tuple(jnp.maximum(tops[k], fold(scores[k], jnp.max)) for k in range(kv_heads))

            start = jnp.full((8, rows), NEGATIVE, jnp.float32)
            tops = lax.fori_loop(0, steps, score, (start,) * kv_heads)
            shifts = []
            for k in range(kv_heads):
                top = jnp.max(tops[k], axis=0, keepdims=True) * FACTOR
                shifts.append(jnp.maximum(top, near_tops[k]))
                shift_scr[k] = shifts[k]
            o_scr[...] = jnp.zeros_like(o_scr)

            def gather(c, sums):
                weights = weigh(old, c, qx, shifts)
                keep(weights)
                more = valued(old, c)
                for k in range(kv_heads):
                    o_scr[k] += more[k]
                return tuple(sums[k] + fold(weights[k], jnp.sum) for k in range(kv_heads))

            sums = lax.fori_loop(0, steps, gather, (jnp.zeros((8, rows), jnp.float32),) * kv_heads)
            for k in range(kv_heads):
                sum_scr[k, 0:1, :] = jnp.sum(sums[k], axis=0, keepdims=True)

        for move in arrival(old, in_sems, late, len(early)):
            move.wait()
        upper_ref, att_ref, stats_ref = tile_rows(up_all, old), tile_rows(att_all, old), tile_rows(stat_ref, old)
        squares = jnp.zeros((TILE, HEAD_SIZE), jnp.float32)
        inner = jnp.zeros((TILE, HEAD_SIZE), jnp.float32)
        for k in range(kv_heads):
            shift = shift_scr[k]
            fade = jnp.exp2(near_tops[k] - shift)
            total = sum_scr[k, 0:1, :] + fade * both_ref[old, k, 1:2, :]
            attended = ((o_scr[k] + fade * near_all[old, k]) * (1.0 / total)).T
            lse_ref[old, k, 0:1, :] = shift + jnp.log2(total)
            for g in range(groups):
                slab = attended[g * TILE : (g + 1) * TILE, :]
                upper = upper_ref[:, head_columns(k * groups + g)].astype(jnp.float32)
                att_ref[:, head_columns(k * groups + g)] = slab
                squares += slab * slab
                inner += slab * upper
        stats_ref[:, 0:HEAD_SIZE] = squares
        stats_ref[:, HEAD_SIZE : 2 * HEAD_SIZE] = inner
        departure(old).start()

    def tile(now, first):
        for move in arrival(now, in_sems, early):
            move.wait()
        old = now - 1
        qx, shifts = queries_of(now), near_shifts(now)
        if not first:
            last = valued(old, jnp.maximum(steps_ref[old] - 1, 0))
        fresh = weigh(now, 0, qx, shifts)
        if not first:
            finish(old, last)
        keep(fresh)
        for k in range(kv_heads):
            sum_scr[k] = fold(fresh[k], jnp.sum)
            o_scr[k] = jnp.zeros_like(o_scr[k])

        def advance(c, carry):
            more = valued(now, c - 1)
            weights = weigh(now, c, qx, shifts)
            keep(weights)
            for k in range(kv_heads):
                o_scr[k] += more[k]
                sum_scr[k] += fold(weights[k], jnp.sum)
            return carry

        lax.fori_loop(1, steps_ref[now], advance, 0)

    def later(now, carry):
        tile(now, False)
        return carry

    tile(0, True)
    lax.fori_loop(1, tiles, later, 0)
    finish(tiles - 1, valued(tiles - 1, jnp.maximum(steps_ref[tiles - 1] - 1, 0)))
    for t in range(tiles):
        departure(t).wait()


def norm_terms(stat_ref, other_ref):
    columns = QUERY_HEADS * HEAD_SIZE
    stats = stat_ref[...] + other_ref[...]
    squares = jnp.sum(stats[:, :HEAD_SIZE], axis=1, keepdims=True)
    inner = jnp.sum(stats[:, HEAD_SIZE:], axis=1, keepdims=True)
    scaler = lax.rsqrt(squares / columns + EPSILON)
    return scaler, scaler * scaler * scaler * inner / columns


def output_gradients(att_ref, up_ref, scaler, pull, kv_heads, groups):
    found, extended = [], []
    for k in range(kv_heads):
        slabs, extra = [], []
        for g in range(groups):
            slab = att_ref[:, head_columns(k * groups + g)]
            upper = up_ref[:, head_columns(k * groups + g)].astype(jnp.float32)
            rounded = (scaler * upper - slab * pull).astype(jnp.bfloat16)
            delta = jnp.sum(rounded.astype(jnp.float32) * slab, axis=1, keepdims=True)
            extra.append(pieces(-delta, 0))
            slabs.append(rounded)
        found.append(jnp.concatenate(slabs, axis=0))
        extended.append(jnp.concatenate([found[k], jnp.concatenate(extra, axis=0)], axis=1))
    return found, extended


def ones_columns(rows, place):
    lane = lax.broadcasted_iota(jnp.int32, (rows, HEAD_SIZE), 1)
    return ((lane >= place) & (lane < place + 3)).astype(jnp.bfloat16)


def gradient_scores(t, c, list_ref, anc_ref, bias_ref, ones, qx, d_outx, lse):
    ids, clipped = chunk_ids(list_ref, t, c, anc_ref.shape[0])
    bias = chunk_bias(bias_ref, ids)
    weights, d_scores = [], []
    for k in range(len(qx)):
        keys = jnp.concatenate([chunk_rows(anc_ref, clipped, 0, k), bias], axis=1)
        values = jnp.concatenate([chunk_rows(anc_ref, clipped, 1, k), ones], axis=1)
        weights.append(jnp.exp2(dot(keys, qx[k], ROWS_BY_ROWS) * FACTOR - lse[k]))
        d_scores.append(weights[k] * dot(values, d_outx[k], ROWS_BY_ROWS))
    return weights, d_scores


def shared_gradient_kernel(
    steps_ref, list_ref, q_far, up_far, att_far, stat_ref, other_ref, lse_ref, hot_ref, anc_ref, bias_ref,
    terms_far,
    q_all, up_all, att_all, in_sems, terms_scr, out_sems, acc_scr, w_scr, ds_scr, q_scr, do_scr,
):
    tiles, kv_heads, _, rows = lse_ref.shape
    groups = rows // TILE
    owners, _, owned, _ = anc_ref.shape
    ones = ones_columns(CHUNK * owned, 0)
    pairs = [(q_far, q_all, False), (up_far, up_all, False), (att_far, att_all, False)]
    for t in range(tiles):
        for move in arrival(t, in_sems, pairs):
            move.start()
    acc_scr[...] = jnp.zeros_like(acc_scr)

    def products():
        return [(dot(ds_scr[k], q_scr[k], PLAIN), dot(w_scr[k], do_scr[k], PLAIN)) for k in range(kv_heads)]

    def add(t, c, found):
        _, clipped = chunk_ids(list_ref, t, c, owners)
        for k in range(kv_heads):
            for i, j in enumerate(clipped):
                place = slice(i * owned, (i + 1) * owned)
                for part in range(2):
                    acc_scr[j, part, :, head_columns(k)] += found[k][part][place]

    def keep(weights, d_scores):
        for k in range(kv_heads):
            w_scr[k] = weights[k].astype(jnp.bfloat16)
            ds_scr[k] = d_scores[k].astype(jnp.bfloat16)

    def tile(t, first):
        for move in arrival(t, in_sems, pairs):
            move.wait()
        if not first:
            found = products()
        scaler, pull = norm_terms(tile_rows(stat_ref, t), tile_rows(other_ref, t))
        d_out, d_outx = output_gradients(
            tile_rows(att_all, t), tile_rows(up_all, t), scaler, pull, kv_heads, groups
        )
        q = [stacked(tile_rows(q_all, t), k, groups) for k in range(kv_heads)]
        hot = jnp.concatenate([tile_rows(hot_ref, t)[...]] * groups, axis=0)
        qx = [jnp.concatenate([q[k], hot], axis=1) for k in range(kv_heads)]
        lse = [lse_ref[t, k, 0:1, :] for k in range(kv_heads)]
        fixed = (list_ref, anc_ref, bias_ref, ones, qx, d_outx, lse)
        weights, d_scores = gradient_scores(t, 0, *fixed)
        keep(weights, d_scores)
        for k in range(kv_heads):
            q_scr[k] = q[k]
            do_scr[k] = d_out[k]
        if not first:
            add(t - 1, jnp.maximum(steps_ref[t - 1] - 1, 0), found)

        def advance(c, carry):
            found = products()
            weights, d_scores = gradient_scores(t, c, *fixed)
            keep(weights, d_scores)
            add(t, c - 1, found)
            return carry

        lax.fori_loop(1, steps_ref[t], advance, 0)

    def later(t, carry):
        tile(t, False)
        return carry

    tile(0, True)
    lax.fori_loop(1, tiles, later, 0)
    add(tiles - 1, jnp.maximum(steps_ref[tiles - 1] - 1, 0), products())
    some = owners // PIECES

    def departure(i):
        place = pl.ds(i * some, some)
        return pltpu.make_async_copy(terms_scr.at[place], terms_far.at[place], out_sems.at[i])

    for i in range(PIECES):
        for j in range(i * some, (i + 1) * some):
            terms_scr[j, 0] = (acc_scr[j, 0] * SCALING).astype(jnp.bfloat16)
            terms_scr[j, 1] = acc_scr[j, 1].astype(jnp.bfloat16)
        departure(i).start()
    for i in range(PIECES):
        departure(i).wait()


def own_gradient_kernel(
    steps_ref, list_ref, q_ref, up_ref, anc_ref, bias_ref, att_ref, lse_ref, stat_ref, other_ref, hot_ref,
    bkv_ref, row_ref, norm_ref, dq_ref, dbr_ref, dq_scr, ds_scr,
):
    t = pl.program_id(0)
    owners, _, owned, _ = anc_ref.shape
    kv_heads = lse_ref.shape[1]
    groups = q_ref.shape[1] // HEAD_SIZE // kv_heads
    rows, near = groups * TILE, REACH + TILE
    scaler, pull = norm_terms(stat_ref, other_ref)
    norm_ref[...] = att_ref[...] * scaler
    d_out, d_outx = output_gradients(att_ref, up_ref, scaler, pull, kv_heads, groups)
    q = [stacked(q_ref, k, groups) for k in range(kv_heads)]
    hot = jnp.concatenate([hot_ref[...]] * groups, axis=0)
    qx = [jnp.concatenate([q[k], hot], axis=1) for k in range(kv_heads)]
    lse = [lse_ref[0, k, 0:1, :] for k in range(kv_heads)]
    ones = ones_columns(CHUNK * owned, 0)
    fixed = (list_ref, anc_ref, bias_ref, ones, qx, d_outx, lse)

    @pl.when(t == 0)
    def _():
        dbr_ref[...] = jnp.zeros_like(dbr_ref)

    window, allowed = allowed_keys(t, row_ref[0], (near, rows), 0)
    for k in range(kv_heads):
        keys = bkv_ref[0, pl.ds(window, near), head_columns(k)]
        values = bkv_ref[1, pl.ds(window, near), head_columns(k)]
        valuesx = jnp.concatenate([values, ones[:near]], axis=1)
        scores = jnp.where(allowed, dot(keys, q[k], ROWS_BY_ROWS), NEGATIVE)
        weights = jnp.exp2(scores * FACTOR - lse[k])
        d_scores = (weights * dot(valuesx, d_outx[k], ROWS_BY_ROWS)).astype(jnp.bfloat16)
        dbr_ref[0, pl.ds(window, near), head_columns(k)] += dot(d_scores, q[k], PLAIN) * SCALING
        dbr_ref[1, pl.ds(window, near), head_columns(k)] += dot(
            weights.astype(jnp.bfloat16), d_out[k], PLAIN
        )
        dq_scr[k] = dot(keys, d_scores, COLS_BY_COLS)

    def keep(d_scores):
        for k in range(kv_heads):
            ds_scr[k] = d_scores[k].astype(jnp.bfloat16)

    def pulled(c):
        _, clipped = chunk_ids(list_ref, t, c, owners)
        return [dot(chunk_rows(anc_ref, clipped, 0, k), ds_scr[k], COLS_BY_COLS) for k in range(kv_heads)]

    keep(gradient_scores(t, 0, *fixed)[1])

    def advance(c, carry):
        more = pulled(c - 1)
        keep(gradient_scores(t, c, *fixed)[1])
        for k in range(kv_heads):
            dq_scr[k] += more[k]
        return carry

    lax.fori_loop(1, steps_ref[t], advance, 0)
    more = pulled(jnp.maximum(steps_ref[t] - 1, 0))
    for k in range(kv_heads):
        d_query = ((dq_scr[k] + more[k]) * SCALING).T
        for g in range(groups):
            dq_ref[:, head_columns(k * groups + g)] = d_query[g * TILE : (g + 1) * TILE, :]


def copies_kernel(one_ref, many_ref, some_scr, sems):
    each = some_scr.shape[0]
    for i in range(each):
        some_scr[i] = one_ref[...]
    moves = [
        pltpu.make_async_copy(some_scr, many_ref.at[pl.ds(i * each, each)], sems.at[i]) for i in range(PIECES)
    ]
    for move in moves:
        move.start()
    for move in moves:
        move.wait()


def total_kernel(terms_ref, sum_ref):
    sum_ref[...] = jnp.sum(terms_ref[...].astype(jnp.float32), axis=0)


FAR, WHOLE, SLICED, SCALARS = "far", "whole", "sliced", "scalars"


def call(kernel, tiles, ins, outs, scratch=(), limit=60):
    def spec(array, way):
        if way == SCALARS:
            return pl.BlockSpec(memory_space=pltpu.SMEM)
        if way == FAR:
            return pl.BlockSpec(memory_space=pl.ANY)
        if way == WHOLE:
            return pl.BlockSpec(memory_space=pltpu.VMEM)
        rest = (0,) * (len(array.shape) - 1)
        return pl.BlockSpec((array.shape[0] // tiles,) + array.shape[1:], lambda t: (t,) + rest)

    def placed(array, way):
        return pltpu.with_memory_space_constraint(array, pltpu.MemorySpace.HBM) if way == FAR else array

    def shaped(array, way):
        return pltpu.MemorySpace.HBM(array.shape, array.dtype) if way == FAR else array

    return pl.pallas_call(
        kernel,
        **({"grid": (tiles,)} if tiles else {}),
        in_specs=[spec(*one) for one in ins],
        out_shape=[shaped(*one) for one in outs],
        out_specs=[spec(*one) for one in outs],
        scratch_shapes=list(scratch),
        compiler_params=pltpu.CompilerParams(vmem_limit_bytes=limit * 1024 * 1024),
    )(*[placed(*one) for one in ins])


def prepare(seg_lengths, anc_rows, token_count, groups):
    segments, owners = anc_rows.shape
    order = jnp.arange(segments, dtype=jnp.int32)
    finish = jnp.sum(jnp.where(order[:, None] <= order[None, :], seg_lengths[:, None], 0), axis=0)
    begin = finish - seg_lengths
    positions = jnp.arange(token_count, dtype=jnp.int32)
    member = (positions[:, None] >= begin) & (positions[:, None] < finish)
    starts = jnp.sum(jnp.where(member, begin, 0), axis=1)
    row = jnp.tile(starts.reshape(token_count // TILE, 1, TILE), (1, 1, groups))
    column = jnp.arange(HEAD_SIZE, dtype=jnp.int32)
    hot = jnp.sum(
        jnp.where(member[:, :, None] & (column == order[:, None]), 1.0, 0.0), axis=1
    ).astype(jnp.bfloat16)
    banned = jnp.concatenate([anc_rows == 0, jnp.ones((segments, 1), bool)], axis=1)
    bias = jnp.sum(
        jnp.where(banned[:, :, None] & (column == order[:, None, None]), NEGATIVE, 0.0), axis=0
    ).astype(jnp.bfloat16)
    bias = jnp.broadcast_to(bias[:, None, :], (owners + 1, 16, HEAD_SIZE))
    tiles = jnp.arange(token_count // TILE, dtype=jnp.int32)[:, None] * TILE
    active = (begin < tiles + TILE) & (finish > tiles)
    union = jnp.any(active[:, :, None] & (anc_rows != 0), axis=1)
    each = jnp.arange(owners, dtype=jnp.int32)
    place = jnp.sum((union[:, None, :] & (each[None, :] < each[:, None])).astype(jnp.int32), axis=2)
    counts = jnp.sum(union.astype(jnp.int32), axis=1)
    hit = union[:, None, :] & (place[:, None, :] == each[:, None])
    listed = jnp.sum(jnp.where(hit, each, 0), axis=2)
    listed = jnp.where(each < counts[:, None], listed, owners)
    return (counts + CHUNK - 1) // CHUNK, listed, bias, hot, row


def local(queries, branch_kv, ancestor_key_value, upstream, lengths, ancestors):
    token_count, width = queries.shape
    kv_heads = branch_kv.shape[2] // HEAD_SIZE
    groups = width // HEAD_SIZE // kv_heads
    owners = ancestors.shape[1]
    owned = ancestor_key_value.shape[1]
    tiles = token_count // TILE
    rows = groups * TILE
    each = (owners,) + ancestor_key_value.shape
    some = (owners // PIECES,) + ancestor_key_value.shape
    f32, bf16 = jnp.float32, jnp.bfloat16

    def new(shape, dtype=f32):
        return jax.ShapeDtypeStruct(shape, dtype)

    (copies,) = call(
        copies_kernel, 0, [(ancestor_key_value, WHOLE)], [(new(each, bf16), FAR)],
        [pltpu.VMEM(some, bf16), pltpu.SemaphoreType.DMA((PIECES,))],
    )
    gathered = lax.all_to_all(copies, ("dp", "leaf"), 0, 0, tiled=True)
    steps, listed, bias, hot, row = prepare(lengths[0], ancestors, token_count, groups)
    scalars = [(steps, SCALARS), (listed, SCALARS)]
    near, both = call(
        near_kernel, tiles,
        [(queries, SLICED), (branch_kv, WHOLE), (row, SLICED)],
        [(new((tiles, kv_heads, HEAD_SIZE, rows)), SLICED), (new((tiles, kv_heads, 8, rows)), SLICED)],
    )
    whole = (token_count, width)
    attended, lse, stats = call(
        forward_kernel, 0,
        scalars + [
            (queries, FAR), (upstream, FAR), (near, FAR), (both, FAR), (hot, WHOLE), (gathered, WHOLE),
            (bias, WHOLE),
        ],
        [
            (new(whole), FAR), (new((tiles, kv_heads, 8, rows)), WHOLE),
            (new((token_count, 2 * HEAD_SIZE)), WHOLE),
        ],
        [
            pltpu.VMEM(whole, bf16),
            pltpu.VMEM(whole, bf16),
            pltpu.VMEM((tiles, kv_heads, HEAD_SIZE, rows), f32),
            pltpu.VMEM((tiles, kv_heads, 8, rows), f32),
            pltpu.VMEM(whole, f32),
            pltpu.SemaphoreType.DMA((4, tiles)),
            pltpu.SemaphoreType.DMA((tiles,)),
            pltpu.VMEM((kv_heads, CHUNK * owned, rows), bf16),
            pltpu.VMEM((kv_heads, 8, rows), f32),
            pltpu.VMEM((kv_heads, HEAD_SIZE, rows), f32),
            pltpu.VMEM((kv_heads, 1, rows), f32),
        ],
        limit=28,
    )
    other = lax.ppermute(stats, "head", [(0, 1), (1, 0)])
    (terms,) = call(
        shared_gradient_kernel, 0,
        scalars + [
            (queries, FAR), (upstream, FAR), (attended, FAR), (stats, WHOLE), (other, WHOLE), (lse, WHOLE),
            (hot, WHOLE), (gathered, WHOLE), (bias, WHOLE),
        ],
        [(new(each, bf16), FAR)],
        [
            pltpu.VMEM(whole, bf16),
            pltpu.VMEM(whole, bf16),
            pltpu.VMEM(whole, f32),
            pltpu.SemaphoreType.DMA((3, tiles)),
            pltpu.VMEM(each, bf16),
            pltpu.SemaphoreType.DMA((PIECES,)),
            pltpu.VMEM(each, f32),
            pltpu.VMEM((kv_heads, CHUNK * owned, rows), bf16),
            pltpu.VMEM((kv_heads, CHUNK * owned, rows), bf16),
            pltpu.VMEM((kv_heads, rows, HEAD_SIZE), bf16),
            pltpu.VMEM((kv_heads, rows, HEAD_SIZE), bf16),
        ],
        limit=28,
    )
    received = lax.all_to_all(terms, ("dp", "leaf"), 0, 0, tiled=True)
    normed, d_queries, d_branch = call(
        own_gradient_kernel, tiles,
        scalars + [
            (queries, SLICED), (upstream, SLICED), (gathered, WHOLE), (bias, WHOLE), (attended, SLICED),
            (lse, SLICED), (stats, SLICED), (other, SLICED), (hot, SLICED), (branch_kv, WHOLE), (row, SLICED),
        ],
        [(new(whole), SLICED), (new(whole), SLICED), (new(branch_kv.shape), WHOLE)],
        [
            pltpu.VMEM((kv_heads, HEAD_SIZE, rows), f32),
            pltpu.VMEM((kv_heads, CHUNK * owned, rows), bf16),
        ],
    )
    (summed,) = call(
        total_kernel, 0, [(received, WHOLE)], [(new(ancestor_key_value.shape), WHOLE)], limit=8
    )
    return (normed, d_queries, d_branch, summed)


def solution(mesh):
    placed = (
        P(("dp", "leaf"), "head"),
        P(None, ("dp", "leaf"), "head"),
        P(None, ("dp", "leaf"), "head"),
        P(("dp", "leaf"), "head"),
        P(("dp", "leaf"), None),
        P(("dp", "leaf"), None),
    )
    return jax.shard_map(
        local,
        mesh=mesh,
        in_specs=placed,
        out_specs=(
            P(("dp", "leaf"), "head"),
            P(("dp", "leaf"), "head"),
            P(None, ("dp", "leaf"), "head"),
            P(None, ("dp", "leaf"), "head"),
        ),
        check_vma=False,
    )
```

```python
import jax
import jax.numpy as jnp
from jax import lax
from jax.experimental import pallas as pl
from jax.experimental.pallas import tpu as pltpu
from jax.sharding import PartitionSpec as P

QUERY_HEADS = 32
HEAD_SIZE = 128
NEGATIVE = -1e30
EPSILON = 1e-05
RANGE = 1e25
PIECES = 8
LOG2E = 1.4426950408889634

TILE = 64
CHUNK = 8
REACH = 128
SEGMENTS = 4
SCALING = HEAD_SIZE ** (-0.5)
FACTOR = SCALING * LOG2E

ROWS_BY_ROWS = (((1,), (1,)), ((), ()))
COLS_BY_COLS = (((0,), (0,)), ((), ()))
PLAIN = (((1,), (0,)), ((), ()))


def dot(a, b, dims):
    return lax.dot_general(a, b, dims, preferred_element_type=jnp.float32)


def head_columns(index):
    return pl.ds(index * HEAD_SIZE, HEAD_SIZE)


def stacked(ref, kv_head, groups):
    return jnp.concatenate(
        [ref[:, head_columns(kv_head * groups + g)] for g in range(groups)], axis=0
    )


def halves(values, op):
    return op(values[:, :HEAD_SIZE], values[:, HEAD_SIZE:])


def column(values):
    lane = lax.broadcasted_iota(jnp.int32, values.shape[:1] + (HEAD_SIZE,), 1)
    first = values.astype(jnp.bfloat16).astype(jnp.float32)
    second = (values - first).astype(jnp.bfloat16).astype(jnp.float32)
    return lane, first, second, values - first - second


def pieces(values, place):
    lane, first, second, third = column(values)
    parts = jnp.where(lane == place, first, jnp.where(lane == place + 1, second, third))
    wanted = (lane >= place) & (lane < place + 3)
    return jnp.where(wanted, parts, 0.0).astype(jnp.bfloat16)


def allowed_keys(t, starts, shape, key_axis):
    window = pl.multiple_of(jnp.maximum(t * TILE - REACH, 0), TILE)
    keys = window + lax.broadcasted_iota(jnp.int32, shape, key_axis)
    tokens = t * TILE + (lax.broadcasted_iota(jnp.int32, shape, 1 - key_axis) & (TILE - 1))
    return window, (keys <= tokens) & (keys >= starts)


def chunk_ids(list_ref, t, c, owners):
    ids = [list_ref[t, c * CHUNK + i] for i in range(CHUNK)]
    return ids, [jnp.minimum(j, owners - 1) for j in ids]


def chunk_rows(anc_ref, clipped, part, kv_head):
    return jnp.concatenate([anc_ref[j, part, :, head_columns(kv_head)] for j in clipped], axis=0)


def chunk_bias(bias_ref, ids):
    return jnp.concatenate([bias_ref[j] for j in ids for _ in range(2)], axis=0)


def near_kernel(q_ref, bkv_ref, row_ref, out_ref, both_ref):
    t = pl.program_id(0)
    kv_heads = bkv_ref.shape[2] // HEAD_SIZE
    groups = q_ref.shape[1] // HEAD_SIZE // kv_heads
    rows, near = groups * TILE, REACH + TILE
    window, allowed = allowed_keys(t, row_ref[0], (near, rows), 0)
    for k in range(kv_heads):
        keys = bkv_ref[0, pl.ds(window, near), head_columns(k)]
        values = bkv_ref[1, pl.ds(window, near), head_columns(k)]
        scores = jnp.where(allowed, dot(keys, stacked(q_ref, k, groups), ROWS_BY_ROWS), NEGATIVE)
        top = jnp.max(scores, axis=0, keepdims=True)
        weights = jnp.exp2((scores - top) * FACTOR)
        out_ref[0, k] = dot(values, weights.astype(jnp.bfloat16), COLS_BY_COLS)
        both_ref[0, k, 0:1, :] = top
        both_ref[0, k, 1:2, :] = jnp.sum(weights, axis=0, keepdims=True)


def fold(values, op):
    rows, width = values.shape
    return op(values.reshape(rows // 8, 8, width), axis=0)


def tile_rows(ref, t):
    return ref.at[pl.ds(pl.multiple_of(t * TILE, TILE), TILE)]


def arrival(t, sems, pairs, first=0):
    moves = []
    for i, (far, near, stacked_tiles) in enumerate(pairs, first):
        if stacked_tiles:
            moves.append(pltpu.make_async_copy(far.at[t], near.at[t], sems.at[i, t]))
        else:
            moves.append(pltpu.make_async_copy(tile_rows(far, t), tile_rows(near, t), sems.at[i, t]))
    return moves


def forward_kernel(
    steps_ref, list_ref, q_far, up_far, near_far, both_far, hot_ref, anc_ref, bias_ref,
    att_all, lse_ref, stat_ref, q_all, up_all,
    near_all, both_ref, in_sems, w_scr, sum_scr, o_scr, shift_scr,
):
    tiles, kv_heads, _, rows = both_ref.shape
    owners = anc_ref.shape[0]
    groups = rows // TILE
    early = [(q_far, q_all, False), (both_far, both_ref, True)]
    late = [(up_far, up_all, False), (near_far, near_all, True)]
    for t in range(tiles):
        for move in arrival(t, in_sems, early + late):
            move.start()

    def hot_of(t):
        return jnp.concatenate([tile_rows(hot_ref, t)[...]] * groups, axis=0)

    def queries_of(t):
        hot = hot_of(t)
        return [
            jnp.concatenate([stacked(tile_rows(q_all, t), k, groups), hot], axis=1) for k in range(kv_heads)
        ]

    def scored(t, c, qx):
        ids, clipped = chunk_ids(list_ref, t, c, owners)
        bias = chunk_bias(bias_ref, ids)
        keys = [jnp.concatenate([chunk_rows(anc_ref, clipped, 0, k), bias], axis=1) for k in range(kv_heads)]
        return [dot(keys[k], qx[k], ROWS_BY_ROWS) for k in range(kv_heads)]

    def weigh(t, c, qx, shifts):
        scores = scored(t, c, qx)
        return [jnp.exp2(scores[k] * FACTOR - shifts[k]) for k in range(kv_heads)]

    def valued(t, c):
        _, clipped = chunk_ids(list_ref, t, c, owners)
        return [dot(chunk_rows(anc_ref, clipped, 1, k), w_scr[k], COLS_BY_COLS) for k in range(kv_heads)]

    def keep(weights):
        for k in range(kv_heads):
            w_scr[k] = weights[k].astype(jnp.bfloat16)

    def near_shifts(t):
        return [both_ref[t, k, 0:1, :] * FACTOR for k in range(kv_heads)]

    def finish(old, last):
        near_tops = near_shifts(old)
        for k in range(kv_heads):
            o_scr[k] += last[k]
            sum_scr[k, 0:1, :] = jnp.sum(sum_scr[k], axis=0, keepdims=True)
            shift_scr[k] = near_tops[k]

        largest = jnp.max(jnp.maximum(sum_scr[0, 0:1, :], sum_scr[1, 0:1, :]))

        @pl.when(jnp.logical_not(largest < RANGE))
        def _():
            steps = steps_ref[old]
            qx = queries_of(old)

            def score(c, tops):
                scores = scored(old, c, qx)
                return tuple(jnp.maximum(tops[k], fold(scores[k], jnp.max)) for k in range(kv_heads))

            start = jnp.full((8, rows), NEGATIVE, jnp.float32)
            tops = lax.fori_loop(0, steps, score, (start,) * kv_heads)
            shifts = []
            for k in range(kv_heads):
                top = jnp.max(tops[k], axis=0, keepdims=True) * FACTOR
                shifts.append(jnp.maximum(top, near_tops[k]))
                shift_scr[k] = shifts[k]
            o_scr[...] = jnp.zeros_like(o_scr)

            def gather(c, sums):
                weights = weigh(old, c, qx, shifts)
                keep(weights)
                more = valued(old, c)
                for k in range(kv_heads):
                    o_scr[k] += more[k]
                return tuple(sums[k] + fold(weights[k], jnp.sum) for k in range(kv_heads))

            sums = lax.fori_loop(0, steps, gather, (jnp.zeros((8, rows), jnp.float32),) * kv_heads)
            for k in range(kv_heads):
                sum_scr[k, 0:1, :] = jnp.sum(sums[k], axis=0, keepdims=True)

        for move in arrival(old, in_sems, late, len(early)):
            move.wait()
        upper_ref, att_ref, stats_ref = tile_rows(up_all, old), tile_rows(att_all, old), tile_rows(stat_ref, old)
        squares = jnp.zeros((TILE, HEAD_SIZE), jnp.float32)
        inner = jnp.zeros((TILE, HEAD_SIZE), jnp.float32)
        for k in range(kv_heads):
            shift = shift_scr[k]
            fade = jnp.exp2(near_tops[k] - shift)
            total = sum_scr[k, 0:1, :] + fade * both_ref[old, k, 1:2, :]
            attended = ((o_scr[k] + fade * near_all[old, k]) * (1.0 / total)).T
            lse_ref[old, k, 0:1, :] = shift + jnp.log2(total)
            for g in range(groups):
                slab = attended[g * TILE : (g + 1) * TILE, :]
                upper = upper_ref[:, head_columns(k * groups + g)].astype(jnp.float32)
                att_ref[:, head_columns(k * groups + g)] = slab
                squares += slab * slab
                inner += slab * upper
        stats_ref[:, 0:HEAD_SIZE] = squares
        stats_ref[:, HEAD_SIZE : 2 * HEAD_SIZE] = inner

    def tile(now, first):
        for move in arrival(now, in_sems, early):
            move.wait()
        old = now - 1
        qx, shifts = queries_of(now), near_shifts(now)
        if not first:
            last = valued(old, jnp.maximum(steps_ref[old] - 1, 0))
        fresh = weigh(now, 0, qx, shifts)
        if not first:
            finish(old, last)
        keep(fresh)
        for k in range(kv_heads):
            sum_scr[k] = fold(fresh[k], jnp.sum)
            o_scr[k] = jnp.zeros_like(o_scr[k])

        def advance(c, carry):
            more = valued(now, c - 1)
            weights = weigh(now, c, qx, shifts)
            keep(weights)
            for k in range(kv_heads):
                o_scr[k] += more[k]
                sum_scr[k] += fold(weights[k], jnp.sum)
            return carry

        lax.fori_loop(1, steps_ref[now], advance, 0)

    def later(now, carry):
        tile(now, False)
        return carry

    tile(0, True)
    lax.fori_loop(1, tiles, later, 0)
    finish(tiles - 1, valued(tiles - 1, jnp.maximum(steps_ref[tiles - 1] - 1, 0)))


def norm_terms(stat_ref, other_ref):
    columns = QUERY_HEADS * HEAD_SIZE
    stats = stat_ref[...] + other_ref[...]
    squares = jnp.sum(stats[:, :HEAD_SIZE], axis=1, keepdims=True)
    inner = jnp.sum(stats[:, HEAD_SIZE:], axis=1, keepdims=True)
    scaler = lax.rsqrt(squares / columns + EPSILON)
    return scaler, scaler * scaler * scaler * inner / columns


def output_gradients(att_ref, up_ref, scaler, pull, kv_heads, groups):
    found, extended = [], []
    for k in range(kv_heads):
        slabs, extra = [], []
        for g in range(groups):
            slab = att_ref[:, head_columns(k * groups + g)]
            upper = up_ref[:, head_columns(k * groups + g)].astype(jnp.float32)
            rounded = (scaler * upper - slab * pull).astype(jnp.bfloat16)
            delta = jnp.sum(rounded.astype(jnp.float32) * slab, axis=1, keepdims=True)
            extra.append(pieces(-delta, 0))
            slabs.append(rounded)
        found.append(jnp.concatenate(slabs, axis=0))
        extended.append(jnp.concatenate([found[k], jnp.concatenate(extra, axis=0)], axis=1))
    return found, extended


def ones_columns(rows, place):
    lane = lax.broadcasted_iota(jnp.int32, (rows, HEAD_SIZE), 1)
    return ((lane >= place) & (lane < place + 3)).astype(jnp.bfloat16)


def gradient_scores(t, c, list_ref, anc_ref, bias_ref, ones, qx, d_outx, lse):
    ids, clipped = chunk_ids(list_ref, t, c, anc_ref.shape[0])
    bias = chunk_bias(bias_ref, ids)
    weights, d_scores = [], []
    for k in range(len(qx)):
        keys = jnp.concatenate([chunk_rows(anc_ref, clipped, 0, k), bias], axis=1)
        values = jnp.concatenate([chunk_rows(anc_ref, clipped, 1, k), ones], axis=1)
        weights.append(jnp.exp2(dot(keys, qx[k], ROWS_BY_ROWS) * FACTOR - lse[k]))
        d_scores.append(weights[k] * dot(values, d_outx[k], ROWS_BY_ROWS))
    return weights, d_scores


def shared_gradient_kernel(
    steps_ref, list_ref, q_all, up_all, att_all, stat_ref, other_ref, lse_ref, hot_ref, anc_ref, bias_ref,
    terms_far, att_far,
    terms_scr, out_sems, acc_scr, w_scr, ds_scr, q_scr, do_scr,
):
    tiles, kv_heads, _, rows = lse_ref.shape
    groups = rows // TILE
    owners, _, owned, _ = anc_ref.shape
    ones = ones_columns(CHUNK * owned, 0)
    spill = pltpu.make_async_copy(att_all, att_far, out_sems.at[PIECES])
    spill.start()
    acc_scr[...] = jnp.zeros_like(acc_scr)

    def products():
        return [(dot(ds_scr[k], q_scr[k], PLAIN), dot(w_scr[k], do_scr[k], PLAIN)) for k in range(kv_heads)]

    def add(t, c, found):
        _, clipped = chunk_ids(list_ref, t, c, owners)
        for k in range(kv_heads):
            for i, j in enumerate(clipped):
                place = slice(i * owned, (i + 1) * owned)
                for part in range(2):
                    acc_scr[j, part, :, head_columns(k)] += found[k][part][place]

    def keep(weights, d_scores):
        for k in range(kv_heads):
            w_scr[k] = weights[k].astype(jnp.bfloat16)
            ds_scr[k] = d_scores[k].astype(jnp.bfloat16)

    def tile(t, first):
        if not first:
            found = products()
        scaler, pull = norm_terms(tile_rows(stat_ref, t), tile_rows(other_ref, t))
        d_out, d_outx = output_gradients(
            tile_rows(att_all, t), tile_rows(up_all, t), scaler, pull, kv_heads, groups
        )
        q = [stacked(tile_rows(q_all, t), k, groups) for k in range(kv_heads)]
        hot = jnp.concatenate([tile_rows(hot_ref, t)[...]] * groups, axis=0)
        qx = [jnp.concatenate([q[k], hot], axis=1) for k in range(kv_heads)]
        lse = [lse_ref[t, k, 0:1, :] for k in range(kv_heads)]
        fixed = (list_ref, anc_ref, bias_ref, ones, qx, d_outx, lse)
        weights, d_scores = gradient_scores(t, 0, *fixed)
        keep(weights, d_scores)
        for k in range(kv_heads):
            q_scr[k] = q[k]
            do_scr[k] = d_out[k]
        if not first:
            add(t - 1, jnp.maximum(steps_ref[t - 1] - 1, 0), found)

        def advance(c, carry):
            found = products()
            weights, d_scores = gradient_scores(t, c, *fixed)
            keep(weights, d_scores)
            add(t, c - 1, found)
            return carry

        lax.fori_loop(1, steps_ref[t], advance, 0)

    def later(t, carry):
        tile(t, False)
        return carry

    tile(0, True)
    lax.fori_loop(1, tiles, later, 0)
    add(tiles - 1, jnp.maximum(steps_ref[tiles - 1] - 1, 0), products())
    some = owners // PIECES

    def departure(i):
        place = pl.ds(i * some, some)
        return pltpu.make_async_copy(terms_scr.at[place], terms_far.at[place], out_sems.at[i])

    for i in range(PIECES):
        for j in range(i * some, (i + 1) * some):
            terms_scr[j, 0] = (acc_scr[j, 0] * SCALING).astype(jnp.bfloat16)
            terms_scr[j, 1] = acc_scr[j, 1].astype(jnp.bfloat16)
        departure(i).start()
    for i in range(PIECES):
        departure(i).wait()
    spill.wait()


def own_gradient_kernel(
    steps_ref, list_ref, q_ref, up_ref, anc_ref, bias_ref, att_ref, lse_ref, stat_ref, other_ref, hot_ref,
    bkv_ref, row_ref, norm_ref, dq_ref, dbr_ref, dq_scr, ds_scr,
):
    t = pl.program_id(0)
    owners, _, owned, _ = anc_ref.shape
    kv_heads = lse_ref.shape[1]
    groups = q_ref.shape[1] // HEAD_SIZE // kv_heads
    rows, near = groups * TILE, REACH + TILE
    scaler, pull = norm_terms(stat_ref, other_ref)
    norm_ref[...] = att_ref[...] * scaler
    d_out, d_outx = output_gradients(att_ref, up_ref, scaler, pull, kv_heads, groups)
    q = [stacked(q_ref, k, groups) for k in range(kv_heads)]
    hot = jnp.concatenate([hot_ref[...]] * groups, axis=0)
    qx = [jnp.concatenate([q[k], hot], axis=1) for k in range(kv_heads)]
    lse = [lse_ref[0, k, 0:1, :] for k in range(kv_heads)]
    ones = ones_columns(CHUNK * owned, 0)
    fixed = (list_ref, anc_ref, bias_ref, ones, qx, d_outx, lse)

    @pl.when(t == 0)
    def _():
        dbr_ref[...] = jnp.zeros_like(dbr_ref)

    window, allowed = allowed_keys(t, row_ref[0], (near, rows), 0)
    for k in range(kv_heads):
        keys = bkv_ref[0, pl.ds(window, near), head_columns(k)]
        values = bkv_ref[1, pl.ds(window, near), head_columns(k)]
        valuesx = jnp.concatenate([values, ones[:near]], axis=1)
        scores = jnp.where(allowed, dot(keys, q[k], ROWS_BY_ROWS), NEGATIVE)
        weights = jnp.exp2(scores * FACTOR - lse[k])
        d_scores = (weights * dot(valuesx, d_outx[k], ROWS_BY_ROWS)).astype(jnp.bfloat16)
        dbr_ref[0, pl.ds(window, near), head_columns(k)] += dot(d_scores, q[k], PLAIN) * SCALING
        dbr_ref[1, pl.ds(window, near), head_columns(k)] += dot(
            weights.astype(jnp.bfloat16), d_out[k], PLAIN
        )
        dq_scr[k] = dot(keys, d_scores, COLS_BY_COLS)

    def keep(d_scores):
        for k in range(kv_heads):
            ds_scr[k] = d_scores[k].astype(jnp.bfloat16)

    def pulled(c):
        _, clipped = chunk_ids(list_ref, t, c, owners)
        return [dot(chunk_rows(anc_ref, clipped, 0, k), ds_scr[k], COLS_BY_COLS) for k in range(kv_heads)]

    keep(gradient_scores(t, 0, *fixed)[1])

    def advance(c, carry):
        more = pulled(c - 1)
        keep(gradient_scores(t, c, *fixed)[1])
        for k in range(kv_heads):
            dq_scr[k] += more[k]
        return carry

    lax.fori_loop(1, steps_ref[t], advance, 0)
    more = pulled(jnp.maximum(steps_ref[t] - 1, 0))
    for k in range(kv_heads):
        d_query = ((dq_scr[k] + more[k]) * SCALING).T
        for g in range(groups):
            dq_ref[:, head_columns(k * groups + g)] = d_query[g * TILE : (g + 1) * TILE, :]


def copies_kernel(one_ref, many_ref, some_scr, sems):
    each = some_scr.shape[0]
    for i in range(each):
        some_scr[i] = one_ref[...]
    moves = [
        pltpu.make_async_copy(some_scr, many_ref.at[pl.ds(i * each, each)], sems.at[i]) for i in range(PIECES)
    ]
    for move in moves:
        move.start()
    for move in moves:
        move.wait()


def total_kernel(terms_ref, sum_ref):
    sum_ref[...] = jnp.sum(terms_ref[...].astype(jnp.float32), axis=0)


FAR, WHOLE, SLICED, SCALARS = "far", "whole", "sliced", "scalars"


def call(kernel, tiles, ins, outs, scratch=(), limit=60):
    def spec(array, way):
        if way == SCALARS:
            return pl.BlockSpec(memory_space=pltpu.SMEM)
        if way == FAR:
            return pl.BlockSpec(memory_space=pl.ANY)
        if way == WHOLE:
            return pl.BlockSpec(memory_space=pltpu.VMEM)
        rest = (0,) * (len(array.shape) - 1)
        return pl.BlockSpec((array.shape[0] // tiles,) + array.shape[1:], lambda t: (t,) + rest)

    def placed(array, way):
        return pltpu.with_memory_space_constraint(array, pltpu.MemorySpace.HBM) if way == FAR else array

    def shaped(array, way):
        return pltpu.MemorySpace.HBM(array.shape, array.dtype) if way == FAR else array

    return pl.pallas_call(
        kernel,
        **({"grid": (tiles,)} if tiles else {}),
        in_specs=[spec(*one) for one in ins],
        out_shape=[shaped(*one) for one in outs],
        out_specs=[spec(*one) for one in outs],
        scratch_shapes=list(scratch),
        compiler_params=pltpu.CompilerParams(vmem_limit_bytes=limit * 1024 * 1024),
    )(*[placed(*one) for one in ins])


def prepare(seg_lengths, anc_rows, token_count, groups):
    segments, owners = anc_rows.shape
    order = jnp.arange(segments, dtype=jnp.int32)
    finish = jnp.sum(jnp.where(order[:, None] <= order[None, :], seg_lengths[:, None], 0), axis=0)
    begin = finish - seg_lengths
    positions = jnp.arange(token_count, dtype=jnp.int32)
    member = (positions[:, None] >= begin) & (positions[:, None] < finish)
    starts = jnp.sum(jnp.where(member, begin, 0), axis=1)
    row = jnp.tile(starts.reshape(token_count // TILE, 1, TILE), (1, 1, groups))
    column = jnp.arange(HEAD_SIZE, dtype=jnp.int32)
    hot = jnp.sum(
        jnp.where(member[:, :, None] & (column == order[:, None]), 1.0, 0.0), axis=1
    ).astype(jnp.bfloat16)
    banned = jnp.concatenate([anc_rows == 0, jnp.ones((segments, 1), bool)], axis=1)
    bias = jnp.sum(
        jnp.where(banned[:, :, None] & (column == order[:, None, None]), NEGATIVE, 0.0), axis=0
    ).astype(jnp.bfloat16)
    bias = jnp.broadcast_to(bias[:, None, :], (owners + 1, 16, HEAD_SIZE))
    tiles = jnp.arange(token_count // TILE, dtype=jnp.int32)[:, None] * TILE
    active = (begin < tiles + TILE) & (finish > tiles)
    union = jnp.any(active[:, :, None] & (anc_rows != 0), axis=1)
    each = jnp.arange(owners, dtype=jnp.int32)
    place = jnp.sum((union[:, None, :] & (each[None, :] < each[:, None])).astype(jnp.int32), axis=2)
    counts = jnp.sum(union.astype(jnp.int32), axis=1)
    hit = union[:, None, :] & (place[:, None, :] == each[:, None])
    listed = jnp.sum(jnp.where(hit, each, 0), axis=2)
    listed = jnp.where(each < counts[:, None], listed, owners)
    return (counts + CHUNK - 1) // CHUNK, listed, bias, hot, row


def local(queries, branch_kv, ancestor_key_value, upstream, lengths, ancestors):
    token_count, width = queries.shape
    kv_heads = branch_kv.shape[2] // HEAD_SIZE
    groups = width // HEAD_SIZE // kv_heads
    owners = ancestors.shape[1]
    owned = ancestor_key_value.shape[1]
    tiles = token_count // TILE
    rows = groups * TILE
    each = (owners,) + ancestor_key_value.shape
    some = (owners // PIECES,) + ancestor_key_value.shape
    f32, bf16 = jnp.float32, jnp.bfloat16

    def new(shape, dtype=f32):
        return jax.ShapeDtypeStruct(shape, dtype)

    (copies,) = call(
        copies_kernel, 0, [(ancestor_key_value, WHOLE)], [(new(each, bf16), FAR)],
        [pltpu.VMEM(some, bf16), pltpu.SemaphoreType.DMA((PIECES,))],
    )
    gathered = lax.all_to_all(copies, ("dp", "leaf"), 0, 0, tiled=True)
    steps, listed, bias, hot, row = prepare(lengths[0], ancestors, token_count, groups)
    scalars = [(steps, SCALARS), (listed, SCALARS)]
    near, both = call(
        near_kernel, tiles,
        [(queries, SLICED), (branch_kv, WHOLE), (row, SLICED)],
        [(new((tiles, kv_heads, HEAD_SIZE, rows)), SLICED), (new((tiles, kv_heads, 8, rows)), SLICED)],
    )
    whole = (token_count, width)
    attended, lse, stats, near_queries, near_upstream = call(
        forward_kernel, 0,
        scalars + [
            (queries, FAR), (upstream, FAR), (near, FAR), (both, FAR), (hot, WHOLE), (gathered, WHOLE),
            (bias, WHOLE),
        ],
        [
            (new(whole), WHOLE), (new((tiles, kv_heads, 8, rows)), WHOLE),
            (new((token_count, 2 * HEAD_SIZE)), WHOLE), (new(whole, bf16), WHOLE), (new(whole, bf16), WHOLE),
        ],
        [
            pltpu.VMEM((tiles, kv_heads, HEAD_SIZE, rows), f32),
            pltpu.VMEM((tiles, kv_heads, 8, rows), f32),
            pltpu.SemaphoreType.DMA((4, tiles)),
            pltpu.VMEM((kv_heads, CHUNK * owned, rows), bf16),
            pltpu.VMEM((kv_heads, 8, rows), f32),
            pltpu.VMEM((kv_heads, HEAD_SIZE, rows), f32),
            pltpu.VMEM((kv_heads, 1, rows), f32),
        ],
        limit=28,
    )
    other = lax.ppermute(stats, "head", [(0, 1), (1, 0)])
    terms, attended = call(
        shared_gradient_kernel, 0,
        scalars + [
            (near_queries, WHOLE), (near_upstream, WHOLE), (attended, WHOLE), (stats, WHOLE), (other, WHOLE), (lse, WHOLE),
            (hot, WHOLE), (gathered, WHOLE), (bias, WHOLE),
        ],
        [(new(each, bf16), FAR), (new(whole), FAR)],
        [
            pltpu.VMEM(each, bf16),
            pltpu.SemaphoreType.DMA((PIECES + 1,)),
            pltpu.VMEM(each, f32),
            pltpu.VMEM((kv_heads, CHUNK * owned, rows), bf16),
            pltpu.VMEM((kv_heads, CHUNK * owned, rows), bf16),
            pltpu.VMEM((kv_heads, rows, HEAD_SIZE), bf16),
            pltpu.VMEM((kv_heads, rows, HEAD_SIZE), bf16),
        ],
        limit=28,
    )
    received = lax.all_to_all(terms, ("dp", "leaf"), 0, 0, tiled=True)
    normed, d_queries, d_branch = call(
        own_gradient_kernel, tiles,
        scalars + [
            (queries, SLICED), (upstream, SLICED), (gathered, WHOLE), (bias, WHOLE), (attended, SLICED),
            (lse, SLICED), (stats, SLICED), (other, SLICED), (hot, SLICED), (branch_kv, WHOLE), (row, SLICED),
        ],
        [(new(whole), SLICED), (new(whole), SLICED), (new(branch_kv.shape), WHOLE)],
        [
            pltpu.VMEM((kv_heads, HEAD_SIZE, rows), f32),
            pltpu.VMEM((kv_heads, CHUNK * owned, rows), bf16),
        ],
    )
    (summed,) = call(
        total_kernel, 0, [(received, WHOLE)], [(new(ancestor_key_value.shape), WHOLE)], limit=8
    )
    return (normed, d_queries, d_branch, summed)


def solution(mesh):
    placed = (
        P(("dp", "leaf"), "head"),
        P(None, ("dp", "leaf"), "head"),
        P(None, ("dp", "leaf"), "head"),
        P(("dp", "leaf"), "head"),
        P(("dp", "leaf"), None),
        P(("dp", "leaf"), None),
    )
    return jax.shard_map(
        local,
        mesh=mesh,
        in_specs=placed,
        out_specs=(
            P(("dp", "leaf"), "head"),
            P(("dp", "leaf"), "head"),
            P(None, ("dp", "leaf"), "head"),
            P(None, ("dp", "leaf"), "head"),
        ),
        check_vma=False,
    )
```

```python
import jax
import jax.numpy as jnp
from jax import lax
from jax.experimental import pallas as pl
from jax.experimental.pallas import tpu as pltpu
from jax.sharding import PartitionSpec as P

QUERY_HEADS = 32
HEAD_SIZE = 128
NEGATIVE = -1e30
EPSILON = 1e-05
RANGE = 1e25
PIECES = 8
LOG2E = 1.4426950408889634

TILE = 64
CHUNK = 8
REACH = 128
SEGMENTS = 4
SCALING = HEAD_SIZE ** (-0.5)
FACTOR = SCALING * LOG2E

ROWS_BY_ROWS = (((1,), (1,)), ((), ()))
COLS_BY_COLS = (((0,), (0,)), ((), ()))
PLAIN = (((1,), (0,)), ((), ()))


def dot(a, b, dims):
    return lax.dot_general(a, b, dims, preferred_element_type=jnp.float32)


def head_columns(index):
    return pl.ds(index * HEAD_SIZE, HEAD_SIZE)


def stacked(ref, kv_head, groups):
    return jnp.concatenate(
        [ref[:, head_columns(kv_head * groups + g)] for g in range(groups)], axis=0
    )


def halves(values, op):
    return op(values[:, :HEAD_SIZE], values[:, HEAD_SIZE:])


def column(values):
    lane = lax.broadcasted_iota(jnp.int32, values.shape[:1] + (HEAD_SIZE,), 1)
    first = values.astype(jnp.bfloat16).astype(jnp.float32)
    second = (values - first).astype(jnp.bfloat16).astype(jnp.float32)
    return lane, first, second, values - first - second


def pieces(values, place):
    lane, first, second, third = column(values)
    parts = jnp.where(lane == place, first, jnp.where(lane == place + 1, second, third))
    wanted = (lane >= place) & (lane < place + 3)
    return jnp.where(wanted, parts, 0.0).astype(jnp.bfloat16)


def allowed_keys(t, starts, shape, key_axis):
    window = pl.multiple_of(jnp.maximum(t * TILE - REACH, 0), TILE)
    keys = window + lax.broadcasted_iota(jnp.int32, shape, key_axis)
    tokens = t * TILE + (lax.broadcasted_iota(jnp.int32, shape, 1 - key_axis) & (TILE - 1))
    return window, (keys <= tokens) & (keys >= starts)


def chunk_ids(list_ref, t, c, owners):
    ids = [list_ref[t, c * CHUNK + i] for i in range(CHUNK)]
    return ids, [jnp.minimum(j, owners - 1) for j in ids]


def chunk_rows(anc_ref, clipped, part, kv_head):
    return jnp.concatenate([anc_ref[j, part, :, head_columns(kv_head)] for j in clipped], axis=0)


def chunk_bias(bias_ref, ids):
    return jnp.concatenate([bias_ref[j] for j in ids for _ in range(2)], axis=0)


def near_kernel(q_ref, bkv_ref, row_ref, out_ref, both_ref):
    t = pl.program_id(0)
    kv_heads = bkv_ref.shape[2] // HEAD_SIZE
    groups = q_ref.shape[1] // HEAD_SIZE // kv_heads
    rows, near = groups * TILE, REACH + TILE
    window, allowed = allowed_keys(t, row_ref[0], (near, rows), 0)
    for k in range(kv_heads):
        keys = bkv_ref[0, pl.ds(window, near), head_columns(k)]
        values = bkv_ref[1, pl.ds(window, near), head_columns(k)]
        scores = jnp.where(allowed, dot(keys, stacked(q_ref, k, groups), ROWS_BY_ROWS), NEGATIVE)
        top = jnp.max(scores, axis=0, keepdims=True)
        weights = jnp.exp2((scores - top) * FACTOR)
        out_ref[0, k] = dot(values, weights.astype(jnp.bfloat16), COLS_BY_COLS)
        both_ref[0, k, 0:1, :] = top
        both_ref[0, k, 1:2, :] = jnp.sum(weights, axis=0, keepdims=True)


def fold(values, op):
    rows, width = values.shape
    return op(values.reshape(rows // 8, 8, width), axis=0)


def tile_rows(ref, t):
    return ref.at[pl.ds(pl.multiple_of(t * TILE, TILE), TILE)]


def arrival(t, sems, pairs, first=0):
    moves = []
    for i, (far, near, stacked_tiles) in enumerate(pairs, first):
        if stacked_tiles:
            moves.append(pltpu.make_async_copy(far.at[t], near.at[t], sems.at[i, t]))
        else:
            moves.append(pltpu.make_async_copy(tile_rows(far, t), tile_rows(near, t), sems.at[i, t]))
    return moves


def forward_kernel(
    steps_ref, list_ref, q_far, up_far, near_far, both_far, hot_ref, anc_ref, bias_ref,
    att_all, lse_ref, stat_ref, q_all, up_all,
    near_all, both_ref, in_sems, w_scr, sum_scr, o_scr, shift_scr,
):
    tiles, kv_heads, _, rows = both_ref.shape
    owners = anc_ref.shape[0]
    groups = rows // TILE
    early = [(q_far, q_all, False), (both_far, both_ref, True)]
    late = [(up_far, up_all, False), (near_far, near_all, True)]
    for t in range(tiles):
        for move in arrival(t, in_sems, early + late):
            move.start()

    def hot_of(t):
        return jnp.concatenate([tile_rows(hot_ref, t)[...]] * groups, axis=0)

    def queries_of(t):
        hot = hot_of(t)
        return [
            jnp.concatenate([stacked(tile_rows(q_all, t), k, groups), hot], axis=1) for k in range(kv_heads)
        ]

    def scored(t, c, qx):
        ids, clipped = chunk_ids(list_ref, t, c, owners)
        bias = chunk_bias(bias_ref, ids)
        keys = [jnp.concatenate([chunk_rows(anc_ref, clipped, 0, k), bias], axis=1) for k in range(kv_heads)]
        return [dot(keys[k], qx[k], ROWS_BY_ROWS) for k in range(kv_heads)]

    def weigh(t, c, qx, shifts):
        scores = scored(t, c, qx)
        return [jnp.exp2(scores[k] * FACTOR - shifts[k]) for k in range(kv_heads)]

    def valued(t, c):
        _, clipped = chunk_ids(list_ref, t, c, owners)
        return [dot(chunk_rows(anc_ref, clipped, 1, k), w_scr[k], COLS_BY_COLS) for k in range(kv_heads)]

    def keep(weights):
        for k in range(kv_heads):
            w_scr[k] = weights[k].astype(jnp.bfloat16)

    def near_shifts(t):
        return [both_ref[t, k, 0:1, :] * FACTOR for k in range(kv_heads)]

    def finish(old, last):
        near_tops = near_shifts(old)
        for k in range(kv_heads):
            o_scr[k] += last[k]
            sum_scr[k, 0:1, :] = jnp.sum(sum_scr[k], axis=0, keepdims=True)
            shift_scr[k] = near_tops[k]

        largest = jnp.max(jnp.maximum(sum_scr[0, 0:1, :], sum_scr[1, 0:1, :]))

        @pl.when(jnp.logical_not(largest < RANGE))
        def _():
            steps = steps_ref[old]
            qx = queries_of(old)

            def score(c, tops):
                scores = scored(old, c, qx)
                return tuple(jnp.maximum(tops[k], fold(scores[k], jnp.max)) for k in range(kv_heads))

            start = jnp.full((8, rows), NEGATIVE, jnp.float32)
            tops = lax.fori_loop(0, steps, score, (start,) * kv_heads)
            shifts = []
            for k in range(kv_heads):
                top = jnp.max(tops[k], axis=0, keepdims=True) * FACTOR
                shifts.append(jnp.maximum(top, near_tops[k]))
                shift_scr[k] = shifts[k]
            o_scr[...] = jnp.zeros_like(o_scr)

            def gather(c, sums):
                weights = weigh(old, c, qx, shifts)
                keep(weights)
                more = valued(old, c)
                for k in range(kv_heads):
                    o_scr[k] += more[k]
                return tuple(sums[k] + fold(weights[k], jnp.sum) for k in range(kv_heads))

            sums = lax.fori_loop(0, steps, gather, (jnp.zeros((8, rows), jnp.float32),) * kv_heads)
            for k in range(kv_heads):
                sum_scr[k, 0:1, :] = jnp.sum(sums[k], axis=0, keepdims=True)

        for move in arrival(old, in_sems, late, len(early)):
            move.wait()
        upper_ref, att_ref, stats_ref = tile_rows(up_all, old), tile_rows(att_all, old), tile_rows(stat_ref, old)
        squares = jnp.zeros((TILE, HEAD_SIZE), jnp.float32)
        inner = jnp.zeros((TILE, HEAD_SIZE), jnp.float32)
        for k in range(kv_heads):
            shift = shift_scr[k]
            fade = jnp.exp2(near_tops[k] - shift)
            total = sum_scr[k, 0:1, :] + fade * both_ref[old, k, 1:2, :]
            attended = ((o_scr[k] + fade * near_all[old, k]) * (1.0 / total)).T
            lse_ref[old, k, 0:1, :] = shift + jnp.log2(total)
            for g in range(groups):
                slab = attended[g * TILE : (g + 1) * TILE, :]
                upper = upper_ref[:, head_columns(k * groups + g)].astype(jnp.float32)
                att_ref[:, head_columns(k * groups + g)] = slab
                squares += slab * slab
                inner += slab * upper
        stats_ref[:, 0:HEAD_SIZE] = squares
        stats_ref[:, HEAD_SIZE : 2 * HEAD_SIZE] = inner

    def tile(now, first):
        for move in arrival(now, in_sems, early):
            move.wait()
        old = now - 1
        qx, shifts = queries_of(now), near_shifts(now)
        if not first:
            last = valued(old, jnp.maximum(steps_ref[old] - 1, 0))
        fresh = weigh(now, 0, qx, shifts)
        if not first:
            finish(old, last)
        keep(fresh)
        for k in range(kv_heads):
            sum_scr[k] = fold(fresh[k], jnp.sum)
            o_scr[k] = jnp.zeros_like(o_scr[k])

        def advance(c, carry):
            more = valued(now, c - 1)
            weights = weigh(now, c, qx, shifts)
            keep(weights)
            for k in range(kv_heads):
                o_scr[k] += more[k]
                sum_scr[k] += fold(weights[k], jnp.sum)
            return carry

        lax.fori_loop(1, steps_ref[now], advance, 0)

    def later(now, carry):
        tile(now, False)
        return carry

    tile(0, True)
    lax.fori_loop(1, tiles, later, 0)
    finish(tiles - 1, valued(tiles - 1, jnp.maximum(steps_ref[tiles - 1] - 1, 0)))


def norm_terms(stat_ref, other_ref):
    columns = QUERY_HEADS * HEAD_SIZE
    stats = stat_ref[...] + other_ref[...]
    squares = jnp.sum(stats[:, :HEAD_SIZE], axis=1, keepdims=True)
    inner = jnp.sum(stats[:, HEAD_SIZE:], axis=1, keepdims=True)
    scaler = lax.rsqrt(squares / columns + EPSILON)
    return scaler, scaler * scaler * scaler * inner / columns


def output_gradients(att_ref, up_ref, scaler, pull, kv_heads, groups):
    found, extended = [], []
    for k in range(kv_heads):
        slabs, extra = [], []
        for g in range(groups):
            slab = att_ref[:, head_columns(k * groups + g)]
            upper = up_ref[:, head_columns(k * groups + g)].astype(jnp.float32)
            rounded = (scaler * upper - slab * pull).astype(jnp.bfloat16)
            delta = jnp.sum(rounded.astype(jnp.float32) * slab, axis=1, keepdims=True)
            extra.append(pieces(-delta, 0))
            slabs.append(rounded)
        found.append(jnp.concatenate(slabs, axis=0))
        extended.append(jnp.concatenate([found[k], jnp.concatenate(extra, axis=0)], axis=1))
    return found, extended


def ones_columns(rows, place):
    lane = lax.broadcasted_iota(jnp.int32, (rows, HEAD_SIZE), 1)
    return ((lane >= place) & (lane < place + 3)).astype(jnp.bfloat16)


def gradient_scores(t, c, list_ref, anc_ref, bias_ref, ones, qx, d_outx, lse):
    ids, clipped = chunk_ids(list_ref, t, c, anc_ref.shape[0])
    bias = chunk_bias(bias_ref, ids)
    weights, d_scores = [], []
    for k in range(len(qx)):
        keys = jnp.concatenate([chunk_rows(anc_ref, clipped, 0, k), bias], axis=1)
        values = jnp.concatenate([chunk_rows(anc_ref, clipped, 1, k), ones], axis=1)
        weights.append(jnp.exp2(dot(keys, qx[k], ROWS_BY_ROWS) * FACTOR - lse[k]))
        d_scores.append(weights[k] * dot(values, d_outx[k], ROWS_BY_ROWS))
    return weights, d_scores


def shared_gradient_kernel(
    steps_ref, list_ref, place_ref, q_all, up_all, att_all, stat_ref, other_ref, lse_ref, hot_ref, anc_ref, bias_ref,
    terms_far, att_far,
    terms_scr, out_sems, acc_scr, w_scr, ds_scr, q_scr, do_scr,
):
    tiles, kv_heads, _, rows = lse_ref.shape
    groups = rows // TILE
    owners, _, owned, _ = anc_ref.shape
    ones = ones_columns(CHUNK * owned, 0)
    spill = pltpu.make_async_copy(att_all, att_far, out_sems.at[PIECES])
    spill.start()
    acc_scr[...] = jnp.zeros_like(acc_scr)

    def products():
        return [(dot(ds_scr[k], q_scr[k], PLAIN), dot(w_scr[k], do_scr[k], PLAIN)) for k in range(kv_heads)]

    def add(t, c, found):
        _, clipped = chunk_ids(list_ref, t, c, owners)
        for k in range(kv_heads):
            for i, j in enumerate(clipped):
                place = slice(i * owned, (i + 1) * owned)
                for part in range(2):
                    acc_scr[j, part, :, head_columns(k)] += found[k][part][place]

    def keep(weights, d_scores):
        for k in range(kv_heads):
            w_scr[k] = weights[k].astype(jnp.bfloat16)
            ds_scr[k] = d_scores[k].astype(jnp.bfloat16)

    def tile(t, first):
        if not first:
            found = products()
        scaler, pull = norm_terms(tile_rows(stat_ref, t), tile_rows(other_ref, t))
        d_out, d_outx = output_gradients(
            tile_rows(att_all, t), tile_rows(up_all, t), scaler, pull, kv_heads, groups
        )
        q = [stacked(tile_rows(q_all, t), k, groups) for k in range(kv_heads)]
        hot = jnp.concatenate([tile_rows(hot_ref, t)[...]] * groups, axis=0)
        qx = [jnp.concatenate([q[k], hot], axis=1) for k in range(kv_heads)]
        lse = [lse_ref[t, k, 0:1, :] for k in range(kv_heads)]
        fixed = (list_ref, anc_ref, bias_ref, ones, qx, d_outx, lse)
        weights, d_scores = gradient_scores(t, 0, *fixed)
        keep(weights, d_scores)
        for k in range(kv_heads):
            q_scr[k] = q[k]
            do_scr[k] = d_out[k]
        if not first:
            add(t - 1, jnp.maximum(steps_ref[t - 1] - 1, 0), found)

        def advance(c, carry):
            found = products()
            weights, d_scores = gradient_scores(t, c, *fixed)
            keep(weights, d_scores)
            add(t, c - 1, found)
            return carry

        lax.fori_loop(1, steps_ref[t], advance, 0)

    def later(t, carry):
        tile(t, False)
        return carry

    tile(0, True)
    lax.fori_loop(1, tiles, later, 0)
    add(tiles - 1, jnp.maximum(steps_ref[tiles - 1] - 1, 0), products())
    some = owners // PIECES

    def departure(i):
        place = pl.ds(i * some, some)
        return pltpu.make_async_copy(terms_scr.at[place], terms_far.at[place], out_sems.at[i])

    for i in range(PIECES):
        for j in range(i * some, (i + 1) * some):
            found = place_ref[j]
            terms_scr[j, 0] = (acc_scr[found, 0] * SCALING).astype(jnp.bfloat16)
            terms_scr[j, 1] = acc_scr[found, 1].astype(jnp.bfloat16)
        departure(i).start()
    for i in range(PIECES):
        departure(i).wait()
    spill.wait()


def own_gradient_kernel(
    steps_ref, list_ref, q_ref, up_ref, anc_ref, bias_ref, att_ref, lse_ref, stat_ref, other_ref, hot_ref,
    bkv_ref, row_ref, norm_ref, dq_ref, dbr_ref, dq_scr, ds_scr,
):
    t = pl.program_id(0)
    owners, _, owned, _ = anc_ref.shape
    kv_heads = lse_ref.shape[1]
    groups = q_ref.shape[1] // HEAD_SIZE // kv_heads
    rows, near = groups * TILE, REACH + TILE
    scaler, pull = norm_terms(stat_ref, other_ref)
    norm_ref[...] = att_ref[...] * scaler
    d_out, d_outx = output_gradients(att_ref, up_ref, scaler, pull, kv_heads, groups)
    q = [stacked(q_ref, k, groups) for k in range(kv_heads)]
    hot = jnp.concatenate([hot_ref[...]] * groups, axis=0)
    qx = [jnp.concatenate([q[k], hot], axis=1) for k in range(kv_heads)]
    lse = [lse_ref[0, k, 0:1, :] for k in range(kv_heads)]
    ones = ones_columns(CHUNK * owned, 0)
    fixed = (list_ref, anc_ref, bias_ref, ones, qx, d_outx, lse)

    @pl.when(t == 0)
    def _():
        dbr_ref[...] = jnp.zeros_like(dbr_ref)

    window, allowed = allowed_keys(t, row_ref[0], (near, rows), 0)
    for k in range(kv_heads):
        keys = bkv_ref[0, pl.ds(window, near), head_columns(k)]
        values = bkv_ref[1, pl.ds(window, near), head_columns(k)]
        valuesx = jnp.concatenate([values, ones[:near]], axis=1)
        scores = jnp.where(allowed, dot(keys, q[k], ROWS_BY_ROWS), NEGATIVE)
        weights = jnp.exp2(scores * FACTOR - lse[k])
        d_scores = (weights * dot(valuesx, d_outx[k], ROWS_BY_ROWS)).astype(jnp.bfloat16)
        dbr_ref[0, pl.ds(window, near), head_columns(k)] += dot(d_scores, q[k], PLAIN) * SCALING
        dbr_ref[1, pl.ds(window, near), head_columns(k)] += dot(
            weights.astype(jnp.bfloat16), d_out[k], PLAIN
        )
        dq_scr[k] = dot(keys, d_scores, COLS_BY_COLS)

    def keep(d_scores):
        for k in range(kv_heads):
            ds_scr[k] = d_scores[k].astype(jnp.bfloat16)

    def pulled(c):
        _, clipped = chunk_ids(list_ref, t, c, owners)
        return [dot(chunk_rows(anc_ref, clipped, 0, k), ds_scr[k], COLS_BY_COLS) for k in range(kv_heads)]

    keep(gradient_scores(t, 0, *fixed)[1])

    def advance(c, carry):
        more = pulled(c - 1)
        keep(gradient_scores(t, c, *fixed)[1])
        for k in range(kv_heads):
            dq_scr[k] += more[k]
        return carry

    lax.fori_loop(1, steps_ref[t], advance, 0)
    more = pulled(jnp.maximum(steps_ref[t] - 1, 0))
    for k in range(kv_heads):
        d_query = ((dq_scr[k] + more[k]) * SCALING).T
        for g in range(groups):
            dq_ref[:, head_columns(k * groups + g)] = d_query[g * TILE : (g + 1) * TILE, :]


def copies_kernel(one_ref, many_ref, sems):
    count = one_ref.shape[0]
    moves = [
        pltpu.make_async_copy(one_ref, many_ref.at[pl.ds(i * count, count)], sems.at[i])
        for i in range(many_ref.shape[0] // count)
    ]
    for move in moves:
        move.start()
    for move in moves:
        move.wait()


def total_kernel(terms_ref, sum_ref):
    sum_ref[...] = jnp.sum(terms_ref[...].astype(jnp.float32), axis=0)


FAR, WHOLE, SLICED, SCALARS = "far", "whole", "sliced", "scalars"


def call(kernel, tiles, ins, outs, scratch=(), limit=60):
    def spec(array, way):
        if way == SCALARS:
            return pl.BlockSpec(memory_space=pltpu.SMEM)
        if way == FAR:
            return pl.BlockSpec(memory_space=pl.ANY)
        if way == WHOLE:
            return pl.BlockSpec(memory_space=pltpu.VMEM)
        rest = (0,) * (len(array.shape) - 1)
        return pl.BlockSpec((array.shape[0] // tiles,) + array.shape[1:], lambda t: (t,) + rest)

    def placed(array, way):
        return pltpu.with_memory_space_constraint(array, pltpu.MemorySpace.HBM) if way == FAR else array

    def shaped(array, way):
        return pltpu.MemorySpace.HBM(array.shape, array.dtype) if way == FAR else array

    return pl.pallas_call(
        kernel,
        **({"grid": (tiles,)} if tiles else {}),
        in_specs=[spec(*one) for one in ins],
        out_shape=[shaped(*one) for one in outs],
        out_specs=[spec(*one) for one in outs],
        scratch_shapes=list(scratch),
        compiler_params=pltpu.CompilerParams(vmem_limit_bytes=limit * 1024 * 1024),
    )(*[placed(*one) for one in ins])


def prepare(seg_lengths, anc_rows, token_count, groups):
    segments, owners = anc_rows.shape
    order = jnp.arange(segments, dtype=jnp.int32)
    finish = jnp.sum(jnp.where(order[:, None] <= order[None, :], seg_lengths[:, None], 0), axis=0)
    begin = finish - seg_lengths
    positions = jnp.arange(token_count, dtype=jnp.int32)
    member = (positions[:, None] >= begin) & (positions[:, None] < finish)
    starts = jnp.sum(jnp.where(member, begin, 0), axis=1)
    row = jnp.tile(starts.reshape(token_count // TILE, 1, TILE), (1, 1, groups))
    column = jnp.arange(HEAD_SIZE, dtype=jnp.int32)
    hot = jnp.sum(
        jnp.where(member[:, :, None] & (column == order[:, None]), 1.0, 0.0), axis=1
    ).astype(jnp.bfloat16)
    banned = jnp.concatenate([anc_rows == 0, jnp.ones((segments, 1), bool)], axis=1)
    bias = jnp.sum(
        jnp.where(banned[:, :, None] & (column == order[:, None, None]), NEGATIVE, 0.0), axis=0
    ).astype(jnp.bfloat16)
    bias = jnp.broadcast_to(bias[:, None, :], (owners + 1, 16, HEAD_SIZE))
    tiles = jnp.arange(token_count // TILE, dtype=jnp.int32)[:, None] * TILE
    active = (begin < tiles + TILE) & (finish > tiles)
    union = jnp.any(active[:, :, None] & (anc_rows != 0), axis=1)
    each = jnp.arange(owners, dtype=jnp.int32)
    place = jnp.sum((union[:, None, :] & (each[None, :] < each[:, None])).astype(jnp.int32), axis=2)
    counts = jnp.sum(union.astype(jnp.int32), axis=1)
    hit = union[:, None, :] & (place[:, None, :] == each[:, None])
    listed = jnp.sum(jnp.where(hit, each, 0), axis=2)
    listed = jnp.where(each < counts[:, None], listed, owners)
    return (counts + CHUNK - 1) // CHUNK, listed, bias, hot, row


EVERY = ("dp", "leaf", "head")


def exchange_groups(depth, side, cores):
    def flat(z, y, x, core):
        return ((z * side + y) * side + x) * cores + core

    deep, wide = range(depth), range(side)
    lines = [[flat(z, y, x, 0) for x in wide] for z in deep for y in wide]
    planes = [[flat(z, y, x, 0) for z in deep for y in wide] for x in wide]
    for core in range(1, cores):
        lines += [[flat(z, y, x, core) for y in wide] for z in deep for x in wide]
        planes += [[flat(z, y, x, core) for z in deep for x in wide] for y in wide]
    return lines, planes


def exchange(blocks, groups):
    return lax.all_to_all(blocks, EVERY, 0, 0, axis_index_groups=groups, tiled=True)


def arrival_order(values, depth, side):
    cube = values.reshape(values.shape[:-1] + (depth, side, side))
    first = jnp.moveaxis(cube, -1, -3).reshape(values.shape)
    second = jnp.swapaxes(cube, -2, -3).reshape(values.shape)
    return jnp.where(lax.axis_index("head") == 0, first, second)


def local(queries, branch_kv, ancestor_key_value, upstream, lengths, ancestors):
    token_count, width = queries.shape
    kv_heads = branch_kv.shape[2] // HEAD_SIZE
    groups = width // HEAD_SIZE // kv_heads
    owners = ancestors.shape[1]
    owned = ancestor_key_value.shape[1]
    tiles = token_count // TILE
    rows = groups * TILE
    each = (owners,) + ancestor_key_value.shape
    side, cores = lax.axis_size("leaf"), lax.axis_size("head")
    depth = owners // (side * side)
    lines, planes = exchange_groups(depth, side, cores)
    order = arrival_order(jnp.arange(owners, dtype=jnp.int32), depth, side)
    places = jnp.sum(
        jnp.where(order[None, :] == jnp.arange(owners)[:, None], jnp.arange(owners, dtype=jnp.int32)[None, :], 0), axis=1
    )
    f32, bf16 = jnp.float32, jnp.bfloat16

    def new(shape, dtype=f32):
        return jax.ShapeDtypeStruct(shape, dtype)

    def spread(block, times):
        shape = (block.shape[0] * times,) + block.shape[1:]
        return call(
            copies_kernel, 0, [(block, WHOLE)], [(new(shape, bf16), FAR)],
            [pltpu.SemaphoreType.DMA((times,))], limit=8,
        )[0]

    plane = exchange(spread(ancestor_key_value[None], depth * side), planes)
    gathered = exchange(spread(plane, side), lines)
    steps, listed, bias, hot, row = prepare(
        lengths[0], arrival_order(ancestors, depth, side), token_count, groups
    )
    scalars = [(steps, SCALARS), (listed, SCALARS)]
    near, both = call(
        near_kernel, tiles,
        [(queries, SLICED), (branch_kv, WHOLE), (row, SLICED)],
        [(new((tiles, kv_heads, HEAD_SIZE, rows)), SLICED), (new((tiles, kv_heads, 8, rows)), SLICED)],
    )
    whole = (token_count, width)
    attended, lse, stats, near_queries, near_upstream = call(
        forward_kernel, 0,
        scalars + [
            (queries, FAR), (upstream, FAR), (near, FAR), (both, FAR), (hot, WHOLE), (gathered, WHOLE),
            (bias, WHOLE),
        ],
        [
            (new(whole), WHOLE), (new((tiles, kv_heads, 8, rows)), WHOLE),
            (new((token_count, 2 * HEAD_SIZE)), WHOLE), (new(whole, bf16), WHOLE), (new(whole, bf16), WHOLE),
        ],
        [
            pltpu.VMEM((tiles, kv_heads, HEAD_SIZE, rows), f32),
            pltpu.VMEM((tiles, kv_heads, 8, rows), f32),
            pltpu.SemaphoreType.DMA((4, tiles)),
            pltpu.VMEM((kv_heads, CHUNK * owned, rows), bf16),
            pltpu.VMEM((kv_heads, 8, rows), f32),
            pltpu.VMEM((kv_heads, HEAD_SIZE, rows), f32),
            pltpu.VMEM((kv_heads, 1, rows), f32),
        ],
        limit=28,
    )
    other = lax.ppermute(stats, "head", [(0, 1), (1, 0)])
    terms, attended = call(
        shared_gradient_kernel, 0,
        scalars + [
            (places, SCALARS), (near_queries, WHOLE), (near_upstream, WHOLE), (attended, WHOLE), (stats, WHOLE), (other, WHOLE), (lse, WHOLE),
            (hot, WHOLE), (gathered, WHOLE), (bias, WHOLE),
        ],
        [(new(each, bf16), FAR), (new(whole), FAR)],
        [
            pltpu.VMEM(each, bf16),
            pltpu.SemaphoreType.DMA((PIECES + 1,)),
            pltpu.VMEM(each, f32),
            pltpu.VMEM((kv_heads, CHUNK * owned, rows), bf16),
            pltpu.VMEM((kv_heads, CHUNK * owned, rows), bf16),
            pltpu.VMEM((kv_heads, rows, HEAD_SIZE), bf16),
            pltpu.VMEM((kv_heads, rows, HEAD_SIZE), bf16),
        ],
        limit=28,
    )
    received = lax.all_to_all(terms, ("dp", "leaf"), 0, 0, tiled=True)
    normed, d_queries, d_branch = call(
        own_gradient_kernel, tiles,
        scalars + [
            (queries, SLICED), (upstream, SLICED), (gathered, WHOLE), (bias, WHOLE), (attended, SLICED),
            (lse, SLICED), (stats, SLICED), (other, SLICED), (hot, SLICED), (branch_kv, WHOLE), (row, SLICED),
        ],
        [(new(whole), SLICED), (new(whole), SLICED), (new(branch_kv.shape), WHOLE)],
        [
            pltpu.VMEM((kv_heads, HEAD_SIZE, rows), f32),
            pltpu.VMEM((kv_heads, CHUNK * owned, rows), bf16),
        ],
    )
    (summed,) = call(
        total_kernel, 0, [(received, WHOLE)], [(new(ancestor_key_value.shape), WHOLE)], limit=8
    )
    return (normed, d_queries, d_branch, summed)


def solution(mesh):
    placed = (
        P(("dp", "leaf"), "head"),
        P(None, ("dp", "leaf"), "head"),
        P(None, ("dp", "leaf"), "head"),
        P(("dp", "leaf"), "head"),
        P(("dp", "leaf"), None),
        P(("dp", "leaf"), None),
    )
    return jax.shard_map(
        local,
        mesh=mesh,
        in_specs=placed,
        out_specs=(
            P(("dp", "leaf"), "head"),
            P(("dp", "leaf"), "head"),
            P(None, ("dp", "leaf"), "head"),
            P(None, ("dp", "leaf"), "head"),
        ),
        check_vma=False,
    )
```

```python
import jax
import jax.numpy as jnp
from jax import lax
from jax.experimental import pallas as pl
from jax.experimental.pallas import tpu as pltpu
from jax.sharding import PartitionSpec as P

QUERY_HEADS = 32
HEAD_SIZE = 128
NEGATIVE = -1e30
EPSILON = 1e-05
RANGE = 1e25
PIECES = 8
LOG2E = 1.4426950408889634

TILE = 64
CHUNK = 8
REACH = 128
SEGMENTS = 4
SCALING = HEAD_SIZE ** (-0.5)
FACTOR = SCALING * LOG2E

ROWS_BY_ROWS = (((1,), (1,)), ((), ()))
COLS_BY_COLS = (((0,), (0,)), ((), ()))
PLAIN = (((1,), (0,)), ((), ()))


def dot(a, b, dims):
    return lax.dot_general(a, b, dims, preferred_element_type=jnp.float32)


def head_columns(index):
    return pl.ds(index * HEAD_SIZE, HEAD_SIZE)


def stacked(ref, kv_head, groups):
    return jnp.concatenate(
        [ref[:, head_columns(kv_head * groups + g)] for g in range(groups)], axis=0
    )


def halves(values, op):
    return op(values[:, :HEAD_SIZE], values[:, HEAD_SIZE:])


def column(values):
    lane = lax.broadcasted_iota(jnp.int32, values.shape[:1] + (HEAD_SIZE,), 1)
    first = values.astype(jnp.bfloat16).astype(jnp.float32)
    second = (values - first).astype(jnp.bfloat16).astype(jnp.float32)
    return lane, first, second, values - first - second


def pieces(values, place):
    lane, first, second, third = column(values)
    parts = jnp.where(lane == place, first, jnp.where(lane == place + 1, second, third))
    wanted = (lane >= place) & (lane < place + 3)
    return jnp.where(wanted, parts, 0.0).astype(jnp.bfloat16)


def allowed_keys(t, starts, shape, key_axis):
    window = pl.multiple_of(jnp.maximum(t * TILE - REACH, 0), TILE)
    keys = window + lax.broadcasted_iota(jnp.int32, shape, key_axis)
    tokens = t * TILE + (lax.broadcasted_iota(jnp.int32, shape, 1 - key_axis) & (TILE - 1))
    return window, (keys <= tokens) & (keys >= starts)


def chunk_ids(list_ref, t, c, owners):
    ids = [list_ref[t, c * CHUNK + i] for i in range(CHUNK)]
    return ids, [jnp.minimum(j, owners - 1) for j in ids]


def chunk_rows(anc_ref, clipped, part, kv_head):
    return jnp.concatenate([anc_ref[j, part, :, head_columns(kv_head)] for j in clipped], axis=0)


def chunk_bias(bias_ref, ids):
    return jnp.concatenate([bias_ref[j] for j in ids for _ in range(2)], axis=0)


def near_kernel(q_ref, bkv_ref, row_ref, hot_ref, plane_ref, bias_ref, out_ref, both_ref):
    t = pl.program_id(0)
    kv_heads = bkv_ref.shape[2] // HEAD_SIZE
    groups = q_ref.shape[1] // HEAD_SIZE // kv_heads
    rows, near = groups * TILE, REACH + TILE
    window, allowed = allowed_keys(t, row_ref[0], (near, rows), 0)
    hot = jnp.concatenate([hot_ref[...]] * groups, axis=0)
    chunks = [list(range(c, c + CHUNK)) for c in range(0, plane_ref.shape[0], CHUNK)]
    for k in range(kv_heads):
        q = stacked(q_ref, k, groups)
        qx = jnp.concatenate([q, hot], axis=1)
        keys = bkv_ref[0, pl.ds(window, near), head_columns(k)]
        scores = [jnp.where(allowed, dot(keys, q, ROWS_BY_ROWS), NEGATIVE)]
        values = [bkv_ref[1, pl.ds(window, near), head_columns(k)]]
        for ids in chunks:
            keys = jnp.concatenate([chunk_rows(plane_ref, ids, 0, k), chunk_bias(bias_ref, ids)], axis=1)
            scores.append(dot(keys, qx, ROWS_BY_ROWS))
            values.append(chunk_rows(plane_ref, ids, 1, k))
        top = scores[0].max(axis=0, keepdims=True)
        for part in scores[1:]:
            top = jnp.maximum(top, jnp.max(part, axis=0, keepdims=True))
        weights = [jnp.exp2((part - top) * FACTOR) for part in scores]
        out_ref[0, k] = sum(
            dot(value, weight.astype(jnp.bfloat16), COLS_BY_COLS) for value, weight in zip(values, weights)
        )
        both_ref[0, k, 0:1, :] = top
        both_ref[0, k, 1:2, :] = sum(jnp.sum(weight, axis=0, keepdims=True) for weight in weights)


def fold(values, op):
    rows, width = values.shape
    return op(values.reshape(rows // 8, 8, width), axis=0)


def tile_rows(ref, t):
    return ref.at[pl.ds(pl.multiple_of(t * TILE, TILE), TILE)]


def arrival(t, sems, pairs, first=0):
    moves = []
    for i, (far, near, stacked_tiles) in enumerate(pairs, first):
        if stacked_tiles:
            moves.append(pltpu.make_async_copy(far.at[t], near.at[t], sems.at[i, t]))
        else:
            moves.append(pltpu.make_async_copy(tile_rows(far, t), tile_rows(near, t), sems.at[i, t]))
    return moves


def forward_kernel(
    steps_ref, list_ref, q_far, up_far, near_far, both_far, hot_ref, anc_ref, bias_ref,
    att_all, lse_ref, stat_ref, q_all, up_all,
    near_all, both_ref, in_sems, w_scr, sum_scr, o_scr, shift_scr,
):
    tiles, kv_heads, _, rows = both_ref.shape
    owners = anc_ref.shape[0]
    groups = rows // TILE
    early = [(q_far, q_all, False), (both_far, both_ref, True)]
    late = [(up_far, up_all, False), (near_far, near_all, True)]
    for t in range(tiles):
        for move in arrival(t, in_sems, early + late):
            move.start()

    def hot_of(t):
        return jnp.concatenate([tile_rows(hot_ref, t)[...]] * groups, axis=0)

    def queries_of(t):
        hot = hot_of(t)
        return [
            jnp.concatenate([stacked(tile_rows(q_all, t), k, groups), hot], axis=1) for k in range(kv_heads)
        ]

    def scored(t, c, qx):
        ids, clipped = chunk_ids(list_ref, t, c, owners)
        bias = chunk_bias(bias_ref, ids)
        keys = [jnp.concatenate([chunk_rows(anc_ref, clipped, 0, k), bias], axis=1) for k in range(kv_heads)]
        return [dot(keys[k], qx[k], ROWS_BY_ROWS) for k in range(kv_heads)]

    def weigh(t, c, qx, shifts):
        scores = scored(t, c, qx)
        return [jnp.exp2(scores[k] * FACTOR - shifts[k]) for k in range(kv_heads)]

    def valued(t, c):
        _, clipped = chunk_ids(list_ref, t, c, owners)
        return [dot(chunk_rows(anc_ref, clipped, 1, k), w_scr[k], COLS_BY_COLS) for k in range(kv_heads)]

    def keep(weights):
        for k in range(kv_heads):
            w_scr[k] = weights[k].astype(jnp.bfloat16)

    def near_shifts(t):
        return [both_ref[t, k, 0:1, :] * FACTOR for k in range(kv_heads)]

    def finish(old, last):
        near_tops = near_shifts(old)
        for k in range(kv_heads):
            o_scr[k] += last[k]
            sum_scr[k, 0:1, :] = jnp.sum(sum_scr[k], axis=0, keepdims=True)
            shift_scr[k] = near_tops[k]

        largest = jnp.max(jnp.maximum(sum_scr[0, 0:1, :], sum_scr[1, 0:1, :]))

        @pl.when(jnp.logical_not(largest < RANGE))
        def _():
            steps = steps_ref[old]
            qx = queries_of(old)

            def score(c, tops):
                scores = scored(old, c, qx)
                return tuple(jnp.maximum(tops[k], fold(scores[k], jnp.max)) for k in range(kv_heads))

            start = jnp.full((8, rows), NEGATIVE, jnp.float32)
            tops = lax.fori_loop(0, steps, score, (start,) * kv_heads)
            shifts = []
            for k in range(kv_heads):
                top = jnp.max(tops[k], axis=0, keepdims=True) * FACTOR
                shifts.append(jnp.maximum(top, near_tops[k]))
                shift_scr[k] = shifts[k]
            o_scr[...] = jnp.zeros_like(o_scr)

            def gather(c, sums):
                weights = weigh(old, c, qx, shifts)
                keep(weights)
                more = valued(old, c)
                for k in range(kv_heads):
                    o_scr[k] += more[k]
                return tuple(sums[k] + fold(weights[k], jnp.sum) for k in range(kv_heads))

            sums = lax.fori_loop(0, steps, gather, (jnp.zeros((8, rows), jnp.float32),) * kv_heads)
            for k in range(kv_heads):
                sum_scr[k, 0:1, :] = jnp.sum(sums[k], axis=0, keepdims=True)

        for move in arrival(old, in_sems, late, len(early)):
            move.wait()
        upper_ref, att_ref, stats_ref = tile_rows(up_all, old), tile_rows(att_all, old), tile_rows(stat_ref, old)
        squares = jnp.zeros((TILE, HEAD_SIZE), jnp.float32)
        inner = jnp.zeros((TILE, HEAD_SIZE), jnp.float32)
        for k in range(kv_heads):
            shift = shift_scr[k]
            fade = jnp.exp2(near_tops[k] - shift)
            total = sum_scr[k, 0:1, :] + fade * both_ref[old, k, 1:2, :]
            attended = ((o_scr[k] + fade * near_all[old, k]) * (1.0 / total)).T
            lse_ref[old, k, 0:1, :] = shift + jnp.log2(total)
            for g in range(groups):
                slab = attended[g * TILE : (g + 1) * TILE, :]
                upper = upper_ref[:, head_columns(k * groups + g)].astype(jnp.float32)
                att_ref[:, head_columns(k * groups + g)] = slab
                squares += slab * slab
                inner += slab * upper
        stats_ref[:, 0:HEAD_SIZE] = squares
        stats_ref[:, HEAD_SIZE : 2 * HEAD_SIZE] = inner

    def tile(now, first):
        for move in arrival(now, in_sems, early):
            move.wait()
        old = now - 1
        qx, shifts = queries_of(now), near_shifts(now)
        if not first:
            last = valued(old, jnp.maximum(steps_ref[old] - 1, 0))
        fresh = weigh(now, 0, qx, shifts)
        if not first:
            finish(old, last)
        keep(fresh)
        for k in range(kv_heads):
            sum_scr[k] = fold(fresh[k], jnp.sum)
            o_scr[k] = jnp.zeros_like(o_scr[k])

        def advance(c, carry):
            more = valued(now, c - 1)
            weights = weigh(now, c, qx, shifts)
            keep(weights)
            for k in range(kv_heads):
                o_scr[k] += more[k]
                sum_scr[k] += fold(weights[k], jnp.sum)
            return carry

        lax.fori_loop(1, steps_ref[now], advance, 0)

    def later(now, carry):
        tile(now, False)
        return carry

    tile(0, True)
    lax.fori_loop(1, tiles, later, 0)
    finish(tiles - 1, valued(tiles - 1, jnp.maximum(steps_ref[tiles - 1] - 1, 0)))


def norm_terms(stat_ref, other_ref):
    columns = QUERY_HEADS * HEAD_SIZE
    stats = stat_ref[...] + other_ref[...]
    squares = jnp.sum(stats[:, :HEAD_SIZE], axis=1, keepdims=True)
    inner = jnp.sum(stats[:, HEAD_SIZE:], axis=1, keepdims=True)
    scaler = lax.rsqrt(squares / columns + EPSILON)
    return scaler, scaler * scaler * scaler * inner / columns


def output_gradients(att_ref, up_ref, scaler, pull, kv_heads, groups):
    found, extended = [], []
    for k in range(kv_heads):
        slabs, extra = [], []
        for g in range(groups):
            slab = att_ref[:, head_columns(k * groups + g)]
            upper = up_ref[:, head_columns(k * groups + g)].astype(jnp.float32)
            rounded = (scaler * upper - slab * pull).astype(jnp.bfloat16)
            delta = jnp.sum(rounded.astype(jnp.float32) * slab, axis=1, keepdims=True)
            extra.append(pieces(-delta, 0))
            slabs.append(rounded)
        found.append(jnp.concatenate(slabs, axis=0))
        extended.append(jnp.concatenate([found[k], jnp.concatenate(extra, axis=0)], axis=1))
    return found, extended


def ones_columns(rows, place):
    lane = lax.broadcasted_iota(jnp.int32, (rows, HEAD_SIZE), 1)
    return ((lane >= place) & (lane < place + 3)).astype(jnp.bfloat16)


def gradient_scores(t, c, list_ref, anc_ref, bias_ref, ones, qx, d_outx, lse):
    ids, clipped = chunk_ids(list_ref, t, c, anc_ref.shape[0])
    bias = chunk_bias(bias_ref, ids)
    weights, d_scores = [], []
    for k in range(len(qx)):
        keys = jnp.concatenate([chunk_rows(anc_ref, clipped, 0, k), bias], axis=1)
        values = jnp.concatenate([chunk_rows(anc_ref, clipped, 1, k), ones], axis=1)
        weights.append(jnp.exp2(dot(keys, qx[k], ROWS_BY_ROWS) * FACTOR - lse[k]))
        d_scores.append(weights[k] * dot(values, d_outx[k], ROWS_BY_ROWS))
    return weights, d_scores


def shared_gradient_kernel(
    steps_ref, list_ref, place_ref, q_all, up_all, att_all, stat_ref, other_ref, lse_ref, hot_ref, anc_ref, bias_ref,
    terms_far, att_far,
    terms_scr, out_sems, acc_scr, w_scr, ds_scr, q_scr, do_scr,
):
    tiles, kv_heads, _, rows = lse_ref.shape
    groups = rows // TILE
    owners, _, owned, _ = anc_ref.shape
    ones = ones_columns(CHUNK * owned, 0)
    spill = pltpu.make_async_copy(att_all, att_far, out_sems.at[PIECES])
    spill.start()
    acc_scr[...] = jnp.zeros_like(acc_scr)

    def products():
        return [(dot(ds_scr[k], q_scr[k], PLAIN), dot(w_scr[k], do_scr[k], PLAIN)) for k in range(kv_heads)]

    def add(t, c, found):
        _, clipped = chunk_ids(list_ref, t, c, owners)
        for k in range(kv_heads):
            for i, j in enumerate(clipped):
                place = slice(i * owned, (i + 1) * owned)
                for part in range(2):
                    acc_scr[j, part, :, head_columns(k)] += found[k][part][place]

    def keep(weights, d_scores):
        for k in range(kv_heads):
            w_scr[k] = weights[k].astype(jnp.bfloat16)
            ds_scr[k] = d_scores[k].astype(jnp.bfloat16)

    def tile(t, first):
        if not first:
            found = products()
        scaler, pull = norm_terms(tile_rows(stat_ref, t), tile_rows(other_ref, t))
        d_out, d_outx = output_gradients(
            tile_rows(att_all, t), tile_rows(up_all, t), scaler, pull, kv_heads, groups
        )
        q = [stacked(tile_rows(q_all, t), k, groups) for k in range(kv_heads)]
        hot = jnp.concatenate([tile_rows(hot_ref, t)[...]] * groups, axis=0)
        qx = [jnp.concatenate([q[k], hot], axis=1) for k in range(kv_heads)]
        lse = [lse_ref[t, k, 0:1, :] for k in range(kv_heads)]
        fixed = (list_ref, anc_ref, bias_ref, ones, qx, d_outx, lse)
        weights, d_scores = gradient_scores(t, 0, *fixed)
        keep(weights, d_scores)
        for k in range(kv_heads):
            q_scr[k] = q[k]
            do_scr[k] = d_out[k]
        if not first:
            add(t - 1, jnp.maximum(steps_ref[t - 1] - 1, 0), found)

        def advance(c, carry):
            found = products()
            weights, d_scores = gradient_scores(t, c, *fixed)
            keep(weights, d_scores)
            add(t, c - 1, found)
            return carry

        lax.fori_loop(1, steps_ref[t], advance, 0)

    def later(t, carry):
        tile(t, False)
        return carry

    tile(0, True)
    lax.fori_loop(1, tiles, later, 0)
    add(tiles - 1, jnp.maximum(steps_ref[tiles - 1] - 1, 0), products())
    some = owners // PIECES

    def departure(i):
        place = pl.ds(i * some, some)
        return pltpu.make_async_copy(terms_scr.at[place], terms_far.at[place], out_sems.at[i])

    for i in range(PIECES):
        for j in range(i * some, (i + 1) * some):
            found = place_ref[j]
            terms_scr[j, 0] = (acc_scr[found, 0] * SCALING).astype(jnp.bfloat16)
            terms_scr[j, 1] = acc_scr[found, 1].astype(jnp.bfloat16)
        departure(i).start()
    for i in range(PIECES):
        departure(i).wait()
    spill.wait()


def own_gradient_kernel(
    steps_ref, list_ref, q_ref, up_ref, anc_ref, bias_ref, att_ref, lse_ref, stat_ref, other_ref, hot_ref,
    bkv_ref, row_ref, norm_ref, dq_ref, dbr_ref, dq_scr, ds_scr,
):
    t = pl.program_id(0)
    owners, _, owned, _ = anc_ref.shape
    kv_heads = lse_ref.shape[1]
    groups = q_ref.shape[1] // HEAD_SIZE // kv_heads
    rows, near = groups * TILE, REACH + TILE
    scaler, pull = norm_terms(stat_ref, other_ref)
    norm_ref[...] = att_ref[...] * scaler
    d_out, d_outx = output_gradients(att_ref, up_ref, scaler, pull, kv_heads, groups)
    q = [stacked(q_ref, k, groups) for k in range(kv_heads)]
    hot = jnp.concatenate([hot_ref[...]] * groups, axis=0)
    qx = [jnp.concatenate([q[k], hot], axis=1) for k in range(kv_heads)]
    lse = [lse_ref[0, k, 0:1, :] for k in range(kv_heads)]
    ones = ones_columns(CHUNK * owned, 0)
    fixed = (list_ref, anc_ref, bias_ref, ones, qx, d_outx, lse)

    @pl.when(t == 0)
    def _():
        dbr_ref[...] = jnp.zeros_like(dbr_ref)

    window, allowed = allowed_keys(t, row_ref[0], (near, rows), 0)
    for k in range(kv_heads):
        keys = bkv_ref[0, pl.ds(window, near), head_columns(k)]
        values = bkv_ref[1, pl.ds(window, near), head_columns(k)]
        valuesx = jnp.concatenate([values, ones[:near]], axis=1)
        scores = jnp.where(allowed, dot(keys, q[k], ROWS_BY_ROWS), NEGATIVE)
        weights = jnp.exp2(scores * FACTOR - lse[k])
        d_scores = (weights * dot(valuesx, d_outx[k], ROWS_BY_ROWS)).astype(jnp.bfloat16)
        dbr_ref[0, pl.ds(window, near), head_columns(k)] += dot(d_scores, q[k], PLAIN) * SCALING
        dbr_ref[1, pl.ds(window, near), head_columns(k)] += dot(
            weights.astype(jnp.bfloat16), d_out[k], PLAIN
        )
        dq_scr[k] = dot(keys, d_scores, COLS_BY_COLS)

    def keep(d_scores):
        for k in range(kv_heads):
            ds_scr[k] = d_scores[k].astype(jnp.bfloat16)

    def pulled(c):
        _, clipped = chunk_ids(list_ref, t, c, owners)
        return [dot(chunk_rows(anc_ref, clipped, 0, k), ds_scr[k], COLS_BY_COLS) for k in range(kv_heads)]

    keep(gradient_scores(t, 0, *fixed)[1])

    def advance(c, carry):
        more = pulled(c - 1)
        keep(gradient_scores(t, c, *fixed)[1])
        for k in range(kv_heads):
            dq_scr[k] += more[k]
        return carry

    lax.fori_loop(1, steps_ref[t], advance, 0)
    more = pulled(jnp.maximum(steps_ref[t] - 1, 0))
    for k in range(kv_heads):
        d_query = ((dq_scr[k] + more[k]) * SCALING).T
        for g in range(groups):
            dq_ref[:, head_columns(k * groups + g)] = d_query[g * TILE : (g + 1) * TILE, :]


def copies_kernel(one_ref, many_ref, sems):
    count = one_ref.shape[0]
    moves = [
        pltpu.make_async_copy(one_ref, many_ref.at[pl.ds(i * count, count)], sems.at[i])
        for i in range(many_ref.shape[0] // count)
    ]
    for move in moves:
        move.start()
    for move in moves:
        move.wait()


def total_kernel(terms_ref, sum_ref):
    sum_ref[...] = jnp.sum(terms_ref[...].astype(jnp.float32), axis=0)


FAR, WHOLE, SLICED, SCALARS = "far", "whole", "sliced", "scalars"


def call(kernel, tiles, ins, outs, scratch=(), limit=60):
    def spec(array, way):
        if way == SCALARS:
            return pl.BlockSpec(memory_space=pltpu.SMEM)
        if way == FAR:
            return pl.BlockSpec(memory_space=pl.ANY)
        if way == WHOLE:
            return pl.BlockSpec(memory_space=pltpu.VMEM)
        rest = (0,) * (len(array.shape) - 1)
        return pl.BlockSpec((array.shape[0] // tiles,) + array.shape[1:], lambda t: (t,) + rest)

    def placed(array, way):
        return pltpu.with_memory_space_constraint(array, pltpu.MemorySpace.HBM) if way == FAR else array

    def shaped(array, way):
        return pltpu.MemorySpace.HBM(array.shape, array.dtype) if way == FAR else array

    return pl.pallas_call(
        kernel,
        **({"grid": (tiles,)} if tiles else {}),
        in_specs=[spec(*one) for one in ins],
        out_shape=[shaped(*one) for one in outs],
        out_specs=[spec(*one) for one in outs],
        scratch_shapes=list(scratch),
        compiler_params=pltpu.CompilerParams(vmem_limit_bytes=limit * 1024 * 1024),
    )(*[placed(*one) for one in ins])


def prepare(seg_lengths, anc_rows, token_count, groups, first, count):
    segments, owners = anc_rows.shape
    order = jnp.arange(segments, dtype=jnp.int32)
    finish = jnp.sum(jnp.where(order[:, None] <= order[None, :], seg_lengths[:, None], 0), axis=0)
    begin = finish - seg_lengths
    positions = jnp.arange(token_count, dtype=jnp.int32)
    member = (positions[:, None] >= begin) & (positions[:, None] < finish)
    starts = jnp.sum(jnp.where(member, begin, 0), axis=1)
    row = jnp.tile(starts.reshape(token_count // TILE, 1, TILE), (1, 1, groups))
    column = jnp.arange(HEAD_SIZE, dtype=jnp.int32)
    hot = jnp.sum(
        jnp.where(member[:, :, None] & (column == order[:, None]), 1.0, 0.0), axis=1
    ).astype(jnp.bfloat16)
    banned = jnp.concatenate([anc_rows == 0, jnp.ones((segments, 1), bool)], axis=1)
    bias = jnp.sum(
        jnp.where(banned[:, :, None] & (column == order[:, None, None]), NEGATIVE, 0.0), axis=0
    ).astype(jnp.bfloat16)
    bias = jnp.broadcast_to(bias[:, None, :], (owners + 1, 16, HEAD_SIZE))
    tiles = jnp.arange(token_count // TILE, dtype=jnp.int32)[:, None] * TILE
    active = (begin < tiles + TILE) & (finish > tiles)
    union = jnp.any(active[:, :, None] & (anc_rows != 0), axis=1)
    each = jnp.arange(owners, dtype=jnp.int32)

    def ordered(union):
        place = jnp.sum((union[:, None, :] & (each[None, :] < each[:, None])).astype(jnp.int32), axis=2)
        counts = jnp.sum(union.astype(jnp.int32), axis=1)
        hit = union[:, None, :] & (place[:, None, :] == each[:, None])
        listed = jnp.sum(jnp.where(hit, each, 0), axis=2)
        listed = jnp.where(each < counts[:, None], listed, owners)
        return (counts + CHUNK - 1) // CHUNK, listed

    mine = (each >= first) & (each < first + count)
    return ordered(union), ordered(union & ~mine), bias, hot, row


EVERY = ("dp", "leaf", "head")


def exchange_groups(depth, side, cores):
    def flat(z, y, x, core):
        return ((z * side + y) * side + x) * cores + core

    deep, wide = range(depth), range(side)
    lines = [[flat(z, y, x, 0) for x in wide] for z in deep for y in wide]
    planes = [[flat(z, y, x, 0) for z in deep for y in wide] for x in wide]
    for core in range(1, cores):
        lines += [[flat(z, y, x, core) for y in wide] for z in deep for x in wide]
        planes += [[flat(z, y, x, core) for z in deep for x in wide] for y in wide]
    return lines, planes


def exchange(blocks, groups):
    return lax.all_to_all(blocks, EVERY, 0, 0, axis_index_groups=groups, tiled=True)


def arrival_order(values, depth, side):
    cube = values.reshape(values.shape[:-1] + (depth, side, side))
    first = jnp.moveaxis(cube, -1, -3).reshape(values.shape)
    second = jnp.swapaxes(cube, -2, -3).reshape(values.shape)
    return jnp.where(lax.axis_index("head") == 0, first, second)


def local(queries, branch_kv, ancestor_key_value, upstream, lengths, ancestors):
    token_count, width = queries.shape
    kv_heads = branch_kv.shape[2] // HEAD_SIZE
    groups = width // HEAD_SIZE // kv_heads
    owners = ancestors.shape[1]
    owned = ancestor_key_value.shape[1]
    tiles = token_count // TILE
    rows = groups * TILE
    each = (owners,) + ancestor_key_value.shape
    side, cores = lax.axis_size("leaf"), lax.axis_size("head")
    depth = owners // (side * side)
    lines, planes = exchange_groups(depth, side, cores)
    order = arrival_order(jnp.arange(owners, dtype=jnp.int32), depth, side)
    places = jnp.sum(
        jnp.where(order[None, :] == jnp.arange(owners)[:, None], jnp.arange(owners, dtype=jnp.int32)[None, :], 0), axis=1
    )
    f32, bf16 = jnp.float32, jnp.bfloat16

    def new(shape, dtype=f32):
        return jax.ShapeDtypeStruct(shape, dtype)

    def spread(block, times, way):
        shape = (block.shape[0] * times,) + block.shape[1:]
        return call(
            copies_kernel, 0, [(block, way)], [(new(shape, bf16), FAR)],
            [pltpu.SemaphoreType.DMA((times,))], limit=8,
        )[0]

    count = depth * side
    plane = exchange(spread(ancestor_key_value[None], count, WHOLE), planes)
    row_of, column_of = lax.axis_index("dp") % side, lax.axis_index("leaf")
    first = jnp.where(lax.axis_index("head") == 0, column_of, row_of) * count
    (steps, listed), (far_steps, far_listed), bias, hot, row = prepare(
        lengths[0], arrival_order(ancestors, depth, side), token_count, groups, first, count
    )
    own_bias = lax.dynamic_slice_in_dim(bias, first, count, 0)
    row, plane = lax.optimization_barrier((row, plane))
    gathered = exchange(spread(plane, side, WHOLE), lines)
    scalars = [(steps, SCALARS), (listed, SCALARS)]
    near, both = call(
        near_kernel, tiles,
        [
            (queries, SLICED), (branch_kv, WHOLE), (row, SLICED), (hot, SLICED), (plane, WHOLE), (own_bias, WHOLE),
        ],
        [(new((tiles, kv_heads, HEAD_SIZE, rows)), SLICED), (new((tiles, kv_heads, 8, rows)), SLICED)],
    )
    whole = (token_count, width)
    attended, lse, stats, near_queries, near_upstream = call(
        forward_kernel, 0,
        [
            (far_steps, SCALARS), (far_listed, SCALARS),
            (queries, FAR), (upstream, FAR), (near, FAR), (both, FAR), (hot, WHOLE), (gathered, WHOLE),
            (bias, WHOLE),
        ],
        [
            (new(whole), WHOLE), (new((tiles, kv_heads, 8, rows)), WHOLE),
            (new((token_count, 2 * HEAD_SIZE)), WHOLE), (new(whole, bf16), WHOLE), (new(whole, bf16), WHOLE),
        ],
        [
            pltpu.VMEM((tiles, kv_heads, HEAD_SIZE, rows), f32),
            pltpu.VMEM((tiles, kv_heads, 8, rows), f32),
            pltpu.SemaphoreType.DMA((4, tiles)),
            pltpu.VMEM((kv_heads, CHUNK * owned, rows), bf16),
            pltpu.VMEM((kv_heads, 8, rows), f32),
            pltpu.VMEM((kv_heads, HEAD_SIZE, rows), f32),
            pltpu.VMEM((kv_heads, 1, rows), f32),
        ],
        limit=28,
    )
    other = lax.ppermute(stats, "head", [(0, 1), (1, 0)])
    terms, attended = call(
        shared_gradient_kernel, 0,
        scalars + [
            (places, SCALARS), (near_queries, WHOLE), (near_upstream, WHOLE), (attended, WHOLE), (stats, WHOLE), (other, WHOLE), (lse, WHOLE),
            (hot, WHOLE), (gathered, WHOLE), (bias, WHOLE),
        ],
        [(new(each, bf16), FAR), (new(whole), FAR)],
        [
            pltpu.VMEM(each, bf16),
            pltpu.SemaphoreType.DMA((PIECES + 1,)),
            pltpu.VMEM(each, f32),
            pltpu.VMEM((kv_heads, CHUNK * owned, rows), bf16),
            pltpu.VMEM((kv_heads, CHUNK * owned, rows), bf16),
            pltpu.VMEM((kv_heads, rows, HEAD_SIZE), bf16),
            pltpu.VMEM((kv_heads, rows, HEAD_SIZE), bf16),
        ],
        limit=28,
    )
    received = lax.all_to_all(terms, ("dp", "leaf"), 0, 0, tiled=True)
    normed, d_queries, d_branch = call(
        own_gradient_kernel, tiles,
        scalars + [
            (queries, SLICED), (upstream, SLICED), (gathered, WHOLE), (bias, WHOLE), (attended, SLICED),
            (lse, SLICED), (stats, SLICED), (other, SLICED), (hot, SLICED), (branch_kv, WHOLE), (row, SLICED),
        ],
        [(new(whole), SLICED), (new(whole), SLICED), (new(branch_kv.shape), WHOLE)],
        [
            pltpu.VMEM((kv_heads, HEAD_SIZE, rows), f32),
            pltpu.VMEM((kv_heads, CHUNK * owned, rows), bf16),
        ],
    )
    (summed,) = call(
        total_kernel, 0, [(received, WHOLE)], [(new(ancestor_key_value.shape), WHOLE)], limit=8
    )
    return (normed, d_queries, d_branch, summed)


def solution(mesh):
    placed = (
        P(("dp", "leaf"), "head"),
        P(None, ("dp", "leaf"), "head"),
        P(None, ("dp", "leaf"), "head"),
        P(("dp", "leaf"), "head"),
        P(("dp", "leaf"), None),
        P(("dp", "leaf"), None),
    )
    return jax.shard_map(
        local,
        mesh=mesh,
        in_specs=placed,
        out_specs=(
            P(("dp", "leaf"), "head"),
            P(("dp", "leaf"), "head"),
            P(None, ("dp", "leaf"), "head"),
            P(None, ("dp", "leaf"), "head"),
        ),
        check_vma=False,
    )
```

```python
import jax
import jax.numpy as jnp
from jax import lax
from jax.experimental import pallas as pl
from jax.experimental.pallas import tpu as pltpu
from jax.sharding import PartitionSpec as P

QUERY_HEADS = 32
HEAD_SIZE = 128
NEGATIVE = -1e30
EPSILON = 1e-05
RANGE = 1e25
PIECES = 8
LOG2E = 1.4426950408889634

TILE = 64
CHUNK = 8
REACH = 128
SEGMENTS = 4
SCALING = HEAD_SIZE ** (-0.5)
FACTOR = SCALING * LOG2E

ROWS_BY_ROWS = (((1,), (1,)), ((), ()))
COLS_BY_COLS = (((0,), (0,)), ((), ()))
PLAIN = (((1,), (0,)), ((), ()))


def dot(a, b, dims):
    return lax.dot_general(a, b, dims, preferred_element_type=jnp.float32)


def head_columns(index):
    return pl.ds(index * HEAD_SIZE, HEAD_SIZE)


def stacked(ref, kv_head, groups):
    return jnp.concatenate(
        [ref[:, head_columns(kv_head * groups + g)] for g in range(groups)], axis=0
    )


def halves(values, op):
    return op(values[:, :HEAD_SIZE], values[:, HEAD_SIZE:])


def column(values):
    lane = lax.broadcasted_iota(jnp.int32, values.shape[:1] + (HEAD_SIZE,), 1)
    first = values.astype(jnp.bfloat16).astype(jnp.float32)
    second = (values - first).astype(jnp.bfloat16).astype(jnp.float32)
    return lane, first, second, values - first - second


def pieces(values, place):
    lane, first, second, third = column(values)
    parts = jnp.where(lane == place, first, jnp.where(lane == place + 1, second, third))
    wanted = (lane >= place) & (lane < place + 3)
    return jnp.where(wanted, parts, 0.0).astype(jnp.bfloat16)


def allowed_keys(t, starts, shape, key_axis):
    window = pl.multiple_of(jnp.maximum(t * TILE - REACH, 0), TILE)
    keys = window + lax.broadcasted_iota(jnp.int32, shape, key_axis)
    tokens = t * TILE + (lax.broadcasted_iota(jnp.int32, shape, 1 - key_axis) & (TILE - 1))
    return window, (keys <= tokens) & (keys >= starts)


def chunk_ids(list_ref, t, c, owners):
    ids = [list_ref[t, c * CHUNK + i] for i in range(CHUNK)]
    return ids, [jnp.minimum(j, owners - 1) for j in ids]


def chunk_rows(anc_ref, clipped, part, kv_head):
    return jnp.concatenate([anc_ref[j, part, :, head_columns(kv_head)] for j in clipped], axis=0)


def chunk_bias(bias_ref, ids):
    return jnp.concatenate([bias_ref[j] for j in ids for _ in range(2)], axis=0)


def near_kernel(q_ref, bkv_ref, row_ref, hot_ref, plane_ref, bias_ref, out_ref, both_ref):
    t = pl.program_id(0)
    kv_heads = bkv_ref.shape[2] // HEAD_SIZE
    groups = q_ref.shape[1] // HEAD_SIZE // kv_heads
    rows, near = groups * TILE, REACH + TILE
    window, allowed = allowed_keys(t, row_ref[0], (near, rows), 0)
    hot = jnp.concatenate([hot_ref[...]] * groups, axis=0)
    chunks = [list(range(c, c + CHUNK)) for c in range(0, plane_ref.shape[0], CHUNK)]
    for k in range(kv_heads):
        q = stacked(q_ref, k, groups)
        qx = jnp.concatenate([q, hot], axis=1)
        keys = bkv_ref[0, pl.ds(window, near), head_columns(k)]
        scores = [jnp.where(allowed, dot(keys, q, ROWS_BY_ROWS), NEGATIVE)]
        values = [bkv_ref[1, pl.ds(window, near), head_columns(k)]]
        for ids in chunks:
            keys = jnp.concatenate([chunk_rows(plane_ref, ids, 0, k), chunk_bias(bias_ref, ids)], axis=1)
            scores.append(dot(keys, qx, ROWS_BY_ROWS))
            values.append(chunk_rows(plane_ref, ids, 1, k))
        top = scores[0].max(axis=0, keepdims=True)
        for part in scores[1:]:
            top = jnp.maximum(top, jnp.max(part, axis=0, keepdims=True))
        weights = [jnp.exp2((part - top) * FACTOR) for part in scores]
        out_ref[0, k] = sum(
            dot(value, weight.astype(jnp.bfloat16), COLS_BY_COLS) for value, weight in zip(values, weights)
        )
        both_ref[0, k, 0:1, :] = top
        both_ref[0, k, 1:2, :] = sum(jnp.sum(weight, axis=0, keepdims=True) for weight in weights)


def fold(values, op):
    rows, width = values.shape
    return op(values.reshape(rows // 8, 8, width), axis=0)


def tile_rows(ref, t):
    return ref.at[pl.ds(pl.multiple_of(t * TILE, TILE), TILE)]


def arrival(t, sems, pairs, first=0):
    moves = []
    for i, (far, near, stacked_tiles) in enumerate(pairs, first):
        if stacked_tiles:
            moves.append(pltpu.make_async_copy(far.at[t], near.at[t], sems.at[i, t]))
        else:
            moves.append(pltpu.make_async_copy(tile_rows(far, t), tile_rows(near, t), sems.at[i, t]))
    return moves


def forward_kernel(
    steps_ref, list_ref, q_far, up_far, near_far, both_far, hot_ref, anc_ref, bias_ref,
    att_all, lse_ref, stat_ref, q_all, up_all,
    near_all, both_ref, in_sems, w_scr, sum_scr, o_scr, shift_scr,
):
    tiles, kv_heads, _, rows = both_ref.shape
    owners = anc_ref.shape[0]
    groups = rows // TILE
    early = [(q_far, q_all, False), (both_far, both_ref, True)]
    late = [(up_far, up_all, False), (near_far, near_all, True)]
    for t in range(tiles):
        for move in arrival(t, in_sems, early + late):
            move.start()

    def hot_of(t):
        return jnp.concatenate([tile_rows(hot_ref, t)[...]] * groups, axis=0)

    def queries_of(t):
        hot = hot_of(t)
        return [
            jnp.concatenate([stacked(tile_rows(q_all, t), k, groups), hot], axis=1) for k in range(kv_heads)
        ]

    def scored(t, c, qx):
        ids, clipped = chunk_ids(list_ref, t, c, owners)
        bias = chunk_bias(bias_ref, ids)
        keys = [jnp.concatenate([chunk_rows(anc_ref, clipped, 0, k), bias], axis=1) for k in range(kv_heads)]
        return [dot(keys[k], qx[k], ROWS_BY_ROWS) for k in range(kv_heads)]

    def weigh(t, c, qx, shifts):
        scores = scored(t, c, qx)
        return [jnp.exp2(scores[k] * FACTOR - shifts[k]) for k in range(kv_heads)]

    def valued(t, c):
        _, clipped = chunk_ids(list_ref, t, c, owners)
        return [dot(chunk_rows(anc_ref, clipped, 1, k), w_scr[k], COLS_BY_COLS) for k in range(kv_heads)]

    def keep(weights):
        for k in range(kv_heads):
            w_scr[k] = weights[k].astype(jnp.bfloat16)

    def near_shifts(t):
        return [both_ref[t, k, 0:1, :] * FACTOR for k in range(kv_heads)]

    def finish(old, last):
        near_tops = near_shifts(old)
        for k in range(kv_heads):
            o_scr[k] += last[k]
            sum_scr[k, 0:1, :] = jnp.sum(sum_scr[k], axis=0, keepdims=True)
            shift_scr[k] = near_tops[k]

        largest = jnp.max(jnp.maximum(sum_scr[0, 0:1, :], sum_scr[1, 0:1, :]))

        @pl.when(jnp.logical_not(largest < RANGE))
        def _():
            steps = steps_ref[old]
            qx = queries_of(old)

            def score(c, tops):
                scores = scored(old, c, qx)
                return tuple(jnp.maximum(tops[k], fold(scores[k], jnp.max)) for k in range(kv_heads))

            start = jnp.full((8, rows), NEGATIVE, jnp.float32)
            tops = lax.fori_loop(0, steps, score, (start,) * kv_heads)
            shifts = []
            for k in range(kv_heads):
                top = jnp.max(tops[k], axis=0, keepdims=True) * FACTOR
                shifts.append(jnp.maximum(top, near_tops[k]))
                shift_scr[k] = shifts[k]
            o_scr[...] = jnp.zeros_like(o_scr)

            def gather(c, sums):
                weights = weigh(old, c, qx, shifts)
                keep(weights)
                more = valued(old, c)
                for k in range(kv_heads):
                    o_scr[k] += more[k]
                return tuple(sums[k] + fold(weights[k], jnp.sum) for k in range(kv_heads))

            sums = lax.fori_loop(0, steps, gather, (jnp.zeros((8, rows), jnp.float32),) * kv_heads)
            for k in range(kv_heads):
                sum_scr[k, 0:1, :] = jnp.sum(sums[k], axis=0, keepdims=True)

        for move in arrival(old, in_sems, late, len(early)):
            move.wait()
        upper_ref, att_ref, stats_ref = tile_rows(up_all, old), tile_rows(att_all, old), tile_rows(stat_ref, old)
        squares = jnp.zeros((TILE, HEAD_SIZE), jnp.float32)
        inner = jnp.zeros((TILE, HEAD_SIZE), jnp.float32)
        for k in range(kv_heads):
            shift = shift_scr[k]
            fade = jnp.exp2(near_tops[k] - shift)
            total = sum_scr[k, 0:1, :] + fade * both_ref[old, k, 1:2, :]
            attended = ((o_scr[k] + fade * near_all[old, k]) * (1.0 / total)).T
            lse_ref[old, k, 0:1, :] = shift + jnp.log2(total)
            for g in range(groups):
                slab = attended[g * TILE : (g + 1) * TILE, :]
                upper = upper_ref[:, head_columns(k * groups + g)].astype(jnp.float32)
                att_ref[:, head_columns(k * groups + g)] = slab
                squares += slab * slab
                inner += slab * upper
        stats_ref[:, 0:HEAD_SIZE] = squares
        stats_ref[:, HEAD_SIZE : 2 * HEAD_SIZE] = inner

    def tile(now, first):
        for move in arrival(now, in_sems, early):
            move.wait()
        old = now - 1
        qx, shifts = queries_of(now), near_shifts(now)
        if not first:
            last = valued(old, jnp.maximum(steps_ref[old] - 1, 0))
        fresh = weigh(now, 0, qx, shifts)
        if not first:
            finish(old, last)
        keep(fresh)
        for k in range(kv_heads):
            sum_scr[k] = fold(fresh[k], jnp.sum)
            o_scr[k] = jnp.zeros_like(o_scr[k])

        def advance(c, carry):
            more = valued(now, c - 1)
            weights = weigh(now, c, qx, shifts)
            keep(weights)
            for k in range(kv_heads):
                o_scr[k] += more[k]
                sum_scr[k] += fold(weights[k], jnp.sum)
            return carry

        lax.fori_loop(1, steps_ref[now], advance, 0)

    def later(now, carry):
        tile(now, False)
        return carry

    tile(0, True)
    lax.fori_loop(1, tiles, later, 0)
    finish(tiles - 1, valued(tiles - 1, jnp.maximum(steps_ref[tiles - 1] - 1, 0)))


def norm_terms(stat_ref, other_ref):
    columns = QUERY_HEADS * HEAD_SIZE
    stats = stat_ref[...] + other_ref[...]
    squares = jnp.sum(stats[:, :HEAD_SIZE], axis=1, keepdims=True)
    inner = jnp.sum(stats[:, HEAD_SIZE:], axis=1, keepdims=True)
    scaler = lax.rsqrt(squares / columns + EPSILON)
    return scaler, scaler * scaler * scaler * inner / columns


def output_gradients(att_ref, up_ref, scaler, pull, kv_heads, groups):
    found, extended = [], []
    for k in range(kv_heads):
        slabs, extra = [], []
        for g in range(groups):
            slab = att_ref[:, head_columns(k * groups + g)]
            upper = up_ref[:, head_columns(k * groups + g)].astype(jnp.float32)
            rounded = (scaler * upper - slab * pull).astype(jnp.bfloat16)
            delta = jnp.sum(rounded.astype(jnp.float32) * slab, axis=1, keepdims=True)
            extra.append(pieces(-delta, 0))
            slabs.append(rounded)
        found.append(jnp.concatenate(slabs, axis=0))
        extended.append(jnp.concatenate([found[k], jnp.concatenate(extra, axis=0)], axis=1))
    return found, extended


def ones_columns(rows, place):
    lane = lax.broadcasted_iota(jnp.int32, (rows, HEAD_SIZE), 1)
    return ((lane >= place) & (lane < place + 3)).astype(jnp.bfloat16)


def gradient_scores(t, c, list_ref, anc_ref, bias_ref, ones, qx, d_outx, lse):
    ids, clipped = chunk_ids(list_ref, t, c, anc_ref.shape[0])
    bias = chunk_bias(bias_ref, ids)
    weights, d_scores = [], []
    for k in range(len(qx)):
        keys = jnp.concatenate([chunk_rows(anc_ref, clipped, 0, k), bias], axis=1)
        values = jnp.concatenate([chunk_rows(anc_ref, clipped, 1, k), ones], axis=1)
        weights.append(jnp.exp2(dot(keys, qx[k], ROWS_BY_ROWS) * FACTOR - lse[k]))
        d_scores.append(weights[k] * dot(values, d_outx[k], ROWS_BY_ROWS))
    return weights, d_scores


def shared_gradient_kernel(
    steps_ref, list_ref, place_ref, q_all, up_all, att_all, stat_ref, other_ref, lse_ref, hot_ref, anc_ref, bias_ref,
    terms_far, att_far,
    terms_scr, out_sems, acc_scr, w_scr, ds_scr, q_scr, do_scr,
):
    tiles, kv_heads, _, rows = lse_ref.shape
    groups = rows // TILE
    owners, _, owned, _ = anc_ref.shape
    ones = ones_columns(CHUNK * owned, 0)
    spill = pltpu.make_async_copy(att_all, att_far, out_sems.at[PIECES])
    spill.start()
    acc_scr[...] = jnp.zeros_like(acc_scr)

    def products():
        return [(dot(ds_scr[k], q_scr[k], PLAIN), dot(w_scr[k], do_scr[k], PLAIN)) for k in range(kv_heads)]

    def add(t, c, found):
        _, clipped = chunk_ids(list_ref, t, c, owners)
        for k in range(kv_heads):
            for i, j in enumerate(clipped):
                place = slice(i * owned, (i + 1) * owned)
                for part in range(2):
                    acc_scr[j, part, :, head_columns(k)] += found[k][part][place]

    def keep(weights, d_scores):
        for k in range(kv_heads):
            w_scr[k] = weights[k].astype(jnp.bfloat16)
            ds_scr[k] = d_scores[k].astype(jnp.bfloat16)

    def tile(t, first):
        if not first:
            found = products()
        scaler, pull = norm_terms(tile_rows(stat_ref, t), tile_rows(other_ref, t))
        d_out, d_outx = output_gradients(
            tile_rows(att_all, t), tile_rows(up_all, t), scaler, pull, kv_heads, groups
        )
        q = [stacked(tile_rows(q_all, t), k, groups) for k in range(kv_heads)]
        hot = jnp.concatenate([tile_rows(hot_ref, t)[...]] * groups, axis=0)
        qx = [jnp.concatenate([q[k], hot], axis=1) for k in range(kv_heads)]
        lse = [lse_ref[t, k, 0:1, :] for k in range(kv_heads)]
        fixed = (list_ref, anc_ref, bias_ref, ones, qx, d_outx, lse)
        weights, d_scores = gradient_scores(t, 0, *fixed)
        keep(weights, d_scores)
        for k in range(kv_heads):
            q_scr[k] = q[k]
            do_scr[k] = d_out[k]
        if not first:
            add(t - 1, jnp.maximum(steps_ref[t - 1] - 1, 0), found)

        def advance(c, carry):
            found = products()
            weights, d_scores = gradient_scores(t, c, *fixed)
            keep(weights, d_scores)
            add(t, c - 1, found)
            return carry

        lax.fori_loop(1, steps_ref[t], advance, 0)

    def later(t, carry):
        tile(t, False)
        return carry

    tile(0, True)
    lax.fori_loop(1, tiles, later, 0)
    add(tiles - 1, jnp.maximum(steps_ref[tiles - 1] - 1, 0), products())
    some = owners // PIECES

    def departure(i):
        place = pl.ds(i * some, some)
        return pltpu.make_async_copy(terms_scr.at[place], terms_far.at[place], out_sems.at[i])

    for i in range(PIECES):
        for j in range(i * some, (i + 1) * some):
            found = place_ref[j]
            terms_scr[j, 0] = (acc_scr[found, 0] * SCALING).astype(jnp.bfloat16)
            terms_scr[j, 1] = acc_scr[found, 1].astype(jnp.bfloat16)
        departure(i).start()
    for i in range(PIECES):
        departure(i).wait()
    spill.wait()


def own_gradient_kernel(
    steps_ref, list_ref, q_ref, up_ref, anc_ref, bias_ref, att_ref, lse_ref, stat_ref, other_ref, hot_ref,
    bkv_ref, row_ref, norm_ref, dq_ref, dbr_ref, dq_scr, ds_scr,
):
    t = pl.program_id(0)
    owners, _, owned, _ = anc_ref.shape
    kv_heads = lse_ref.shape[1]
    groups = q_ref.shape[1] // HEAD_SIZE // kv_heads
    rows, near = groups * TILE, REACH + TILE
    scaler, pull = norm_terms(stat_ref, other_ref)
    norm_ref[...] = att_ref[...] * scaler
    d_out, d_outx = output_gradients(att_ref, up_ref, scaler, pull, kv_heads, groups)
    q = [stacked(q_ref, k, groups) for k in range(kv_heads)]
    hot = jnp.concatenate([hot_ref[...]] * groups, axis=0)
    qx = [jnp.concatenate([q[k], hot], axis=1) for k in range(kv_heads)]
    lse = [lse_ref[0, k, 0:1, :] for k in range(kv_heads)]
    ones = ones_columns(CHUNK * owned, 0)
    fixed = (list_ref, anc_ref, bias_ref, ones, qx, d_outx, lse)

    @pl.when(t == 0)
    def _():
        dbr_ref[...] = jnp.zeros_like(dbr_ref)

    window, allowed = allowed_keys(t, row_ref[0], (near, rows), 0)
    for k in range(kv_heads):
        keys = bkv_ref[0, pl.ds(window, near), head_columns(k)]
        values = bkv_ref[1, pl.ds(window, near), head_columns(k)]
        valuesx = jnp.concatenate([values, ones[:near]], axis=1)
        scores = jnp.where(allowed, dot(keys, q[k], ROWS_BY_ROWS), NEGATIVE)
        weights = jnp.exp2(scores * FACTOR - lse[k])
        d_scores = (weights * dot(valuesx, d_outx[k], ROWS_BY_ROWS)).astype(jnp.bfloat16)
        dbr_ref[0, pl.ds(window, near), head_columns(k)] += dot(d_scores, q[k], PLAIN) * SCALING
        dbr_ref[1, pl.ds(window, near), head_columns(k)] += dot(
            weights.astype(jnp.bfloat16), d_out[k], PLAIN
        )
        dq_scr[k] = dot(keys, d_scores, COLS_BY_COLS)

    def keep(d_scores):
        for k in range(kv_heads):
            ds_scr[k] = d_scores[k].astype(jnp.bfloat16)

    def pulled(c):
        _, clipped = chunk_ids(list_ref, t, c, owners)
        return [dot(chunk_rows(anc_ref, clipped, 0, k), ds_scr[k], COLS_BY_COLS) for k in range(kv_heads)]

    keep(gradient_scores(t, 0, *fixed)[1])

    def advance(c, carry):
        more = pulled(c - 1)
        keep(gradient_scores(t, c, *fixed)[1])
        for k in range(kv_heads):
            dq_scr[k] += more[k]
        return carry

    lax.fori_loop(1, steps_ref[t], advance, 0)
    more = pulled(jnp.maximum(steps_ref[t] - 1, 0))
    for k in range(kv_heads):
        d_query = ((dq_scr[k] + more[k]) * SCALING).T
        for g in range(groups):
            dq_ref[:, head_columns(k * groups + g)] = d_query[g * TILE : (g + 1) * TILE, :]


def total_kernel(terms_ref, sum_ref):
    sum_ref[...] = jnp.sum(terms_ref[...].astype(jnp.float32), axis=0)


FAR, WHOLE, SLICED, SCALARS = "far", "whole", "sliced", "scalars"


def call(kernel, tiles, ins, outs, scratch=(), limit=60):
    def spec(array, way):
        if way == SCALARS:
            return pl.BlockSpec(memory_space=pltpu.SMEM)
        if way == FAR:
            return pl.BlockSpec(memory_space=pl.ANY)
        if way == WHOLE:
            return pl.BlockSpec(memory_space=pltpu.VMEM)
        rest = (0,) * (len(array.shape) - 1)
        return pl.BlockSpec((array.shape[0] // tiles,) + array.shape[1:], lambda t: (t,) + rest)

    def placed(array, way):
        return pltpu.with_memory_space_constraint(array, pltpu.MemorySpace.HBM) if way == FAR else array

    def shaped(array, way):
        return pltpu.MemorySpace.HBM(array.shape, array.dtype) if way == FAR else array

    return pl.pallas_call(
        kernel,
        **({"grid": (tiles,)} if tiles else {}),
        in_specs=[spec(*one) for one in ins],
        out_shape=[shaped(*one) for one in outs],
        out_specs=[spec(*one) for one in outs],
        scratch_shapes=list(scratch),
        compiler_params=pltpu.CompilerParams(vmem_limit_bytes=limit * 1024 * 1024),
    )(*[placed(*one) for one in ins])


def prepare(seg_lengths, anc_rows, token_count, groups, first, count):
    segments, owners = anc_rows.shape
    order = jnp.arange(segments, dtype=jnp.int32)
    finish = jnp.sum(jnp.where(order[:, None] <= order[None, :], seg_lengths[:, None], 0), axis=0)
    begin = finish - seg_lengths
    positions = jnp.arange(token_count, dtype=jnp.int32)
    member = (positions[:, None] >= begin) & (positions[:, None] < finish)
    starts = jnp.sum(jnp.where(member, begin, 0), axis=1)
    row = jnp.tile(starts.reshape(token_count // TILE, 1, TILE), (1, 1, groups))
    column = jnp.arange(HEAD_SIZE, dtype=jnp.int32)
    hot = jnp.sum(
        jnp.where(member[:, :, None] & (column == order[:, None]), 1.0, 0.0), axis=1
    ).astype(jnp.bfloat16)
    banned = jnp.concatenate([anc_rows == 0, jnp.ones((segments, 1), bool)], axis=1)
    bias = jnp.sum(
        jnp.where(banned[:, :, None] & (column == order[:, None, None]), NEGATIVE, 0.0), axis=0
    ).astype(jnp.bfloat16)
    bias = jnp.broadcast_to(bias[:, None, :], (owners + 1, 16, HEAD_SIZE))
    tiles = jnp.arange(token_count // TILE, dtype=jnp.int32)[:, None] * TILE
    active = (begin < tiles + TILE) & (finish > tiles)
    union = jnp.any(active[:, :, None] & (anc_rows != 0), axis=1)
    each = jnp.arange(owners, dtype=jnp.int32)

    def ordered(union):
        place = jnp.sum((union[:, None, :] & (each[None, :] < each[:, None])).astype(jnp.int32), axis=2)
        counts = jnp.sum(union.astype(jnp.int32), axis=1)
        hit = union[:, None, :] & (place[:, None, :] == each[:, None])
        listed = jnp.sum(jnp.where(hit, each, 0), axis=2)
        listed = jnp.where(each < counts[:, None], listed, owners)
        return (counts + CHUNK - 1) // CHUNK, listed

    mine = (each >= first) & (each < first + count)
    return ordered(union), ordered(union & ~mine), bias, hot, row


EVERY = ("dp", "leaf", "head")


def exchange_groups(depth, side, cores):
    def flat(z, y, x, core):
        return ((z * side + y) * side + x) * cores + core

    deep, wide = range(depth), range(side)
    lines = [[flat(z, y, x, 0) for x in wide] for z in deep for y in wide]
    planes = [[flat(z, y, x, 0) for z in deep for y in wide] for x in wide]
    for core in range(1, cores):
        lines += [[flat(z, y, x, core) for y in wide] for z in deep for x in wide]
        planes += [[flat(z, y, x, core) for z in deep for x in wide] for y in wide]
    return lines, planes


def exchange(blocks, groups):
    return lax.all_to_all(blocks, EVERY, 0, 0, axis_index_groups=groups, tiled=True)


def arrival_order(values, depth, side):
    cube = values.reshape(values.shape[:-1] + (depth, side, side))
    first = jnp.moveaxis(cube, -1, -3).reshape(values.shape)
    second = jnp.swapaxes(cube, -2, -3).reshape(values.shape)
    return jnp.where(lax.axis_index("head") == 0, first, second)


def local(queries, branch_kv, ancestor_key_value, upstream, lengths, ancestors):
    token_count, width = queries.shape
    kv_heads = branch_kv.shape[2] // HEAD_SIZE
    groups = width // HEAD_SIZE // kv_heads
    owners = ancestors.shape[1]
    owned = ancestor_key_value.shape[1]
    tiles = token_count // TILE
    rows = groups * TILE
    each = (owners,) + ancestor_key_value.shape
    side, cores = lax.axis_size("leaf"), lax.axis_size("head")
    depth = owners // (side * side)
    lines, planes = exchange_groups(depth, side, cores)
    order = arrival_order(jnp.arange(owners, dtype=jnp.int32), depth, side)
    places = jnp.sum(
        jnp.where(order[None, :] == jnp.arange(owners)[:, None], jnp.arange(owners, dtype=jnp.int32)[None, :], 0), axis=1
    )
    f32, bf16 = jnp.float32, jnp.bfloat16

    def new(shape, dtype=f32):
        return jax.ShapeDtypeStruct(shape, dtype)

    def spread(block, times):
        copies = jnp.broadcast_to(block[None], (times,) + block.shape)
        return copies.reshape((times * block.shape[0],) + block.shape[1:])

    count = depth * side
    plane = exchange(jnp.broadcast_to(ancestor_key_value[None], (count,) + ancestor_key_value.shape), planes)
    row_of, column_of = lax.axis_index("dp") % side, lax.axis_index("leaf")
    first = jnp.where(lax.axis_index("head") == 0, column_of, row_of) * count
    (steps, listed), (far_steps, far_listed), bias, hot, row = prepare(
        lengths[0], arrival_order(ancestors, depth, side), token_count, groups, first, count
    )
    own_bias = lax.dynamic_slice_in_dim(bias, first, count, 0)
    row, plane = lax.optimization_barrier((row, plane))
    gathered = exchange(spread(plane, side), lines)
    scalars = [(steps, SCALARS), (listed, SCALARS)]
    near, both = call(
        near_kernel, tiles,
        [
            (queries, SLICED), (branch_kv, WHOLE), (row, SLICED), (hot, SLICED), (plane, WHOLE), (own_bias, WHOLE),
        ],
        [(new((tiles, kv_heads, HEAD_SIZE, rows)), SLICED), (new((tiles, kv_heads, 8, rows)), SLICED)],
    )
    whole = (token_count, width)
    attended, lse, stats, near_queries, near_upstream = call(
        forward_kernel, 0,
        [
            (far_steps, SCALARS), (far_listed, SCALARS),
            (queries, FAR), (upstream, FAR), (near, FAR), (both, FAR), (hot, WHOLE), (gathered, WHOLE),
            (bias, WHOLE),
        ],
        [
            (new(whole), WHOLE), (new((tiles, kv_heads, 8, rows)), WHOLE),
            (new((token_count, 2 * HEAD_SIZE)), WHOLE), (new(whole, bf16), WHOLE), (new(whole, bf16), WHOLE),
        ],
        [
            pltpu.VMEM((tiles, kv_heads, HEAD_SIZE, rows), f32),
            pltpu.VMEM((tiles, kv_heads, 8, rows), f32),
            pltpu.SemaphoreType.DMA((4, tiles)),
            pltpu.VMEM((kv_heads, CHUNK * owned, rows), bf16),
            pltpu.VMEM((kv_heads, 8, rows), f32),
            pltpu.VMEM((kv_heads, HEAD_SIZE, rows), f32),
            pltpu.VMEM((kv_heads, 1, rows), f32),
        ],
        limit=28,
    )
    other = lax.ppermute(stats, "head", [(0, 1), (1, 0)])
    terms, attended = call(
        shared_gradient_kernel, 0,
        scalars + [
            (places, SCALARS), (near_queries, WHOLE), (near_upstream, WHOLE), (attended, WHOLE), (stats, WHOLE), (other, WHOLE), (lse, WHOLE),
            (hot, WHOLE), (gathered, WHOLE), (bias, WHOLE),
        ],
        [(new(each, bf16), FAR), (new(whole), FAR)],
        [
            pltpu.VMEM(each, bf16),
            pltpu.SemaphoreType.DMA((PIECES + 1,)),
            pltpu.VMEM(each, f32),
            pltpu.VMEM((kv_heads, CHUNK * owned, rows), bf16),
            pltpu.VMEM((kv_heads, CHUNK * owned, rows), bf16),
            pltpu.VMEM((kv_heads, rows, HEAD_SIZE), bf16),
            pltpu.VMEM((kv_heads, rows, HEAD_SIZE), bf16),
        ],
        limit=28,
    )
    received = lax.all_to_all(terms, ("dp", "leaf"), 0, 0, tiled=True)
    normed, d_queries, d_branch = call(
        own_gradient_kernel, tiles,
        scalars + [
            (queries, SLICED), (upstream, SLICED), (gathered, WHOLE), (bias, WHOLE), (attended, SLICED),
            (lse, SLICED), (stats, SLICED), (other, SLICED), (hot, SLICED), (branch_kv, WHOLE), (row, SLICED),
        ],
        [(new(whole), SLICED), (new(whole), SLICED), (new(branch_kv.shape), WHOLE)],
        [
            pltpu.VMEM((kv_heads, HEAD_SIZE, rows), f32),
            pltpu.VMEM((kv_heads, CHUNK * owned, rows), bf16),
        ],
    )
    (summed,) = call(
        total_kernel, 0, [(received, WHOLE)], [(new(ancestor_key_value.shape), WHOLE)], limit=8
    )
    return (normed, d_queries, d_branch, summed)


def solution(mesh):
    placed = (
        P(("dp", "leaf"), "head"),
        P(None, ("dp", "leaf"), "head"),
        P(None, ("dp", "leaf"), "head"),
        P(("dp", "leaf"), "head"),
        P(("dp", "leaf"), None),
        P(("dp", "leaf"), None),
    )
    return jax.shard_map(
        local,
        mesh=mesh,
        in_specs=placed,
        out_specs=(
            P(("dp", "leaf"), "head"),
            P(("dp", "leaf"), "head"),
            P(None, ("dp", "leaf"), "head"),
            P(None, ("dp", "leaf"), "head"),
        ),
        check_vma=False,
    )
```
